32 devices in a mesh: dp: 8 (over y, x, core), section: 4 (over z).
Axes of the slice: x: 2, y: 2, z: 4, core: 2. Of those that a mesh axis runs over, the one named last changes fastest.
Arguments:
- saved_inputs: bfloat16 [4, 8, 2, 384, 2048], P('section', 'dp'), may hold values from -6 to 6
- hidden_grads: bfloat16 [4, 8, 2, 384, 256], P('section', 'dp'), may hold values from -0.029907227 to 0.029907227
- block_expert: int32 [4, 8, 2, 3], P('section', 'dp'), may hold values from 0 to 1, as said below
- live_counts: int32 [4, 8, 2, 2], P('section', 'dp'), may hold values from 0 to 384, as said below
- first_moment: float32 [4, 2048, 2, 256], P('section', 'dp'), may hold values from -3 to 3
- second_moment: float32 [4, 2048, 2, 256], P('section', 'dp'), may hold values from 0.05 to 2
Outputs:
- grad_total: float32 [4, 2048, 2, 256], P('section', 'dp')
- new_first: float32 [4, 2048, 2, 256], P('section', 'dp')
- new_second: float32 [4, 2048, 2, 256], P('section', 'dp')
- step_direction: float32 [4, 2048, 2, 256], P('section', 'dp')
The draws below stay inside these ranges and needn't reach their ends.
Inputs may be any that keep to these rules, and one draw needn't show every extreme that they name: block_expert[p, d, k, b] names the expert of rows b * 128 to (b + 1) * 128 - 1 of that device's direction-k rows. live_counts[p, d, k, e] is 0 when no block of that direction names expert e; for n such blocks it lies between 128 * (n - 1) + 1 and 128 * n. On every device one of the two directions has all its blocks on one expert with all 384 rows live.
All inputs are finite; a program needn't handle non-finite values.
Results may differ from the reference program's by a relative error of at most 0.0021.
Values may be sent and summed in bfloat16 or wider, within the bound.
No kernel may reach another device: no remote copies, remote signals or barrier semaphores. Data moves between devices by JAX's collectives and lax.ppermute only.
A program may use at most 64 MiB of HBM per device.

```python
import math
import jax
import jax.numpy as jnp
from jax import lax

D = 2048
FF = 256
EXPERTS = 2
BLOCK = 128
ROWS = 384
NBLK = 3
SECTIONS = 4
RANKS = 8


def routing(key):
    lead_shape = (SECTIONS, RANKS, 2)
    block_draw = jax.random.randint(jax.random.fold_in(key, 101), lead_shape + (NBLK,), 0, EXPERTS)
    full_side = jax.random.randint(jax.random.fold_in(key, 102), (SECTIONS, RANKS, 1), 0, 2)
    full_expert = jax.random.randint(jax.random.fold_in(key, 103), (SECTIONS, RANKS, 1, 1), 0, EXPERTS)
    is_full = jnp.arange(2, dtype=jnp.int32)[None, None, :] == full_side
    block_expert = jnp.where(is_full[..., None], full_expert, block_draw).astype(jnp.int32)
    padding = jax.random.randint(jax.random.fold_in(key, 104), lead_shape + (EXPERTS,), 0, BLOCK)
    padding = jnp.where(is_full[..., None], 0, padding)
    onehot = (block_expert[..., :, None] == jnp.arange(EXPERTS, dtype=jnp.int32)).astype(jnp.int32)
    numbers = jnp.sum(onehot, axis=-2)
    live_counts = jnp.where(numbers > 0, BLOCK * numbers - padding, 0).astype(jnp.int32)
    return (block_expert, live_counts)


def draw_block_expert(key, part):
    return routing(key)[0]


def draw_live_counts(key, part):
    return routing(key)[1]


def raised(array, rng, source, target, shards_of, factor):
    owner, partner = [(jnp.arange(array.shape[axis_at]) // (array.shape[axis_at] // shards_of)).reshape([-1 if axis == axis_at else 1 for axis in range(array.ndim)]) for axis_at in (source, target)]
    chosen = jax.random.permutation(rng, shards_of)[partner]
    strong = (owner == chosen) | (owner == (partner + shards_of // 2) % shards_of)
    return jnp.where(strong, factor * array, array)


def level_of(stream_key, dims, pieces, smallest, largest):
    gain, own = 1.0, jax.random.fold_in(stream_key, 6)
    for axis_at, shards_of in pieces:
        steps = jnp.exp(jax.random.uniform(jax.random.fold_in(own, axis_at), (shards_of,), jnp.float32, smallest / len(pieces), largest / len(pieces)))
        gain = gain * jnp.repeat(steps, dims[axis_at] // shards_of).reshape([-1 if axis == axis_at else 1 for axis in range(len(dims))])
    return gain


def centred(stream_key, dims, width, reach, pieces=(), kind=jnp.bfloat16):
    array = jax.random.normal(stream_key, dims, jnp.float32) * width
    if len(pieces) > 0:
        array = level_of(stream_key, dims, pieces, -0.22, 0.18) * array
    return jnp.clip(array, min=-reach, max=reach).astype(kind)


def heavy_noise(rng, shape, width, reach, cuts, heavy, kind=jnp.bfloat16):
    result = width * jax.random.normal(rng, shape, jnp.float32)
    if cuts:
        result = result * level_of(rng, shape, cuts, -0.22, 0.18)
    return jnp.clip(raised(result, jax.random.fold_in(rng, 3), *heavy), -reach, reach).astype(kind)


def setup_inputs(seed: int = 0) -> dict:
    key_list = jax.random.split(jax.random.key(seed), 7)
    return {
        "saved_inputs": heavy_noise(key_list[0], (SECTIONS, RANKS, 2, ROWS, D), 1.0, 6.0, ((0, 4), (1, 8)), (1, 4, 8, 2.0)),
        "hidden_grads": centred(key_list[1], (SECTIONS, RANKS, 2, ROWS, FF), 0.005, 0.029907227, ((0, 4), (1, 8))),
        "block_expert": draw_block_expert(jax.random.fold_in(key_list[6], 71), 0),
        "live_counts": draw_live_counts(jax.random.fold_in(key_list[6], 71), 0),
        "first_moment": centred(key_list[4], (SECTIONS, D, EXPERTS, FF), 0.5, 3.0, ((0, 4), (1, 8)), jnp.float32),
        "second_moment": jnp.clip(jnp.exp(math.log(2.0) - 3.6888794 * jax.random.uniform(key_list[5], (SECTIONS, D, EXPERTS, FF), jnp.float32) ** level_of(key_list[5], (SECTIONS, D, EXPERTS, FF), ((0, 4), (1, 8)), -0.2, 0.2)), 0.05, 2.0),
    }


beta_one = 0.9
beta_two = 0.95
adam_epsilon = 1e-08
bias_first = 1.0 - 0.9 ** 50
bias_second = 1.0 - 0.95 ** 50

def route_select(block_expert, live_counts):
    experts = jnp.arange(EXPERTS, dtype=jnp.int32)
    onehot = (block_expert[..., :, None] == experts).astype(jnp.int32)
    earlier = jnp.cumsum(onehot, axis=-2) - onehot
    before = lax.optimization_barrier(jnp.sum(earlier * onehot, axis=-1))
    limits = lax.optimization_barrier(jnp.sum(live_counts[..., None, :] * onehot, axis=-1))
    offsets = jnp.arange(BLOCK, dtype=jnp.int32)
    positions = before[..., None] * BLOCK + offsets
    live_rows = positions < limits[..., None]
    return (live_rows, onehot)

def reference(saved_inputs, hidden_grads, block_expert, live_counts, first_moment, second_moment):
    live_rows, onehot = route_select(block_expert, live_counts)
    weights = onehot.astype(jnp.float32)
    masked = hidden_grads.reshape(SECTIONS, RANKS, 2, NBLK, BLOCK, FF).astype(jnp.float32) * live_rows[..., None].astype(jnp.float32)
    inputs = saved_inputs.reshape(SECTIONS, RANKS, 2, NBLK, BLOCK, D)

    def accumulate(rank_index, running):
        rows_in = lax.dynamic_index_in_dim(inputs, rank_index, 1, keepdims=False).astype(jnp.float32)
        grads_in = lax.dynamic_index_in_dim(masked, rank_index, 1, keepdims=False)
        weight_in = lax.dynamic_index_in_dim(weights, rank_index, 1, keepdims=False)
        blocks = jnp.einsum('skbrd,skbrf->skbdf', rows_in, grads_in)
        per_section = jnp.einsum('skbdf,skbe->skdef', blocks, weight_in, precision=lax.Precision.HIGHEST)
        own_part = per_section[:, 0]
        sent_part = lax.optimization_barrier(per_section[:, 1].astype(jnp.bfloat16)).astype(jnp.float32)
        mirror = jnp.roll(sent_part, SECTIONS // 2, axis=0)
        return running + own_part + mirror
    start_sum = jnp.zeros((SECTIONS, D, EXPERTS, FF), jnp.float32)
    grad_total = lax.fori_loop(0, RANKS, accumulate, start_sum)
    new_first = beta_one * first_moment + (1.0 - beta_one) * grad_total
    new_second = beta_two * second_moment + (1.0 - beta_two) * grad_total * grad_total
    step_direction = new_first / bias_first / (jnp.sqrt(new_second / bias_second) + adam_epsilon)
    return (grad_total, new_first, new_second, step_direction)
```

```python
import functools

import jax
import jax.numpy as jnp
from jax import lax
from jax.experimental import pallas as pl
from jax.experimental.pallas import tpu as pltpu
from jax.sharding import PartitionSpec as P

beta_one = 0.9
beta_two = 0.95
adam_epsilon = 1e-08
bias_first = 1.0 - 0.9**50
bias_second = 1.0 - 0.95**50

LANES = 128


def exchanged(value, axis, mask):
    count = lax.axis_size(axis)
    return lax.ppermute(value, axis, [(source, source ^ mask) for source in range(count)])


def mirrored(value):
    count = lax.axis_size("section")
    pairs = [(source, (source + count // 2) % count) for source in range(count)]
    return lax.ppermute(value, "section", pairs)


def expand_hidden(route, counts, direction, hidden, wide, blocks, experts):
    rows, width = hidden.shape
    block = rows // blocks
    seen = [jnp.int32(0) for _ in range(experts)]
    place = lax.broadcasted_iota(jnp.int32, (block, width), 0)
    for b in range(blocks):
        expert = route[direction, b]
        values = hidden[b * block : (b + 1) * block, :].astype(jnp.float32)
        for e in range(experts):
            named = expert == e
            limit = jnp.where(named, counts[direction, e] - seen[e] * block, 0)
            kept = jnp.where(place < limit, values, 0.0)
            wide[b * block : (b + 1) * block, e * width : (e + 1) * width] = kept.astype(wide.dtype)
            seen[e] = seen[e] + named.astype(jnp.int32)


def product_kernel(direction, blocks, experts, place, route, counts, inputs, hidden, out, wide):
    @pl.when(pl.program_id(0) == 0)
    def _():
        expand_hidden(route, counts, direction, hidden, wide, blocks, experts)

    product = lax.dot_general(
        inputs[...], wide[...], (((0,), (0,)), ((), ())), preferred_element_type=jnp.float32
    )
    out[...] = product.astype(out.dtype)


def products(direction, sibling, place, route, counts, inputs, hidden, share, chips, experts, dtype):
    _, rows, _ = inputs.shape
    width = hidden.shape[2]
    blocks = route.shape[1]
    columns = experts * width

    def column(k, place, route, counts):
        chip = place[0] ^ k
        core = place[1] ^ (1 if sibling else 0)
        return (direction, 0, chip * 2 + core)

    return pl.pallas_call(
        functools.partial(product_kernel, direction, blocks, experts),
        grid_spec=pltpu.PrefetchScalarGridSpec(
            num_scalar_prefetch=3,
            grid=(chips,),
            in_specs=[
                pl.BlockSpec((None, rows, share), column),
                pl.BlockSpec((None, rows, width), lambda k, *_: (direction, 0, 0)),
            ],
            out_specs=pl.BlockSpec((None, share, columns), lambda k, *_: (k, 0, 0)),
            scratch_shapes=[pltpu.VMEM((rows, columns), jnp.bfloat16)],
        ),
        out_shape=jax.ShapeDtypeStruct((chips, share, columns), dtype),
        cost_estimate=pl.CostEstimate(
            flops=2 * rows * chips * share * columns,
            bytes_accessed=2 * rows * (chips * share + width)
            + chips * share * columns * jnp.dtype(dtype).itemsize,
            transcendentals=0,
        ),
    )(place, route, counts, inputs, hidden)


def join_kernel(own, received, kept, *sent):
    total = own[...].astype(jnp.float32) + received[...].astype(jnp.float32)
    kept[...] = total[0]
    for k, out in enumerate(sent):
        out[...] = total[k + 1].astype(out.dtype)


def joined(own, received):
    chips, share, columns = own.shape
    rows = share // 2
    piece = pl.BlockSpec((rows, columns), lambda i: (i, 0))
    whole = pl.BlockSpec((chips, rows, columns), lambda i: (0, i, 0))
    return pl.pallas_call(
        join_kernel,
        grid=(2,),
        in_specs=[whole, whole],
        out_specs=[piece] * chips,
        out_shape=[jax.ShapeDtypeStruct((share, columns), jnp.float32)]
        + [jax.ShapeDtypeStruct((share, columns), jnp.bfloat16)] * (chips - 1),
        cost_estimate=pl.CostEstimate(
            flops=own.size,
            bytes_accessed=own.nbytes + received.nbytes + share * columns * (4 + 2 * (chips - 1)),
            transcendentals=0,
        ),
    )(own, received)


def total_kernel(kept, *refs):
    *received, out = refs
    total = kept[...]
    for part in received:
        total = total + part[...].astype(jnp.float32)
    out[...] = total.astype(out.dtype)


def totalled(kept, received, dtype):
    return pl.pallas_call(
        total_kernel,
        out_shape=jax.ShapeDtypeStruct(kept.shape, dtype),
        cost_estimate=pl.CostEstimate(
            flops=kept.size * len(received),
            bytes_accessed=kept.nbytes + sum(part.nbytes for part in received),
            transcendentals=0,
        ),
    )(kept, *received)


def update_kernel(experts, received_count, *refs):
    kept = refs[0]
    received = refs[1 : 1 + received_count]
    first, second = refs[1 + received_count : 3 + received_count]
    grad_out, first_out, second_out, step_out = refs[3 + received_count :]
    width = first.shape[2]
    for e in range(experts):
        columns = slice(e * width, (e + 1) * width)
        grad = kept[:, columns]
        for part in received:
            grad = grad + part[:, columns].astype(jnp.float32)
        new_first = beta_one * first[:, e, :] + (1.0 - beta_one) * grad
        new_second = beta_two * second[:, e, :] + (1.0 - beta_two) * grad * grad
        grad_out[:, e, :] = grad
        first_out[:, e, :] = new_first
        second_out[:, e, :] = new_second
        step_out[:, e, :] = (
            new_first / bias_first / (jnp.sqrt(new_second / bias_second) + adam_epsilon)
        )


def updated(kept, received, first, second):
    share, experts, width = first.shape
    rows = share // 2
    flat = pl.BlockSpec((rows, experts * width), lambda i: (i, 0))
    moment = pl.BlockSpec((rows, experts, width), lambda i: (i, 0, 0))
    return pl.pallas_call(
        functools.partial(update_kernel, experts, len(received)),
        grid=(2,),
        in_specs=[flat] * (1 + len(received)) + [moment] * 2,
        out_specs=[moment] * 4,
        out_shape=[jax.ShapeDtypeStruct(first.shape, jnp.float32)] * 4,
        cost_estimate=pl.CostEstimate(
            flops=20 * first.size,
            bytes_accessed=7 * first.nbytes + sum(part.nbytes for part in received),
            transcendentals=2 * first.size,
        ),
    )(kept, *received, first, second)


def fast_device(saved_inputs, hidden_grads, block_expert, live_counts, first_moment, second_moment):
    ranks = lax.axis_size("dp")
    chips = ranks // 2
    me = lax.axis_index("dp")
    place = jnp.stack([me // 2, me % 2]).astype(jnp.int32)
    inputs = saved_inputs[0, 0]
    hidden = hidden_grads[0, 0]
    route = block_expert[0, 0]
    counts = live_counts[0, 0]
    share, experts = first_moment.shape[1:3]
    product = functools.partial(
        products,
        place=place,
        route=route,
        counts=counts,
        inputs=inputs,
        hidden=hidden,
        share=share,
        chips=chips,
        experts=experts,
    )

    def direction_part(direction, dtype):
        other = exchanged(product(direction, True, dtype=dtype), "dp", 1)
        kept, *sent = joined(product(direction, False, dtype=dtype), other)
        return kept, [exchanged(part, "dp", 2 * (k + 1)) for k, part in enumerate(sent)]

    kept_one, received_one = direction_part(1, jnp.bfloat16)
    partner = mirrored(totalled(kept_one, received_one, jnp.bfloat16))
    kept_zero, received_zero = direction_part(0, jnp.float32)
    outs = updated(kept_zero, received_zero + [partner], first_moment[0], second_moment[0])
    return tuple(out[None] for out in outs)


def route_select(block_expert, live_counts, block):
    experts = jnp.arange(live_counts.shape[-1], dtype=jnp.int32)
    onehot = (block_expert[..., :, None] == experts).astype(jnp.int32)
    earlier = jnp.cumsum(onehot, axis=-2) - onehot
    before = jnp.sum(earlier * onehot, axis=-1)
    limits = jnp.sum(live_counts[..., None, :] * onehot, axis=-1)
    positions = before[..., None] * block + jnp.arange(block, dtype=jnp.int32)
    return positions < limits[..., None], onehot


def plain_device(saved_inputs, hidden_grads, block_expert, live_counts, first_moment, second_moment):
    _, _, _, rows, model_width = saved_inputs.shape
    hidden = hidden_grads.shape[4]
    blocks = block_expert.shape[3]
    block = rows // blocks
    live_rows, onehot = route_select(block_expert[0, 0], live_counts[0, 0], block)
    masked = hidden_grads.reshape(2, blocks, block, hidden) * live_rows[..., None].astype(
        jnp.bfloat16
    )
    wide = masked[:, :, :, None, :] * onehot[:, :, None, :, None].astype(jnp.bfloat16)
    wide = wide.reshape(2, rows, -1)
    parts = jnp.einsum(
        "krd,krc->kdc", saved_inputs[0, 0], wide, preferred_element_type=jnp.float32
    )
    sent = lax.optimization_barrier(parts[1].astype(jnp.bfloat16)).astype(jnp.float32)
    summed = lax.psum_scatter(
        jnp.stack([parts[0], sent], axis=1), "dp", scatter_dimension=0, tiled=True
    )
    grad_total = (summed[:, 0] + mirrored(summed[:, 1])).reshape(first_moment.shape[1:])
    new_first = beta_one * first_moment[0] + (1.0 - beta_one) * grad_total
    new_second = beta_two * second_moment[0] + (1.0 - beta_two) * grad_total * grad_total
    step_direction = new_first / bias_first / (jnp.sqrt(new_second / bias_second) + adam_epsilon)
    return (grad_total[None], new_first[None], new_second[None], step_direction[None])


def solution(mesh):
    in_specs = (
        P("section", "dp", None, None, None),
        P("section", "dp", None, None, None),
        P("section", "dp", None, None),
        P("section", "dp", None, None),
        P("section", "dp", None, None),
        P("section", "dp", None, None),
    )
    out_specs = (P("section", "dp", None, None),) * 4

    def run(*arrays):
        ranks = mesh.shape["dp"]
        paired = ranks % 2 == 0 and ranks & (ranks - 1) == 0
        per_device = fast_device if paired and arrays[4].shape[1] // ranks % LANES == 0 else plain_device
        return jax.shard_map(
            per_device, mesh=mesh, in_specs=in_specs, out_specs=out_specs, check_vma=False
        )(*arrays)

    return run
```

```python
import functools

import jax
import jax.numpy as jnp
from jax import lax
from jax.experimental import pallas as pl
from jax.experimental.pallas import tpu as pltpu
from jax.sharding import PartitionSpec as P

beta_one = 0.9
beta_two = 0.95
adam_epsilon = 1e-08
bias_first = 1.0 - 0.9**50
bias_second = 1.0 - 0.95**50

LANES = 128


def exchanged(value, axis, mask):
    count = lax.axis_size(axis)
    return lax.ppermute(value, axis, [(source, source ^ mask) for source in range(count)])


def mirrored(value):
    count = lax.axis_size("section")
    pairs = [(source, (source + count // 2) % count) for source in range(count)]
    return lax.ppermute(value, "section", pairs)


def expand_hidden(route, counts, direction, hidden, wide, blocks, experts):
    rows, width = hidden.shape
    block = rows // blocks
    seen = [jnp.int32(0) for _ in range(experts)]
    place = lax.broadcasted_iota(jnp.int32, (block, width), 0)
    for b in range(blocks):
        expert = route[direction, b]
        values = hidden[b * block : (b + 1) * block, :].astype(jnp.float32)
        for e in range(experts):
            named = expert == e
            limit = jnp.where(named, counts[direction, e] - seen[e] * block, 0)
            kept = jnp.where(place < limit, values, 0.0)
            wide[b * block : (b + 1) * block, e * width : (e + 1) * width] = kept.astype(wide.dtype)
            seen[e] = seen[e] + named.astype(jnp.int32)


VMEM_BYTES = 16 << 20
ANYWHERE = pl.BlockSpec(memory_space=pl.ANY)
IN_VMEM = pl.BlockSpec(memory_space=pltpu.VMEM)
IN_SMEM = pl.BlockSpec(memory_space=pltpu.SMEM)
PARAMS = pltpu.CompilerParams(vmem_limit_bytes=VMEM_BYTES)


def held(value):
    return pltpu.with_memory_space_constraint(value, pltpu.VMEM)


def product_kernel(
    direction, sibling, experts, route, counts, inputs, hidden, *refs
):
    out, wide, columns, rows, column_sems, row_sem = refs[-6:]
    chips, _, share = columns.shape
    me = lax.axis_index("dp")
    chip, core = me // 2, me % 2
    if sibling:
        core = 1 - core
    row_copy = pltpu.make_async_copy(hidden.at[direction], rows, row_sem)
    row_copy.start()
    copies = []
    for k in range(chips):
        begin = pl.multiple_of((lax.bitwise_xor(chip, k) * 2 + core) * share, share)
        copy = pltpu.make_async_copy(
            inputs.at[direction, :, pl.ds(begin, share)], columns.at[k], column_sems.at[k]
        )
        copy.start()
        copies.append(copy)
    row_copy.wait()
    expand_hidden(route, counts, direction, rows, wide, route.shape[1], experts)
    for k in range(chips):
        copies[k].wait()
        product = lax.dot_general(
            columns[k], wide[...], (((0,), (0,)), ((), ())), preferred_element_type=jnp.float32
        )
        out[k] = product.astype(out.dtype)


def products(direction, sibling, after, route, counts, inputs, hidden, share, chips, experts, dtype):
    _, rows, _ = inputs.shape
    width = hidden.shape[2]
    columns = experts * width
    return pl.pallas_call(
        functools.partial(product_kernel, direction, sibling, experts),
        in_specs=[IN_SMEM, IN_SMEM, ANYWHERE, ANYWHERE] + [ANYWHERE] * len(after),
        out_specs=IN_VMEM,
        out_shape=pltpu.VMEM((chips, share, columns), dtype),
        scratch_shapes=[
            pltpu.VMEM((rows, columns), jnp.bfloat16),
            pltpu.VMEM((chips, rows, share), jnp.bfloat16),
            pltpu.VMEM((rows, width), jnp.bfloat16),
            pltpu.SemaphoreType.DMA((chips,)),
            pltpu.SemaphoreType.DMA,
        ],
        compiler_params=PARAMS,
        cost_estimate=pl.CostEstimate(
            flops=2 * rows * chips * share * columns,
            bytes_accessed=2 * rows * (chips * share + width),
            transcendentals=0,
        ),
    )(
        route,
        counts,
        pltpu.with_memory_space_constraint(inputs, pltpu.HBM),
        pltpu.with_memory_space_constraint(hidden, pltpu.HBM),
        *after,
    )


def join_kernel(own, received, kept, *sent):
    kept[...] = own[0].astype(jnp.float32) + received[0].astype(jnp.float32)
    for k, out in enumerate(sent):
        total = own[k + 1].astype(jnp.float32) + received[k + 1].astype(jnp.float32)
        out[...] = total.astype(out.dtype)


def joined(own, received):
    chips, share, columns = own.shape
    return pl.pallas_call(
        join_kernel,
        in_specs=[IN_VMEM, IN_VMEM],
        out_specs=[IN_VMEM] * chips,
        out_shape=[pltpu.VMEM((share, columns), jnp.float32)]
        + [pltpu.VMEM((share, columns), jnp.bfloat16)] * (chips - 1),
        compiler_params=PARAMS,
        cost_estimate=pl.CostEstimate(
            flops=own.size, bytes_accessed=own.nbytes, transcendentals=0
        ),
    )(held(own), held(received))


def total_kernel(count, kept, *refs):
    total = kept[...]
    for part in refs[:count]:
        total = total + part[...].astype(jnp.float32)
    out = refs[-1]
    out[...] = total.astype(out.dtype)


def totalled(kept, received, after, dtype):
    count = len(received)
    return pl.pallas_call(
        functools.partial(total_kernel, count),
        in_specs=[IN_VMEM] * (1 + count) + [ANYWHERE] * len(after),
        out_specs=IN_VMEM,
        out_shape=pltpu.VMEM(kept.shape, dtype),
        compiler_params=PARAMS,
        cost_estimate=pl.CostEstimate(
            flops=kept.size * count, bytes_accessed=kept.nbytes, transcendentals=0
        ),
    )(held(kept), *map(held, received), *after)


def update_kernel(experts, count, steps, *refs):
    kept = refs[0]
    received = refs[1 : 1 + count]
    first, second = refs[1 + count : 3 + count]
    outs = refs[3 + count : 7 + count]
    grad_out, first_out, second_out, step_out, sems = refs[7 + count :]
    share, _, width = first.shape
    rows = share // steps
    copies = []
    for i in range(steps):
        some = slice(i * rows, (i + 1) * rows)
        for e in range(experts):
            columns = slice(e * width, (e + 1) * width)
            grad = kept[some, columns]
            for part in received:
                grad = grad + part[some, columns].astype(jnp.float32)
            new_first = beta_one * first[some, e, :] + (1.0 - beta_one) * grad
            new_second = beta_two * second[some, e, :] + (1.0 - beta_two) * grad * grad
            grad_out[some, e, :] = grad
            first_out[some, e, :] = new_first
            second_out[some, e, :] = new_second
            step_out[some, e, :] = (
                new_first / bias_first / (jnp.sqrt(new_second / bias_second) + adam_epsilon)
            )
        for j, (source, target) in enumerate(
            zip((grad_out, first_out, second_out, step_out), outs)
        ):
            copy = pltpu.make_async_copy(
                source.at[pl.ds(i * rows, rows)], target.at[pl.ds(i * rows, rows)], sems.at[i, j]
            )
            copy.start()
            copies.append(copy)
    for copy in copies:
        copy.wait()


def updated(kept, received, first, second):
    _, experts, _ = first.shape
    count, steps = len(received), 4
    return pl.pallas_call(
        functools.partial(update_kernel, experts, count, steps),
        in_specs=[IN_VMEM] * (3 + count),
        out_specs=[ANYWHERE] * 4,
        out_shape=[jax.ShapeDtypeStruct(first.shape, jnp.float32)] * 4,
        scratch_shapes=[pltpu.VMEM(first.shape, jnp.float32)] * 4
        + [pltpu.SemaphoreType.DMA((steps, 4))],
        compiler_params=PARAMS,
        cost_estimate=pl.CostEstimate(
            flops=20 * first.size,
            bytes_accessed=4 * first.nbytes,
            transcendentals=2 * first.size,
        ),
    )(held(kept), *map(held, received), held(first), held(second))


def fast_device(saved_inputs, hidden_grads, block_expert, live_counts, first_moment, second_moment):
    chips = lax.axis_size("dp") // 2
    share, experts = first_moment.shape[1:3]
    product = functools.partial(
        products,
        route=block_expert[0, 0],
        counts=live_counts[0, 0],
        inputs=saved_inputs[0, 0],
        hidden=hidden_grads[0, 0],
        share=share,
        chips=chips,
        experts=experts,
    )

    def direction_part(direction, after, dtype):
        sibling = product(direction, True, after, dtype=dtype)
        other = exchanged(sibling, "dp", 1)
        kept, *sent = joined(product(direction, False, [sibling], dtype=dtype), other)
        return kept, [exchanged(part, "dp", 2 * (k + 1)) for k, part in enumerate(sent)]

    kept_one, received_one = direction_part(1, [], jnp.bfloat16)
    kept_zero, received_zero = direction_part(0, [kept_one], jnp.float32)
    partner = mirrored(totalled(kept_one, received_one, [kept_zero], jnp.bfloat16))
    outs = updated(kept_zero, received_zero + [partner], first_moment[0], second_moment[0])
    return tuple(out[None] for out in outs)


def route_select(block_expert, live_counts, block):
    experts = jnp.arange(live_counts.shape[-1], dtype=jnp.int32)
    onehot = (block_expert[..., :, None] == experts).astype(jnp.int32)
    earlier = jnp.cumsum(onehot, axis=-2) - onehot
    before = jnp.sum(earlier * onehot, axis=-1)
    limits = jnp.sum(live_counts[..., None, :] * onehot, axis=-1)
    positions = before[..., None] * block + jnp.arange(block, dtype=jnp.int32)
    return positions < limits[..., None], onehot


def plain_device(saved_inputs, hidden_grads, block_expert, live_counts, first_moment, second_moment):
    _, _, _, rows, model_width = saved_inputs.shape
    hidden = hidden_grads.shape[4]
    blocks = block_expert.shape[3]
    block = rows // blocks
    live_rows, onehot = route_select(block_expert[0, 0], live_counts[0, 0], block)
    masked = hidden_grads.reshape(2, blocks, block, hidden) * live_rows[..., None].astype(
        jnp.bfloat16
    )
    wide = masked[:, :, :, None, :] * onehot[:, :, None, :, None].astype(jnp.bfloat16)
    wide = wide.reshape(2, rows, -1)
    parts = jnp.einsum(
        "krd,krc->kdc", saved_inputs[0, 0], wide, preferred_element_type=jnp.float32
    )
    sent = lax.optimization_barrier(parts[1].astype(jnp.bfloat16)).astype(jnp.float32)
    summed = lax.psum_scatter(
        jnp.stack([parts[0], sent], axis=1), "dp", scatter_dimension=0, tiled=True
    )
    grad_total = (summed[:, 0] + mirrored(summed[:, 1])).reshape(first_moment.shape[1:])
    new_first = beta_one * first_moment[0] + (1.0 - beta_one) * grad_total
    new_second = beta_two * second_moment[0] + (1.0 - beta_two) * grad_total * grad_total
    step_direction = new_first / bias_first / (jnp.sqrt(new_second / bias_second) + adam_epsilon)
    return (grad_total[None], new_first[None], new_second[None], step_direction[None])


def solution(mesh):
    in_specs = (
        P("section", "dp", None, None, None),
        P("section", "dp", None, None, None),
        P("section", "dp", None, None),
        P("section", "dp", None, None),
        P("section", "dp", None, None),
        P("section", "dp", None, None),
    )
    out_specs = (P("section", "dp", None, None),) * 4

    def run(*arrays):
        ranks = mesh.shape["dp"]
        paired = ranks % 2 == 0 and ranks & (ranks - 1) == 0
        per_device = fast_device if paired and arrays[4].shape[1] // ranks % LANES == 0 else plain_device
        return jax.shard_map(
            per_device, mesh=mesh, in_specs=in_specs, out_specs=out_specs, check_vma=False
        )(*arrays)

    return run
```

```python
import functools

import jax
import jax.numpy as jnp
from jax import lax
from jax.experimental import pallas as pl
from jax.experimental.pallas import tpu as pltpu
from jax.sharding import PartitionSpec as P

beta_one = 0.9
beta_two = 0.95
adam_epsilon = 1e-08
bias_first = 1.0 - 0.9**50
bias_second = 1.0 - 0.95**50

LANES = 128


def exchanged(value, axis, mask):
    count = lax.axis_size(axis)
    return lax.ppermute(value, axis, [(source, source ^ mask) for source in range(count)])


def mirrored(value):
    count = lax.axis_size("section")
    pairs = [(source, (source + count // 2) % count) for source in range(count)]
    return lax.ppermute(value, "section", pairs)


def expand_hidden(route, counts, direction, hidden, wide, blocks, experts):
    rows, width = hidden.shape
    block = rows // blocks
    seen = [jnp.int32(0) for _ in range(experts)]
    place = lax.broadcasted_iota(jnp.int32, (block, width), 0)
    for b in range(blocks):
        expert = route[direction, b]
        values = hidden[b * block : (b + 1) * block, :].astype(jnp.float32)
        for e in range(experts):
            named = expert == e
            limit = jnp.where(named, counts[direction, e] - seen[e] * block, 0)
            kept = jnp.where(place < limit, values, 0.0)
            wide[b * block : (b + 1) * block, e * width : (e + 1) * width] = kept.astype(wide.dtype)
            seen[e] = seen[e] + named.astype(jnp.int32)


VMEM_BYTES = 16 << 20
ANYWHERE = pl.BlockSpec(memory_space=pl.ANY)
IN_VMEM = pl.BlockSpec(memory_space=pltpu.VMEM)
PARAMS = pltpu.CompilerParams(vmem_limit_bytes=VMEM_BYTES)


def held(value):
    return pltpu.with_memory_space_constraint(value, pltpu.VMEM)


def routed_copies(route, counts, route_now, counts_now, sems):
    return [
        pltpu.make_async_copy(route, route_now, sems.at[0]),
        pltpu.make_async_copy(counts, counts_now, sems.at[1]),
    ]


def column_copies(inputs, direction, sibling, target, share, sem):
    me = lax.axis_index("dp")
    chip, core = me // 2, me % 2
    if sibling:
        core = 1 - core
    copies = []
    for k in range(target.shape[1] // share):
        begin = pl.multiple_of((lax.bitwise_xor(chip, k) * 2 + core) * share, share)
        copies.append(
            pltpu.make_async_copy(
                inputs.at[direction, :, pl.ds(begin, share)],
                target.at[:, pl.ds(k * share, share)],
                sem.at[k],
            )
        )
    return copies


def contracted(columns, wide):
    return lax.dot_general(
        columns, wide, (((0,), (0,)), ((), ())), preferred_element_type=jnp.float32
    )


def product_kernel(sibling, experts, count, route, counts, inputs, hidden, *refs):
    out, wide, columns, rows, route_now, counts_now, column_sems, sems = refs[-8:]
    share = out.shape[1]
    copies = routed_copies(route, counts, route_now, counts_now, sems)
    copies.append(pltpu.make_async_copy(hidden.at[1], rows.at[0], sems.at[2]))
    first = column_copies(inputs, 1, sibling, columns, share, column_sems.at[0])
    later = []
    if not sibling:
        ahead, mine, ahead_wide = refs[count : count + 3]
        later = column_copies(inputs, 0, True, ahead, share, column_sems.at[1])
        later += column_copies(inputs, 0, False, mine, share, column_sems.at[2])
        later.append(pltpu.make_async_copy(hidden.at[0], rows.at[1], sems.at[3]))
    for copy in copies + first + later:
        copy.start()
    for copy in copies:
        copy.wait()
    blocks = route.shape[1]
    expand_hidden(route_now, counts_now, 1, rows.at[0], wide, blocks, experts)
    for copy in first:
        copy.wait()
    out[...] = contracted(columns[...], wide[...]).astype(out.dtype).reshape(out.shape)
    for copy in later:
        copy.wait()
    if not sibling:
        expand_hidden(route_now, counts_now, 0, rows.at[1], ahead_wide, blocks, experts)


def products(sibling, after, route, counts, inputs, hidden, share, chips, experts):
    _, rows, _ = inputs.shape
    width = hidden.shape[2]
    wide = pltpu.VMEM((rows, experts * width), jnp.bfloat16)
    columns = pltpu.VMEM((rows, chips * share), jnp.bfloat16)
    extra = [] if sibling else [columns, columns, wide]
    outs = extra + [pltpu.VMEM((chips, share, experts * width), jnp.bfloat16)]
    return pl.pallas_call(
        functools.partial(product_kernel, sibling, experts, len(after)),
        in_specs=[ANYWHERE] * (4 + len(after)),
        out_specs=[IN_VMEM] * len(outs),
        out_shape=outs,
        scratch_shapes=[
            wide,
            columns,
            pltpu.VMEM((2, rows, width), jnp.bfloat16),
            pltpu.SMEM(route.shape, jnp.int32),
            pltpu.SMEM(counts.shape, jnp.int32),
            pltpu.SemaphoreType.DMA((3, chips)),
            pltpu.SemaphoreType.DMA((4,)),
        ],
        compiler_params=PARAMS,
        cost_estimate=pl.CostEstimate(flops=1, bytes_accessed=1, transcendentals=0),
    )(
        *(pltpu.with_memory_space_constraint(x, pltpu.HBM) for x in (route, counts, inputs, hidden)),
        *after,
    )


def join_kernel(parts, own, received, *outs):
    chips, share, _ = own.shape
    rows = share // parts
    for i in range(parts):
        some = slice(i * rows, (i + 1) * rows)
        for k in range(chips):
            out = outs[i * chips + k]
            total = own[k, some].astype(jnp.float32) + received[k, some].astype(jnp.float32)
            out[...] = total.astype(out.dtype)


def joined(own, received, parts):
    chips, share, columns = own.shape
    shape = (share // parts, columns)
    outs = [pltpu.VMEM(shape, jnp.float32)] + [pltpu.VMEM(shape, jnp.bfloat16)] * (chips - 1)
    flat = pl.pallas_call(
        functools.partial(join_kernel, parts),
        in_specs=[IN_VMEM, IN_VMEM],
        out_specs=[IN_VMEM] * (chips * parts),
        out_shape=outs * parts,
        compiler_params=PARAMS,
        cost_estimate=pl.CostEstimate(flops=1, bytes_accessed=1, transcendentals=0),
    )(held(own), held(received))
    return [flat[i * chips : (i + 1) * chips] for i in range(parts)]


def pair_kernel(mine, wide, other, other_wide, kept, *sent):
    total = contracted(mine[...], wide[...]) + contracted(other[...], other_wide[...])
    total = total.reshape(1 + len(sent), *kept.shape)
    kept[...] = total[0]
    for k, out in enumerate(sent):
        out[...] = total[k + 1].astype(out.dtype)


def paired(mine, wide, other, other_wide, share):
    chips, columns = mine.shape[1] // share, wide.shape[1]
    shape = (share, columns)
    return pl.pallas_call(
        pair_kernel,
        in_specs=[IN_VMEM] * 4,
        out_specs=[IN_VMEM] * chips,
        out_shape=[pltpu.VMEM(shape, jnp.float32)]
        + [pltpu.VMEM(shape, jnp.bfloat16)] * (chips - 1),
        compiler_params=PARAMS,
        cost_estimate=pl.CostEstimate(flops=1, bytes_accessed=1, transcendentals=0),
    )(held(mine), held(wide), held(other), held(other_wide))


def total_kernel(count, kept, *refs):
    total = kept[...]
    for part in refs[:count]:
        total = total + part[...].astype(jnp.float32)
    out = refs[-1]
    out[...] = total.astype(out.dtype)


def totalled(kept, received, after, dtype):
    count = len(received)
    return pl.pallas_call(
        functools.partial(total_kernel, count),
        in_specs=[IN_VMEM] * (1 + count) + [ANYWHERE] * len(after),
        out_specs=IN_VMEM,
        out_shape=pltpu.VMEM(kept.shape, dtype),
        compiler_params=PARAMS,
        cost_estimate=pl.CostEstimate(
            flops=1, bytes_accessed=1, transcendentals=0
        ),
    )(held(kept), *map(held, received), *after)


def update_kernel(experts, count, steps, kept, *refs):
    received, partners = refs[:count], refs[count : count + steps]
    first, second = refs[count + steps : count + steps + 2]
    outs = refs[count + steps + 2 : count + steps + 6]
    grad_out, first_out, second_out, step_out, sems = refs[count + steps + 6 :]
    share, _, width = first.shape
    rows = share // steps
    copies = []
    for i in range(steps):
        some = slice(i * rows, (i + 1) * rows)
        for e in range(experts):
            columns = slice(e * width, (e + 1) * width)
            grad = kept[some, columns]
            for part in received:
                grad = grad + part[some, columns].astype(jnp.float32)
            grad = grad + partners[i][:, columns].astype(jnp.float32)
            new_first = beta_one * first[some, e, :] + (1.0 - beta_one) * grad
            new_second = beta_two * second[some, e, :] + (1.0 - beta_two) * grad * grad
            grad_out[some, e, :] = grad
            first_out[some, e, :] = new_first
            second_out[some, e, :] = new_second
            step_out[some, e, :] = (
                new_first / bias_first / (jnp.sqrt(new_second / bias_second) + adam_epsilon)
            )
        for j, (source, target) in enumerate(
            zip((grad_out, first_out, second_out, step_out), outs)
        ):
            copy = pltpu.make_async_copy(
                source.at[pl.ds(i * rows, rows)], target.at[pl.ds(i * rows, rows)], sems.at[i, j]
            )
            copy.start()
            copies.append(copy)
    for copy in copies:
        copy.wait()


def updated(kept, received, partners, first, second):
    _, experts, _ = first.shape
    count, steps = len(received), len(partners)
    return pl.pallas_call(
        functools.partial(update_kernel, experts, count, steps),
        in_specs=[IN_VMEM] * (3 + count + steps),
        out_specs=[ANYWHERE] * 4,
        out_shape=[jax.ShapeDtypeStruct(first.shape, jnp.float32)] * 4,
        scratch_shapes=[pltpu.VMEM(first.shape, jnp.float32)] * 4
        + [pltpu.SemaphoreType.DMA((steps, 4))],
        compiler_params=PARAMS,
        cost_estimate=pl.CostEstimate(flops=1, bytes_accessed=1, transcendentals=0),
    )(*map(held, (kept, *received, *partners, first, second)))


PARTS = 1


def fast_device(saved_inputs, hidden_grads, block_expert, live_counts, first_moment, second_moment):
    chips = lax.axis_size("dp") // 2
    share, experts = first_moment.shape[1:3]
    product = functools.partial(
        products,
        route=block_expert[0, 0],
        counts=live_counts[0, 0],
        inputs=saved_inputs[0, 0],
        hidden=hidden_grads[0, 0],
        share=share,
        chips=chips,
        experts=experts,
    )

    def to_owners(pieces):
        return [exchanged(piece, "dp", 2 * (k + 1)) for k, piece in enumerate(pieces)]

    (sibling,) = product(True, [])
    other = exchanged(sibling, "dp", 1)
    ahead, mine, wide, own = product(False, [sibling])
    parts = [(kept, to_owners(sent)) for kept, *sent in joined(own, other, PARTS)]
    kept_zero, *sent_zero = paired(
        mine, wide, exchanged(ahead, "dp", 1), exchanged(wide, "dp", 1), share
    )
    received_zero = to_owners(sent_zero)
    partners = [
        mirrored(totalled(kept, received, [kept_zero], jnp.bfloat16)) for kept, received in parts
    ]
    outs = updated(kept_zero, received_zero, partners, first_moment[0], second_moment[0])
    return tuple(out[None] for out in outs)


def route_select(block_expert, live_counts, block):
    experts = jnp.arange(live_counts.shape[-1], dtype=jnp.int32)
    onehot = (block_expert[..., :, None] == experts).astype(jnp.int32)
    earlier = jnp.cumsum(onehot, axis=-2) - onehot
    before = jnp.sum(earlier * onehot, axis=-1)
    limits = jnp.sum(live_counts[..., None, :] * onehot, axis=-1)
    positions = before[..., None] * block + jnp.arange(block, dtype=jnp.int32)
    return positions < limits[..., None], onehot


def plain_device(saved_inputs, hidden_grads, block_expert, live_counts, first_moment, second_moment):
    _, _, _, rows, model_width = saved_inputs.shape
    hidden = hidden_grads.shape[4]
    blocks = block_expert.shape[3]
    block = rows // blocks
    live_rows, onehot = route_select(block_expert[0, 0], live_counts[0, 0], block)
    masked = hidden_grads.reshape(2, blocks, block, hidden) * live_rows[..., None].astype(
        jnp.bfloat16
    )
    wide = masked[:, :, :, None, :] * onehot[:, :, None, :, None].astype(jnp.bfloat16)
    wide = wide.reshape(2, rows, -1)
    parts = jnp.einsum(
        "krd,krc->kdc", saved_inputs[0, 0], wide, preferred_element_type=jnp.float32
    )
    sent = lax.optimization_barrier(parts[1].astype(jnp.bfloat16)).astype(jnp.float32)
    summed = lax.psum_scatter(
        jnp.stack([parts[0], sent], axis=1), "dp", scatter_dimension=0, tiled=True
    )
    grad_total = (summed[:, 0] + mirrored(summed[:, 1])).reshape(first_moment.shape[1:])
    new_first = beta_one * first_moment[0] + (1.0 - beta_one) * grad_total
    new_second = beta_two * second_moment[0] + (1.0 - beta_two) * grad_total * grad_total
    step_direction = new_first / bias_first / (jnp.sqrt(new_second / bias_second) + adam_epsilon)
    return (grad_total[None], new_first[None], new_second[None], step_direction[None])


def solution(mesh):
    in_specs = (
        P("section", "dp", None, None, None),
        P("section", "dp", None, None, None),
        P("section", "dp", None, None),
        P("section", "dp", None, None),
        P("section", "dp", None, None),
        P("section", "dp", None, None),
    )
    out_specs = (P("section", "dp", None, None),) * 4

    def run(*arrays):
        ranks = mesh.shape["dp"]
        paired = ranks % 2 == 0 and ranks & (ranks - 1) == 0
        per_device = fast_device if paired and arrays[4].shape[1] // ranks % LANES == 0 else plain_device
        return jax.shard_map(
            per_device, mesh=mesh, in_specs=in_specs, out_specs=out_specs, check_vma=False
        )(*arrays)

    return run
```

```python
import functools

import jax
import jax.numpy as jnp
from jax import lax
from jax.experimental import pallas as pl
from jax.experimental.pallas import tpu as pltpu
from jax.sharding import PartitionSpec as P

beta_one = 0.9
beta_two = 0.95
adam_epsilon = 1e-08
bias_first = 1.0 - 0.9**50
bias_second = 1.0 - 0.95**50

LANES = 128


def exchanged(value, axis, mask, name):
    count = lax.axis_size(axis)
    with jax.named_scope(name):
        return lax.ppermute(value, axis, [(source, source ^ mask) for source in range(count)])


def mirrored(value, name="mirror"):
    count = lax.axis_size("section")
    pairs = [(source, (source + count // 2) % count) for source in range(count)]
    with jax.named_scope(name):
        return lax.ppermute(value, "section", pairs)


def expand_hidden(route, counts, direction, hidden, wide, blocks, experts):
    rows, width = hidden.shape
    block = rows // blocks
    seen = [jnp.int32(0) for _ in range(experts)]
    place = lax.broadcasted_iota(jnp.int32, (block, width), 0)
    for b in range(blocks):
        expert = route[direction, b]
        values = hidden[b * block : (b + 1) * block, :].astype(jnp.float32)
        for e in range(experts):
            named = expert == e
            limit = jnp.where(named, counts[direction, e] - seen[e] * block, 0)
            kept = jnp.where(place < limit, values, 0.0)
            wide[b * block : (b + 1) * block, e * width : (e + 1) * width] = kept.astype(wide.dtype)
            seen[e] = seen[e] + named.astype(jnp.int32)


VMEM_BYTES = 16 << 20
ANYWHERE = pl.BlockSpec(memory_space=pl.ANY)
IN_VMEM = pl.BlockSpec(memory_space=pltpu.VMEM)
PARAMS = pltpu.CompilerParams(vmem_limit_bytes=VMEM_BYTES)
SMALL = pl.CostEstimate(flops=1, bytes_accessed=1, transcendentals=0)


def held(value):
    return pltpu.with_memory_space_constraint(value, pltpu.VMEM)


def routed_copies(route, counts, route_now, counts_now, sems):
    return [
        pltpu.make_async_copy(route, route_now, sems.at[0]),
        pltpu.make_async_copy(counts, counts_now, sems.at[1]),
    ]


def column_copies(inputs, direction, sibling, target, share, sem):
    me = lax.axis_index("dp")
    chip, core = me // 2, me % 2
    if sibling:
        core = 1 - core
    copies = []
    for k in range(target.shape[1] // share):
        begin = pl.multiple_of((lax.bitwise_xor(chip, k) * 2 + core) * share, share)
        copies.append(
            pltpu.make_async_copy(
                inputs.at[direction, :, pl.ds(begin, share)],
                target.at[:, pl.ds(k * share, share)],
                sem.at[k],
            )
        )
    return copies


def contracted(columns, wide):
    return lax.dot_general(
        columns, wide, (((0,), (0,)), ((), ())), preferred_element_type=jnp.float32
    )


def product_kernel(sibling, experts, count, route, counts, inputs, hidden, *refs):
    out, wide, columns, rows, route_now, counts_now, column_sems, sems = refs[-8:]
    share = out.shape[1]
    copies = routed_copies(route, counts, route_now, counts_now, sems)
    copies.append(pltpu.make_async_copy(hidden.at[1], rows.at[0], sems.at[2]))
    first = column_copies(inputs, 1, sibling, columns, share, column_sems.at[0])
    later = []
    if not sibling:
        ahead, mine = refs[count : count + 2]
        ahead_wide = ahead.at[:, columns.shape[1] :]
        copies.append(pltpu.make_async_copy(hidden.at[0], rows.at[1], sems.at[3]))
        span = columns.shape[1]
        later = column_copies(inputs, 0, True, ahead.at[:, :span], share, column_sems.at[1])
        later += column_copies(inputs, 0, False, mine, share, column_sems.at[2])
    for copy in copies + first + later:
        copy.start()
    for copy in copies:
        copy.wait()
    blocks = route.shape[1]
    expand_hidden(route_now, counts_now, 1, rows.at[0], wide, blocks, experts)
    if not sibling:
        expand_hidden(route_now, counts_now, 0, rows.at[1], ahead_wide, blocks, experts)
    for copy in first:
        copy.wait()
    out[...] = contracted(columns[...], wide[...]).astype(out.dtype).reshape(out.shape)
    for copy in later:
        copy.wait()


def products(sibling, after, route, counts, inputs, hidden, share, chips, experts):
    _, rows, _ = inputs.shape
    width = hidden.shape[2]
    wide = pltpu.VMEM((rows, experts * width), jnp.bfloat16)
    columns = pltpu.VMEM((rows, chips * share), jnp.bfloat16)
    both = pltpu.VMEM((rows, chips * share + experts * width), jnp.bfloat16)
    extra = [] if sibling else [both, columns]
    outs = extra + [pltpu.VMEM((chips, share, experts * width), jnp.bfloat16)]
    return pl.pallas_call(
        functools.partial(product_kernel, sibling, experts, len(after)),
        in_specs=[ANYWHERE] * (4 + len(after)),
        out_specs=[IN_VMEM] * len(outs),
        out_shape=outs,
        scratch_shapes=[
            wide,
            columns,
            pltpu.VMEM((2, rows, width), jnp.bfloat16),
            pltpu.SMEM(route.shape, jnp.int32),
            pltpu.SMEM(counts.shape, jnp.int32),
            pltpu.SemaphoreType.DMA((3, chips)),
            pltpu.SemaphoreType.DMA((4,)),
        ],
        compiler_params=PARAMS,
        cost_estimate=SMALL,
    )(
        *(pltpu.with_memory_space_constraint(x, pltpu.HBM) for x in (route, counts, inputs, hidden)),
        *after,
    )


def join_kernel(parts, own, received, *outs):
    chips, share, _ = own.shape
    rows = share // parts
    for i in range(parts):
        some = slice(i * rows, (i + 1) * rows)
        for k in range(chips):
            out = outs[i * chips + k]
            total = own[k, some].astype(jnp.float32) + received[k, some].astype(jnp.float32)
            out[...] = total.astype(out.dtype)


def joined(own, received, parts):
    chips, share, columns = own.shape
    shape = (share // parts, columns)
    outs = [pltpu.VMEM(shape, jnp.float32)] + [pltpu.VMEM(shape, jnp.bfloat16)] * (chips - 1)
    flat = pl.pallas_call(
        functools.partial(join_kernel, parts),
        in_specs=[IN_VMEM, IN_VMEM],
        out_specs=[IN_VMEM] * (chips * parts),
        out_shape=outs * parts,
        compiler_params=PARAMS,
        cost_estimate=SMALL,
    )(held(own), held(received))
    return [flat[i * chips : (i + 1) * chips] for i in range(parts)]


def pair_kernel(count, mine, ahead, other, *refs):
    kept, *sent = refs[count:]
    span = mine.shape[1]
    total = contracted(mine[...], ahead[:, span:]) + contracted(other[:, :span], other[:, span:])
    total = total.reshape(1 + len(sent), *kept.shape)
    kept[...] = total[0]
    for k, out in enumerate(sent):
        out[...] = total[k + 1].astype(out.dtype)


def paired(mine, ahead, other, after, share):
    span = mine.shape[1]
    chips, columns = span // share, ahead.shape[1] - span
    shape = (share, columns)
    return pl.pallas_call(
        functools.partial(pair_kernel, len(after)),
        in_specs=[IN_VMEM] * 3 + [ANYWHERE] * len(after),
        out_specs=[IN_VMEM] * chips,
        out_shape=[pltpu.VMEM(shape, jnp.float32)]
        + [pltpu.VMEM(shape, jnp.bfloat16)] * (chips - 1),
        compiler_params=PARAMS,
        cost_estimate=SMALL,
    )(held(mine), held(ahead), held(other), *after)


def total_kernel(count, kept, *refs):
    total = kept[...]
    for part in refs[:count]:
        total = total + part[...].astype(jnp.float32)
    out = refs[-1]
    out[...] = total.astype(out.dtype)


def totalled(kept, received, after, dtype):
    count = len(received)
    return pl.pallas_call(
        functools.partial(total_kernel, count),
        in_specs=[IN_VMEM] * (1 + count) + [ANYWHERE] * len(after),
        out_specs=IN_VMEM,
        out_shape=pltpu.VMEM(kept.shape, dtype),
        compiler_params=PARAMS,
        cost_estimate=SMALL,
    )(held(kept), *map(held, received), *after)


def update_kernel(experts, count, steps, kept, *refs):
    received, partners = refs[:count], refs[count : count + steps]
    first, second = refs[count + steps : count + steps + 2]
    outs = refs[count + steps + 2 : count + steps + 6]
    grad_out, first_out, second_out, step_out, sems = refs[count + steps + 6 :]
    share, _, width = first.shape
    rows = share // steps
    copies = []
    for i in range(steps):
        some = slice(i * rows, (i + 1) * rows)
        for e in range(experts):
            columns = slice(e * width, (e + 1) * width)
            grad = kept[some, columns]
            for part in received:
                grad = grad + part[some, columns].astype(jnp.float32)
            grad = grad + partners[i][:, columns].astype(jnp.float32)
            new_first = beta_one * first[some, e, :] + (1.0 - beta_one) * grad
            new_second = beta_two * second[some, e, :] + (1.0 - beta_two) * grad * grad
            grad_out[some, e, :] = grad
            first_out[some, e, :] = new_first
            second_out[some, e, :] = new_second
            step_out[some, e, :] = (
                new_first / bias_first / (jnp.sqrt(new_second / bias_second) + adam_epsilon)
            )
        for j, (source, target) in enumerate(
            zip((grad_out, first_out, second_out, step_out), outs)
        ):
            copy = pltpu.make_async_copy(
                source.at[pl.ds(i * rows, rows)], target.at[pl.ds(i * rows, rows)], sems.at[i, j]
            )
            copy.start()
            copies.append(copy)
    for copy in copies:
        copy.wait()


def updated(kept, received, partners, first, second):
    _, experts, _ = first.shape
    count, steps = len(received), len(partners)
    return pl.pallas_call(
        functools.partial(update_kernel, experts, count, steps),
        in_specs=[IN_VMEM] * (3 + count + steps),
        out_specs=[ANYWHERE] * 4,
        out_shape=[jax.ShapeDtypeStruct(first.shape, jnp.float32)] * 4,
        scratch_shapes=[pltpu.VMEM(first.shape, jnp.float32)] * 4
        + [pltpu.SemaphoreType.DMA((steps, 4))],
        compiler_params=PARAMS,
        cost_estimate=SMALL,
    )(*map(held, (kept, *received, *partners, first, second)))


PARTS = 2


def fast_device(saved_inputs, hidden_grads, block_expert, live_counts, first_moment, second_moment):
    chips = lax.axis_size("dp") // 2
    share, experts = first_moment.shape[1:3]
    product = functools.partial(
        products,
        route=block_expert[0, 0],
        counts=live_counts[0, 0],
        inputs=saved_inputs[0, 0],
        hidden=hidden_grads[0, 0],
        share=share,
        chips=chips,
        experts=experts,
    )

    def to_owners(pieces, name):
        return [
            exchanged(piece, "dp", 2 * (k + 1), f"{name}_to_chip_{k + 1}")
            for k, piece in enumerate(pieces)
        ]

    with jax.named_scope("sibling_products"):
        (sibling,) = product(True, [])
    other = exchanged(sibling, "dp", 1, "sibling_exchange")
    with jax.named_scope("own_products"):
        ahead, mine, own = product(False, [sibling])
    other_ahead = exchanged(ahead, "dp", 1, "operand_exchange")
    with jax.named_scope("join"):
        pieces = joined(own, other, PARTS)
    parts = [(kept, to_owners(sent, f"one_part_{i}")) for i, (kept, *sent) in enumerate(pieces)]
    with jax.named_scope("total_0"):
        first_total = totalled(*parts[0], [], jnp.bfloat16)
    with jax.named_scope("pair"):
        kept_zero, *sent_zero = paired(mine, ahead, other_ahead, [parts[0][1][1]], share)
    received_zero = to_owners(sent_zero, "zero")
    partners = [mirrored(first_total, "mirror_0")]
    for i, (kept, received) in enumerate(parts[1:]):
        with jax.named_scope(f"total_{i + 1}"):
            total = totalled(kept, received, [kept_zero], jnp.bfloat16)
        partners.append(mirrored(total, f"mirror_{i + 1}"))
    with jax.named_scope("update"):
        outs = updated(kept_zero, received_zero, partners, first_moment[0], second_moment[0])
    return tuple(out[None] for out in outs)


def route_select(block_expert, live_counts, block):
    experts = jnp.arange(live_counts.shape[-1], dtype=jnp.int32)
    onehot = (block_expert[..., :, None] == experts).astype(jnp.int32)
    earlier = jnp.cumsum(onehot, axis=-2) - onehot
    before = jnp.sum(earlier * onehot, axis=-1)
    limits = jnp.sum(live_counts[..., None, :] * onehot, axis=-1)
    positions = before[..., None] * block + jnp.arange(block, dtype=jnp.int32)
    return positions < limits[..., None], onehot


def plain_device(saved_inputs, hidden_grads, block_expert, live_counts, first_moment, second_moment):
    _, _, _, rows, model_width = saved_inputs.shape
    hidden = hidden_grads.shape[4]
    blocks = block_expert.shape[3]
    block = rows // blocks
    live_rows, onehot = route_select(block_expert[0, 0], live_counts[0, 0], block)
    masked = hidden_grads.reshape(2, blocks, block, hidden) * live_rows[..., None].astype(
        jnp.bfloat16
    )
    wide = masked[:, :, :, None, :] * onehot[:, :, None, :, None].astype(jnp.bfloat16)
    wide = wide.reshape(2, rows, -1)
    parts = jnp.einsum(
        "krd,krc->kdc", saved_inputs[0, 0], wide, preferred_element_type=jnp.float32
    )
    sent = lax.optimization_barrier(parts[1].astype(jnp.bfloat16)).astype(jnp.float32)
    summed = lax.psum_scatter(
        jnp.stack([parts[0], sent], axis=1), "dp", scatter_dimension=0, tiled=True
    )
    grad_total = (summed[:, 0] + mirrored(summed[:, 1])).reshape(first_moment.shape[1:])
    new_first = beta_one * first_moment[0] + (1.0 - beta_one) * grad_total
    new_second = beta_two * second_moment[0] + (1.0 - beta_two) * grad_total * grad_total
    step_direction = new_first / bias_first / (jnp.sqrt(new_second / bias_second) + adam_epsilon)
    return (grad_total[None], new_first[None], new_second[None], step_direction[None])


def solution(mesh):
    in_specs = (
        P("section", "dp", None, None, None),
        P("section", "dp", None, None, None),
        P("section", "dp", None, None),
        P("section", "dp", None, None),
        P("section", "dp", None, None),
        P("section", "dp", None, None),
    )
    out_specs = (P("section", "dp", None, None),) * 4

    def run(*arrays):
        ranks = mesh.shape["dp"]
        paired = ranks % 2 == 0 and ranks & (ranks - 1) == 0
        per_device = fast_device if paired and arrays[4].shape[1] // ranks % LANES == 0 else plain_device
        return jax.shard_map(
            per_device, mesh=mesh, in_specs=in_specs, out_specs=out_specs, check_vma=False
        )(*arrays)

    return run
```

```python
import functools

import jax
import jax.numpy as jnp
from jax import lax
from jax.experimental import pallas as pl
from jax.experimental.pallas import tpu as pltpu
from jax.sharding import PartitionSpec as P

beta_one = 0.9
beta_two = 0.95
adam_epsilon = 1e-08
bias_first = 1.0 - 0.9**50
bias_second = 1.0 - 0.95**50

LANES = 128


def exchanged(value, axis, mask, name):
    count = lax.axis_size(axis)
    with jax.named_scope(name):
        return lax.ppermute(value, axis, [(source, source ^ mask) for source in range(count)])


def mirrored(value, name="mirror"):
    count = lax.axis_size("section")
    pairs = [(source, (source + count // 2) % count) for source in range(count)]
    with jax.named_scope(name):
        return lax.ppermute(value, "section", pairs)


def expand_hidden(route, counts, direction, hidden, wide, blocks, experts):
    rows, width = hidden.shape
    block = rows // blocks
    seen = [jnp.int32(0) for _ in range(experts)]
    place = lax.broadcasted_iota(jnp.int32, (block, width), 0)
    for b in range(blocks):
        expert = route[direction, b]
        values = hidden[b * block : (b + 1) * block, :].astype(jnp.float32)
        for e in range(experts):
            named = expert == e
            limit = jnp.where(named, counts[direction, e] - seen[e] * block, 0)
            kept = jnp.where(place < limit, values, 0.0)
            wide[b * block : (b + 1) * block, e * width : (e + 1) * width] = kept.astype(wide.dtype)
            seen[e] = seen[e] + named.astype(jnp.int32)


VMEM_BYTES = 16 << 20
ANYWHERE = pl.BlockSpec(memory_space=pl.ANY)
IN_VMEM = pl.BlockSpec(memory_space=pltpu.VMEM)
PARAMS = pltpu.CompilerParams(vmem_limit_bytes=VMEM_BYTES)
SMALL = pl.CostEstimate(flops=1, bytes_accessed=1, transcendentals=0)
LARGE = pl.CostEstimate(flops=1 << 33, bytes_accessed=1, transcendentals=0)


def in_hbm(values):
    return [pltpu.with_memory_space_constraint(x, pltpu.HBM) for x in values]


def held(value):
    return pltpu.with_memory_space_constraint(value, pltpu.VMEM)


def routed_copies(route, counts, route_now, counts_now, sems):
    return [
        pltpu.make_async_copy(route, route_now, sems.at[0]),
        pltpu.make_async_copy(counts, counts_now, sems.at[1]),
    ]


def column_copies(inputs, direction, sibling, target, share, sem):
    me = lax.axis_index("dp")
    chip, core = me // 2, me % 2
    if sibling:
        core = 1 - core
    copies = []
    for k in range(target.shape[1] // share):
        begin = pl.multiple_of((lax.bitwise_xor(chip, k) * 2 + core) * share, share)
        copies.append(
            pltpu.make_async_copy(
                inputs.at[direction, :, pl.ds(begin, share)],
                target.at[:, pl.ds(k * share, share)],
                sem.at[k],
            )
        )
    return copies


def contracted(columns, wide):
    return lax.dot_general(
        columns, wide, (((0,), (0,)), ((), ())), preferred_element_type=jnp.float32
    )


def product_kernel(sibling, experts, count, route, counts, inputs, hidden, *refs):
    wide, columns, rows, route_now, counts_now, column_sems, sems = refs[-7:]
    out, *ahead = refs[count:-7]
    share, span, blocks = out.shape[1], columns.shape[1], route.shape[1]
    copies = routed_copies(route, counts, route_now, counts_now, sems)
    copies.append(pltpu.make_async_copy(hidden.at[1], rows.at[0], sems.at[2]))
    first = column_copies(inputs, 1, sibling, columns, share, column_sems.at[0])
    later = []
    for extra in ahead:
        copies.append(pltpu.make_async_copy(hidden.at[0], rows.at[1], sems.at[3]))
        later = column_copies(inputs, 0, True, extra.at[:, :span], share, column_sems.at[1])
    for copy in copies + first + later:
        copy.start()
    for copy in copies:
        copy.wait()
    expand_hidden(route_now, counts_now, 1, rows.at[0], wide, blocks, experts)
    for extra in ahead:
        expand_hidden(route_now, counts_now, 0, rows.at[1], extra.at[:, span:], blocks, experts)
    for copy in first:
        copy.wait()
    out[...] = contracted(columns[...], wide[...]).astype(out.dtype).reshape(out.shape)
    for copy in later:
        copy.wait()


def products(sibling, after, route, counts, inputs, hidden, share, chips, experts):
    _, rows, _ = inputs.shape
    width = hidden.shape[2]
    span, columns = chips * share, experts * width
    outs = [pltpu.VMEM((chips, share, columns), jnp.bfloat16)]
    if not sibling:
        outs.append(pltpu.VMEM((rows, span + columns), jnp.bfloat16))
    return pl.pallas_call(
        functools.partial(product_kernel, sibling, experts, len(after)),
        in_specs=[ANYWHERE] * (4 + len(after)),
        out_specs=[IN_VMEM] * len(outs),
        out_shape=outs,
        scratch_shapes=[
            pltpu.VMEM((rows, columns), jnp.bfloat16),
            pltpu.VMEM((rows, span), jnp.bfloat16),
            pltpu.VMEM((2, rows, width), jnp.bfloat16),
            pltpu.SMEM(route.shape, jnp.int32),
            pltpu.SMEM(counts.shape, jnp.int32),
            pltpu.SemaphoreType.DMA((2, chips)),
            pltpu.SemaphoreType.DMA((4,)),
        ],
        compiler_params=PARAMS,
        cost_estimate=SMALL,
    )(*in_hbm((route, counts, inputs, hidden)), *after)


def join_kernel(cuts, own, received, *outs):
    chips = own.shape[0]
    for i, some in enumerate(cuts):
        for k in range(chips):
            out = outs[i * chips + k]
            total = own[k, some].astype(jnp.float32) + received[k, some].astype(jnp.float32)
            out[...] = total.astype(out.dtype)


def joined(own, received, cuts):
    chips, _, columns = own.shape
    outs = []
    for some in cuts:
        shape = (some.stop - some.start, columns)
        outs += [pltpu.VMEM(shape, jnp.float32)] + [pltpu.VMEM(shape, jnp.bfloat16)] * (chips - 1)
    flat = pl.pallas_call(
        functools.partial(join_kernel, cuts),
        in_specs=[IN_VMEM, IN_VMEM],
        out_specs=[IN_VMEM] * len(outs),
        out_shape=outs,
        compiler_params=PARAMS,
        cost_estimate=SMALL,
    )(held(own), held(received))
    return [flat[i * chips : (i + 1) * chips] for i in range(len(cuts))]


def pair_kernel(count, messages, inputs, ahead, other, *refs):
    kept, *sent = refs[count:]
    share = kept.shape[0]
    span = ahead.shape[1] - kept.shape[1]
    me = lax.axis_index("dp")
    for k in range(span // share):
        begin = pl.multiple_of((lax.bitwise_xor(me // 2, k) * 2 + me % 2) * share, share)
        total = contracted(inputs[0, :, pl.ds(begin, share)], ahead[:, span:])
        total = total + contracted(other[:, k * share : (k + 1) * share], other[:, span:])
        if k == 0:
            kept[...] = total
        for (place, some), out in zip(messages, sent):
            if place == k:
                out[...] = total[some].astype(out.dtype)


def paired(inputs, ahead, other, after, share, chips, messages):
    columns = ahead.shape[1] - chips * share
    outs = [pltpu.VMEM((share, columns), jnp.float32)]
    outs += [pltpu.VMEM((some.stop - some.start, columns), jnp.bfloat16) for _, some in messages]
    return pl.pallas_call(
        functools.partial(pair_kernel, len(after), messages),
        in_specs=[IN_VMEM] * 3 + [ANYWHERE] * len(after),
        out_specs=[IN_VMEM] * len(outs),
        out_shape=outs,
        compiler_params=PARAMS,
        cost_estimate=SMALL,
    )(*map(held, (inputs, ahead, other)), *after)


def total_kernel(count, kept, *refs):
    total = kept[...]
    for part in refs[:count]:
        total = total + part[...].astype(jnp.float32)
    out = refs[-1]
    out[...] = total.astype(out.dtype)


def totalled(kept, received, after, dtype, cost=None):
    count = len(received)
    return pl.pallas_call(
        functools.partial(total_kernel, count),
        in_specs=[IN_VMEM] * (1 + count) + [ANYWHERE] * len(after),
        out_specs=IN_VMEM,
        out_shape=pltpu.VMEM(kept.shape, dtype),
        compiler_params=PARAMS,
        cost_estimate=cost or SMALL,
    )(held(kept), *map(held, received), *after)


def update_kernel(experts, cuts, messages, kept, *refs):
    count, parts = len(messages), len(cuts)
    received, partners = refs[:count], refs[count : count + parts]
    first, second, *outs = refs[count + parts : count + parts + 6]
    grad_out, first_out, second_out, step_out, sems = refs[count + parts + 6 :]
    share, columns = kept.shape
    lines = columns // LANES
    chunks = columns // experts // LANES
    steps = sorted({0, *(some.stop for some in cuts), *(some.stop for _, some in messages)})
    copies = []
    for i, (begin, end) in enumerate(zip(steps, steps[1:])):
        rows = end - begin

        def inside(spans):
            return [
                (ref, slice(begin - span.start, end - span.start))
                for ref, span in spans
                if span.start <= begin and end <= span.stop
            ]

        terms = inside(zip(received, (span for _, span in messages)))
        terms += inside(zip(partners, cuts))
        for line in range(lines):
            expert, chunk = line // chunks, line % chunks
            some = slice(line * LANES, (line + 1) * LANES)
            grad = kept[begin:end, some]
            for part, place in terms:
                grad = grad + part[place, some].astype(jnp.float32)
            place = begin * lines + chunk * experts + expert
            grad_out[pl.ds(place, rows, stride=lines), :] = grad
        some = slice(begin * lines, end * lines)
        grad = grad_out[some, :]
        new_first = beta_one * first[some, :] + (1.0 - beta_one) * grad
        new_second = beta_two * second[some, :] + (1.0 - beta_two) * grad * grad
        first_out[some, :] = new_first
        second_out[some, :] = new_second
        step_out[some, :] = (
            new_first / bias_first / (jnp.sqrt(new_second / bias_second) + adam_epsilon)
        )
        for j, (source, target) in enumerate(
            zip((grad_out, first_out, second_out, step_out), outs)
        ):
            copy = pltpu.make_async_copy(source.at[some], target.at[some], sems.at[i, j])
            copy.start()
            copies.append(copy)
    for copy in copies:
        copy.wait()


def in_lines(value):
    rows, experts, width = value.shape
    value = value.reshape(rows, experts, width // LANES, LANES)
    return value.transpose(0, 2, 1, 3).reshape(-1, LANES)


def from_lines(value, shape):
    rows, experts, width = shape
    value = value.reshape(rows, width // LANES, experts, LANES)
    return value.transpose(0, 2, 1, 3).reshape(shape)


def updated(kept, received, partners, first, second, cuts, messages):
    most = 1 + len(cuts) + len(messages)
    lines = pltpu.VMEM((first.size // LANES, LANES), jnp.float32)
    outs = pl.pallas_call(
        functools.partial(update_kernel, first.shape[1], cuts, messages),
        in_specs=[IN_VMEM] * (3 + len(received) + len(partners)),
        out_specs=[ANYWHERE] * 4,
        out_shape=[jax.ShapeDtypeStruct(lines.shape, jnp.float32)] * 4,
        scratch_shapes=[lines] * 4 + [pltpu.SemaphoreType.DMA((most, 4))],
        compiler_params=PARAMS,
        cost_estimate=SMALL,
    )(*map(held, (kept, *received, *partners, in_lines(first), in_lines(second))))
    return [from_lines(out, first.shape) for out in outs]


def fast_device(saved_inputs, hidden_grads, block_expert, live_counts, first_moment, second_moment):
    chips = lax.axis_size("dp") // 2
    share, experts = first_moment.shape[1:3]
    product = functools.partial(
        products,
        route=block_expert[0, 0],
        counts=live_counts[0, 0],
        inputs=saved_inputs[0, 0],
        hidden=hidden_grads[0, 0],
        share=share,
        chips=chips,
        experts=experts,
    )

    def to_owners(pieces, places, name):
        return [
            exchanged(piece, "dp", 2 * k, f"{name}_to_chip_{k}")
            for piece, k in zip(pieces, places)
        ]

    cut, half = share * 4 // 8, share // 2
    cuts = [slice(0, cut), slice(cut, share)]
    halves = [slice(0, half), slice(half, share)]
    places = range(1, chips)
    messages = [(k, slice(0, share)) for k in places]
    with jax.named_scope("sibling_products"):
        (sibling,) = product(True, [])
    other = exchanged(sibling, "dp", 1, "sibling_exchange")
    with jax.named_scope("own_products"):
        own, ahead = product(False, [sibling])
    other_ahead = exchanged(ahead, "dp", 1, "operand_exchange")
    with jax.named_scope("join"):
        pieces = joined(own, other, cuts)
    parts = [
        (kept, to_owners(sent, places, f"one_part_{i}")) for i, (kept, *sent) in enumerate(pieces)
    ]
    with jax.named_scope("pair"):
        kept_zero, *sent_zero = paired(
            saved_inputs[0, 0], ahead, other_ahead, [parts[0][1][1]], share, chips, messages
        )
    received_zero = to_owners(sent_zero, [k for k, _ in messages], "zero")
    with jax.named_scope("total_0"):
        first_total = totalled(*parts[0], [kept_zero], jnp.bfloat16)
    partners = [mirrored(first_total, "mirror_0")]
    for i, (kept, received) in enumerate(parts[1:]):
        with jax.named_scope(f"total_{i + 1}"):
            total = totalled(kept, received, [kept_zero], jnp.bfloat16, LARGE)
        partners.append(mirrored(total, f"mirror_{i + 1}"))
    with jax.named_scope("update"):
        outs = updated(
            kept_zero, received_zero, partners, first_moment[0], second_moment[0], cuts, messages
        )
    return tuple(out[None] for out in outs)


def route_select(block_expert, live_counts, block):
    experts = jnp.arange(live_counts.shape[-1], dtype=jnp.int32)
    onehot = (block_expert[..., :, None] == experts).astype(jnp.int32)
    earlier = jnp.cumsum(onehot, axis=-2) - onehot
    before = jnp.sum(earlier * onehot, axis=-1)
    limits = jnp.sum(live_counts[..., None, :] * onehot, axis=-1)
    positions = before[..., None] * block + jnp.arange(block, dtype=jnp.int32)
    return positions < limits[..., None], onehot


def plain_device(saved_inputs, hidden_grads, block_expert, live_counts, first_moment, second_moment):
    _, _, _, rows, model_width = saved_inputs.shape
    hidden = hidden_grads.shape[4]
    blocks = block_expert.shape[3]
    block = rows // blocks
    live_rows, onehot = route_select(block_expert[0, 0], live_counts[0, 0], block)
    masked = hidden_grads.reshape(2, blocks, block, hidden) * live_rows[..., None].astype(
        jnp.bfloat16
    )
    wide = masked[:, :, :, None, :] * onehot[:, :, None, :, None].astype(jnp.bfloat16)
    wide = wide.reshape(2, rows, -1)
    parts = jnp.einsum(
        "krd,krc->kdc", saved_inputs[0, 0], wide, preferred_element_type=jnp.float32
    )
    sent = lax.optimization_barrier(parts[1].astype(jnp.bfloat16)).astype(jnp.float32)
    summed = lax.psum_scatter(
        jnp.stack([parts[0], sent], axis=1), "dp", scatter_dimension=0, tiled=True
    )
    grad_total = (summed[:, 0] + mirrored(summed[:, 1])).reshape(first_moment.shape[1:])
    new_first = beta_one * first_moment[0] + (1.0 - beta_one) * grad_total
    new_second = beta_two * second_moment[0] + (1.0 - beta_two) * grad_total * grad_total
    step_direction = new_first / bias_first / (jnp.sqrt(new_second / bias_second) + adam_epsilon)
    return (grad_total[None], new_first[None], new_second[None], step_direction[None])


def solution(mesh):
    in_specs = (
        P("section", "dp", None, None, None),
        P("section", "dp", None, None, None),
        P("section", "dp", None, None),
        P("section", "dp", None, None),
        P("section", "dp", None, None),
        P("section", "dp", None, None),
    )
    out_specs = (P("section", "dp", None, None),) * 4

    def run(*arrays):
        ranks = mesh.shape["dp"]
        paired = ranks % 2 == 0 and ranks & (ranks - 1) == 0
        per_device = fast_device if paired and arrays[4].shape[1] // ranks % LANES == 0 else plain_device
        return jax.shard_map(
            per_device, mesh=mesh, in_specs=in_specs, out_specs=out_specs, check_vma=False
        )(*arrays)

    return run
```

```python
import functools

import jax
import jax.numpy as jnp
from jax import lax
from jax.experimental import pallas as pl
from jax.experimental.pallas import tpu as pltpu
from jax.sharding import PartitionSpec as P

beta_one = 0.9
beta_two = 0.95
adam_epsilon = 1e-08
bias_first = 1.0 - 0.9**50
bias_second = 1.0 - 0.95**50

LANES = 128


def exchanged(value, axis, mask, name):
    count = lax.axis_size(axis)
    with jax.named_scope(name):
        return lax.ppermute(value, axis, [(source, source ^ mask) for source in range(count)])


def mirrored(value, name="mirror"):
    count = lax.axis_size("section")
    pairs = [(source, (source + count // 2) % count) for source in range(count)]
    with jax.named_scope(name):
        return lax.ppermute(value, "section", pairs)


def expand_hidden(route, counts, direction, hidden, wide, blocks, experts):
    rows, width = hidden.shape
    block = rows // blocks
    seen = [jnp.int32(0) for _ in range(experts)]
    place = lax.broadcasted_iota(jnp.int32, (block, width), 0)
    for b in range(blocks):
        expert = route[direction, b]
        values = hidden[b * block : (b + 1) * block, :].astype(jnp.float32)
        for e in range(experts):
            named = expert == e
            limit = jnp.where(named, counts[direction, e] - seen[e] * block, 0)
            kept = jnp.where(place < limit, values, 0.0)
            wide[b * block : (b + 1) * block, e * width : (e + 1) * width] = kept.astype(wide.dtype)
            seen[e] = seen[e] + named.astype(jnp.int32)


VMEM_BYTES = 16 << 20
ANYWHERE = pl.BlockSpec(memory_space=pl.ANY)
IN_VMEM = pl.BlockSpec(memory_space=pltpu.VMEM)
PARAMS = pltpu.CompilerParams(vmem_limit_bytes=VMEM_BYTES)
PIECES = 4
SMALL = pl.CostEstimate(flops=1, bytes_accessed=1, transcendentals=0)
LARGE = pl.CostEstimate(flops=1 << 33, bytes_accessed=1, transcendentals=0)


def in_hbm(values):
    return [pltpu.with_memory_space_constraint(x, pltpu.HBM) for x in values]


def held(value):
    return pltpu.with_memory_space_constraint(value, pltpu.VMEM)


def routed_copies(route, counts, route_now, counts_now, sems):
    return [
        pltpu.make_async_copy(route, route_now, sems.at[0]),
        pltpu.make_async_copy(counts, counts_now, sems.at[1]),
    ]


def row_copies(source, target, sems):
    pieces = sems.shape[0]
    rows = source.shape[0] // pieces
    some = [pl.ds(i * rows, rows) for i in range(pieces)]
    return [
        pltpu.make_async_copy(source.at[place], target.at[place], sems.at[i])
        for i, place in enumerate(some)
    ]


def contracted(columns, wide):
    return lax.dot_general(
        columns, wide, (((0,), (0,)), ((), ())), preferred_element_type=jnp.float32
    )


def owner_columns(k, sibling, share):
    me = lax.axis_index("dp")
    core = 1 - me % 2 if sibling else me % 2
    begin = (lax.bitwise_xor(me // 2, k) * 2 + core) * share
    return pl.ds(pl.multiple_of(begin, share), share)


def sibling_kernel(experts, cuts, route, counts, inputs, hidden, *refs):
    outs = refs[: len(cuts)]
    columns, wide, rows, route_now, counts_now, column_sems, sems = refs[len(cuts) :]
    copies = routed_copies(route, counts, route_now, counts_now, sems)
    copies.append(pltpu.make_async_copy(hidden.at[1], rows, sems.at[2]))
    column_copies = row_copies(inputs.at[1], columns, column_sems)
    for copy in copies + column_copies:
        copy.start()
    for copy in copies:
        copy.wait()
    expand_hidden(route_now, counts_now, 1, rows, wide, route.shape[1], experts)
    for copy in column_copies:
        copy.wait()
    chips, _, _ = outs[0].shape
    share = cuts[-1].stop
    for k in range(chips):
        product = contracted(columns[:, owner_columns(k, True, share)], wide[...])
        for out, some in zip(outs, cuts):
            out[k] = product[some].astype(out.dtype)


def sibling_products(route, counts, inputs, hidden, chips, experts, cuts):
    _, rows, model = inputs.shape
    width = hidden.shape[2]
    columns = experts * width
    outs = [pltpu.VMEM((chips, some.stop - some.start, columns), jnp.bfloat16) for some in cuts]
    outs += [pltpu.VMEM((rows, model), jnp.bfloat16), pltpu.VMEM((rows, columns), jnp.bfloat16)]
    return pl.pallas_call(
        functools.partial(sibling_kernel, experts, cuts),
        in_specs=[ANYWHERE] * 4,
        out_specs=[IN_VMEM] * len(outs),
        out_shape=outs,
        scratch_shapes=[
            pltpu.VMEM((rows, width), jnp.bfloat16),
            pltpu.SMEM(route.shape, jnp.int32),
            pltpu.SMEM(counts.shape, jnp.int32),
            pltpu.SemaphoreType.DMA((PIECES,)),
            pltpu.SemaphoreType.DMA((3,)),
        ],
        compiler_params=PARAMS,
        cost_estimate=SMALL,
    )(*in_hbm((route, counts, inputs, hidden)))


def own_kernel(experts, route, counts, inputs, hidden, columns, wide, *refs):
    out, ahead, rows, route_now, counts_now, column_sems, sems = refs
    chips, share, _ = out.shape
    model = columns.shape[1]
    copies = routed_copies(route, counts, route_now, counts_now, sems)
    copies.append(pltpu.make_async_copy(hidden.at[0], rows, sems.at[2]))
    column_copies = row_copies(inputs.at[0], ahead.at[:, :model], column_sems)
    for copy in copies + column_copies:
        copy.start()
    for k in range(chips):
        product = contracted(columns[:, owner_columns(k, False, share)], wide[...])
        out[k] = product.astype(out.dtype)
    for copy in copies:
        copy.wait()
    expand_hidden(route_now, counts_now, 0, rows, ahead.at[:, model:], route.shape[1], experts)
    for copy in column_copies:
        copy.wait()


def own_products(route, counts, inputs, hidden, columns, wide, share, chips, experts):
    rows, model = columns.shape
    return pl.pallas_call(
        functools.partial(own_kernel, experts),
        in_specs=[ANYWHERE] * 4 + [IN_VMEM] * 2,
        out_specs=[IN_VMEM] * 2,
        out_shape=[
            pltpu.VMEM((chips, share, wide.shape[1]), jnp.bfloat16),
            pltpu.VMEM((rows, model + wide.shape[1]), jnp.bfloat16),
        ],
        scratch_shapes=[
            pltpu.VMEM(hidden.shape[1:], jnp.bfloat16),
            pltpu.SMEM(route.shape, jnp.int32),
            pltpu.SMEM(counts.shape, jnp.int32),
            pltpu.SemaphoreType.DMA((PIECES,)),
            pltpu.SemaphoreType.DMA((3,)),
        ],
        compiler_params=PARAMS,
        cost_estimate=SMALL,
    )(*in_hbm((route, counts, inputs, hidden)), held(columns), held(wide))


def join_kernel(some, own, received, *refs):
    chips = own.shape[0]
    for k, out in enumerate(refs[-chips:]):
        total = own[k, some].astype(jnp.float32) + received[k].astype(jnp.float32)
        out[...] = total.astype(out.dtype)


def joined(own, received, some, passed):
    chips, rows, columns = received.shape
    outs = [pltpu.VMEM(x.shape, x.dtype) for x in passed]
    outs += [pltpu.VMEM((rows, columns), jnp.float32)]
    outs += [pltpu.VMEM((rows, columns), jnp.bfloat16)] * (chips - 1)
    return pl.pallas_call(
        functools.partial(join_kernel, some),
        in_specs=[IN_VMEM] * (2 + len(passed)),
        out_specs=[IN_VMEM] * len(outs),
        out_shape=outs,
        input_output_aliases={2 + i: i for i in range(len(passed))},
        compiler_params=PARAMS,
        cost_estimate=SMALL,
    )(*map(held, (own, received, *passed)))


def pair_kernel(count, messages, ahead, other, *refs):
    kept, *sent = refs[count:]
    share, columns = kept.shape
    model = ahead.shape[1] - columns
    for k in range(1 + max(place for place, _ in messages)):
        place = owner_columns(k, False, share)
        total = contracted(ahead[:, place], ahead[:, model:])
        total = total + contracted(other[:, place], other[:, model:])
        if k == 0:
            kept[...] = total
        for (chip, some), out in zip(messages, sent):
            if chip == k:
                out[...] = total[some].astype(out.dtype)


def paired(ahead, other, after, share, columns, messages):
    outs = [pltpu.VMEM((share, columns), jnp.float32)]
    outs += [pltpu.VMEM((some.stop - some.start, columns), jnp.bfloat16) for _, some in messages]
    return pl.pallas_call(
        functools.partial(pair_kernel, len(after), messages),
        in_specs=[IN_VMEM] * 2 + [ANYWHERE] * len(after),
        out_specs=[IN_VMEM] * len(outs),
        out_shape=outs,
        compiler_params=PARAMS,
        cost_estimate=SMALL,
    )(held(ahead), held(other), *after)


def total_kernel(count, kept, *refs):
    total = kept[...]
    for part in refs[:count]:
        total = total + part[...].astype(jnp.float32)
    out = refs[-1]
    out[...] = total.astype(out.dtype)


def totalled(kept, received, after, dtype, cost=None):
    count = len(received)
    return pl.pallas_call(
        functools.partial(total_kernel, count),
        in_specs=[IN_VMEM] * (1 + count) + [ANYWHERE] * len(after),
        out_specs=IN_VMEM,
        out_shape=pltpu.VMEM(kept.shape, dtype),
        compiler_params=PARAMS,
        cost_estimate=cost or SMALL,
    )(held(kept), *map(held, received), *after)


def update_kernel(experts, cuts, messages, kept, *refs):
    count, parts = len(messages), len(cuts)
    received, partners = refs[:count], refs[count : count + parts]
    first, second, *outs = refs[count + parts : count + parts + 6]
    grad_out, first_out, second_out, step_out, sems = refs[count + parts + 6 :]
    share, columns = kept.shape
    lines = columns // LANES
    chunks = columns // experts // LANES
    steps = sorted({0, *(some.stop for some in cuts), *(some.stop for _, some in messages)})
    copies = []
    for i, (begin, end) in enumerate(zip(steps, steps[1:])):
        rows = end - begin

        def inside(spans):
            return [
                (ref, slice(begin - span.start, end - span.start))
                for ref, span in spans
                if span.start <= begin and end <= span.stop
            ]

        terms = inside(zip(received, (span for _, span in messages)))
        terms += inside(zip(partners, cuts))
        for line in range(lines):
            expert, chunk = line // chunks, line % chunks
            some = slice(line * LANES, (line + 1) * LANES)
            grad = kept[begin:end, some]
            for part, place in terms:
                grad = grad + part[place, some].astype(jnp.float32)
            place = begin * lines + chunk * experts + expert
            grad_out[pl.ds(place, rows, stride=lines), :] = grad
        some = slice(begin * lines, end * lines)
        grad = grad_out[some, :]
        new_first = beta_one * first[some, :] + (1.0 - beta_one) * grad
        new_second = beta_two * second[some, :] + (1.0 - beta_two) * grad * grad
        first_out[some, :] = new_first
        second_out[some, :] = new_second
        step_out[some, :] = (
            new_first / bias_first / (jnp.sqrt(new_second / bias_second) + adam_epsilon)
        )
        for j, (source, target) in enumerate(
            zip((grad_out, first_out, second_out, step_out), outs)
        ):
            copy = pltpu.make_async_copy(source.at[some], target.at[some], sems.at[i, j])
            copy.start()
            copies.append(copy)
    for copy in copies:
        copy.wait()


def in_lines(value):
    rows, experts, width = value.shape
    value = value.reshape(rows, experts, width // LANES, LANES)
    return value.transpose(0, 2, 1, 3).reshape(-1, LANES)


def from_lines(value, shape):
    rows, experts, width = shape
    value = value.reshape(rows, width // LANES, experts, LANES)
    return value.transpose(0, 2, 1, 3).reshape(shape)


def updated(kept, received, partners, first, second, cuts, messages):
    most = 1 + len(cuts) + len(messages)
    lines = pltpu.VMEM((first.size // LANES, LANES), jnp.float32)
    outs = pl.pallas_call(
        functools.partial(update_kernel, first.shape[1], cuts, messages),
        in_specs=[IN_VMEM] * (3 + len(received) + len(partners)),
        out_specs=[ANYWHERE] * 4,
        out_shape=[jax.ShapeDtypeStruct(lines.shape, jnp.float32)] * 4,
        scratch_shapes=[lines] * 4 + [pltpu.SemaphoreType.DMA((most, 4))],
        compiler_params=PARAMS,
        cost_estimate=SMALL,
    )(*map(held, (kept, *received, *partners, in_lines(first), in_lines(second))))
    return [from_lines(out, first.shape) for out in outs]


def fast_device(saved_inputs, hidden_grads, block_expert, live_counts, first_moment, second_moment):
    chips = lax.axis_size("dp") // 2
    share, experts, width = first_moment.shape[1:]
    given = (block_expert[0, 0], live_counts[0, 0], saved_inputs[0, 0], hidden_grads[0, 0])
    cuts = [slice(0, share // 2), slice(share // 2, share)]
    places = range(1, chips)
    messages = [(k, slice(0, share)) for k in places]

    def to_owners(pieces, name):
        return [
            exchanged(piece, "dp", 2 * k, f"{name}_to_chip_{k}")
            for piece, k in zip(pieces, places)
        ]

    with jax.named_scope("sibling_products"):
        *sibling, columns, wide = sibling_products(*given, chips, experts, cuts)
    others = [exchanged(part, "dp", 1, f"sibling_{i}") for i, part in enumerate(sibling)]
    with jax.named_scope("own_products"):
        own, ahead = own_products(*given, columns, wide, share, chips, experts)
    parts = []
    for i, (other, some) in enumerate(zip(others, cuts)):
        with jax.named_scope(f"join_{i}"):
            if i == 0:
                ahead, kept, *sent = joined(own, other, some, [ahead])
            else:
                kept, *sent = joined(own, other, some, [])
        parts.append((kept, to_owners(sent, f"one_part_{i}")))
    other_ahead = exchanged(ahead, "dp", 1, "operand_exchange")
    with jax.named_scope("pair"):
        kept_zero, *sent_zero = paired(
            ahead, other_ahead, [parts[0][1][1]], share, experts * width, messages
        )
    received_zero = to_owners(sent_zero, "zero")
    partners = []
    for i, (kept, received) in enumerate(parts):
        with jax.named_scope(f"total_{i}"):
            total = totalled(kept, received, [kept_zero], jnp.bfloat16, LARGE if i else SMALL)
        partners.append(mirrored(total, f"mirror_{i}"))
    with jax.named_scope("update"):
        outs = updated(
            kept_zero, received_zero, partners, first_moment[0], second_moment[0], cuts, messages
        )
    return tuple(out[None] for out in outs)


def route_select(block_expert, live_counts, block):
    experts = jnp.arange(live_counts.shape[-1], dtype=jnp.int32)
    onehot = (block_expert[..., :, None] == experts).astype(jnp.int32)
    earlier = jnp.cumsum(onehot, axis=-2) - onehot
    before = jnp.sum(earlier * onehot, axis=-1)
    limits = jnp.sum(live_counts[..., None, :] * onehot, axis=-1)
    positions = before[..., None] * block + jnp.arange(block, dtype=jnp.int32)
    return positions < limits[..., None], onehot


def plain_device(saved_inputs, hidden_grads, block_expert, live_counts, first_moment, second_moment):
    _, _, _, rows, model_width = saved_inputs.shape
    hidden = hidden_grads.shape[4]
    blocks = block_expert.shape[3]
    block = rows // blocks
    live_rows, onehot = route_select(block_expert[0, 0], live_counts[0, 0], block)
    masked = hidden_grads.reshape(2, blocks, block, hidden) * live_rows[..., None].astype(
        jnp.bfloat16
    )
    wide = masked[:, :, :, None, :] * onehot[:, :, None, :, None].astype(jnp.bfloat16)
    wide = wide.reshape(2, rows, -1)
    parts = jnp.einsum(
        "krd,krc->kdc", saved_inputs[0, 0], wide, preferred_element_type=jnp.float32
    )
    sent = lax.optimization_barrier(parts[1].astype(jnp.bfloat16)).astype(jnp.float32)
    summed = lax.psum_scatter(
        jnp.stack([parts[0], sent], axis=1), "dp", scatter_dimension=0, tiled=True
    )
    grad_total = (summed[:, 0] + mirrored(summed[:, 1])).reshape(first_moment.shape[1:])
    new_first = beta_one * first_moment[0] + (1.0 - beta_one) * grad_total
    new_second = beta_two * second_moment[0] + (1.0 - beta_two) * grad_total * grad_total
    step_direction = new_first / bias_first / (jnp.sqrt(new_second / bias_second) + adam_epsilon)
    return (grad_total[None], new_first[None], new_second[None], step_direction[None])


def solution(mesh):
    in_specs = (
        P("section", "dp", None, None, None),
        P("section", "dp", None, None, None),
        P("section", "dp", None, None),
        P("section", "dp", None, None),
        P("section", "dp", None, None),
        P("section", "dp", None, None),
    )
    out_specs = (P("section", "dp", None, None),) * 4

    def run(*arrays):
        ranks = mesh.shape["dp"]
        paired = ranks % 2 == 0 and ranks & (ranks - 1) == 0
        per_device = fast_device if paired and arrays[4].shape[1] // ranks % LANES == 0 else plain_device
        return jax.shard_map(
            per_device, mesh=mesh, in_specs=in_specs, out_specs=out_specs, check_vma=False
        )(*arrays)

    return run
```

```python
import functools

import jax
import jax.numpy as jnp
from jax import lax
from jax.experimental import pallas as pl
from jax.experimental.pallas import tpu as pltpu
from jax.sharding import PartitionSpec as P

beta_one = 0.9
beta_two = 0.95
adam_epsilon = 1e-08
bias_first = 1.0 - 0.9**50
bias_second = 1.0 - 0.95**50

LANES = 128


def neighbour(piece, core, chips, crossed):
    if crossed and piece in (1, 2) and chips > 2:
        return 1 + core if piece == 1 else 2 - core
    return piece


def exchanged(value, axis, mask_of, name):
    count = lax.axis_size(axis)
    with jax.named_scope(name):
        return lax.ppermute(value, axis, [(i, i ^ mask_of(i)) for i in range(count)])


def mirrored(value, name="mirror"):
    count = lax.axis_size("section")
    pairs = [(source, (source + count // 2) % count) for source in range(count)]
    with jax.named_scope(name):
        return lax.ppermute(value, "section", pairs)


def expand_hidden(route, counts, direction, hidden, wide, blocks, experts):
    rows, width = hidden.shape
    block = rows // blocks
    seen = [jnp.int32(0) for _ in range(experts)]
    place = lax.broadcasted_iota(jnp.int32, (block, width), 0)
    for b in range(blocks):
        expert = route[direction, b]
        values = hidden[b * block : (b + 1) * block, :].astype(jnp.float32)
        for e in range(experts):
            named = expert == e
            limit = jnp.where(named, counts[direction, e] - seen[e] * block, 0)
            kept = jnp.where(place < limit, values, 0.0)
            wide[b * block : (b + 1) * block, e * width : (e + 1) * width] = kept.astype(wide.dtype)
            seen[e] = seen[e] + named.astype(jnp.int32)


VMEM_BYTES = 16 << 20
ANYWHERE = pl.BlockSpec(memory_space=pl.ANY)
IN_VMEM = pl.BlockSpec(memory_space=pltpu.VMEM)
PARAMS = pltpu.CompilerParams(vmem_limit_bytes=VMEM_BYTES)
PIECES = 4
SMALL = pl.CostEstimate(flops=1, bytes_accessed=1, transcendentals=0)
LARGE = pl.CostEstimate(flops=1 << 33, bytes_accessed=1, transcendentals=0)


def in_hbm(values):
    return [pltpu.with_memory_space_constraint(x, pltpu.HBM) for x in values]


def held(value):
    return pltpu.with_memory_space_constraint(value, pltpu.VMEM)


def routed_copies(route, counts, route_now, counts_now, sems):
    return [
        pltpu.make_async_copy(route, route_now, sems.at[0]),
        pltpu.make_async_copy(counts, counts_now, sems.at[1]),
    ]


def row_copies(source, target, sems):
    pieces = sems.shape[0]
    rows = source.shape[0] // pieces
    some = [pl.ds(i * rows, rows) for i in range(pieces)]
    return [
        pltpu.make_async_copy(source.at[place], target.at[place], sems.at[i])
        for i, place in enumerate(some)
    ]


def contracted(columns, wide):
    return lax.dot_general(
        columns, wide, (((0,), (0,)), ((), ())), preferred_element_type=jnp.float32
    )


def owner_columns(chip, sibling, share):
    me = lax.axis_index("dp")
    core = 1 - me % 2 if sibling else me % 2
    begin = (lax.bitwise_xor(me // 2, chip) * 2 + core) * share
    return pl.ds(pl.multiple_of(begin, share), share)


def sibling_kernel(experts, cuts, route, counts, inputs, hidden, *refs):
    outs = refs[: len(cuts)]
    columns, wide, rows, route_now, counts_now, column_sems, sems = refs[len(cuts) :]
    copies = routed_copies(route, counts, route_now, counts_now, sems)
    copies.append(pltpu.make_async_copy(hidden.at[1], rows, sems.at[2]))
    column_copies = row_copies(inputs.at[1], columns, column_sems)
    for copy in copies + column_copies:
        copy.start()
    for copy in copies:
        copy.wait()
    expand_hidden(route_now, counts_now, 1, rows, wide, route.shape[1], experts)
    for copy in column_copies:
        copy.wait()
    chips, _, _ = outs[0].shape
    share = cuts[-1].stop
    for k in range(chips):
        product = contracted(columns[:, owner_columns(k, True, share)], wide[...])
        for out, some in zip(outs, cuts):
            out[k] = product[some].astype(out.dtype)


def sibling_products(route, counts, inputs, hidden, chips, experts, cuts):
    _, rows, model = inputs.shape
    width = hidden.shape[2]
    columns = experts * width
    outs = [pltpu.VMEM((chips, some.stop - some.start, columns), jnp.bfloat16) for some in cuts]
    outs += [pltpu.VMEM((rows, model), jnp.bfloat16), pltpu.VMEM((rows, columns), jnp.bfloat16)]
    return pl.pallas_call(
        functools.partial(sibling_kernel, experts, cuts),
        in_specs=[ANYWHERE] * 4,
        out_specs=[IN_VMEM] * len(outs),
        out_shape=outs,
        scratch_shapes=[
            pltpu.VMEM((rows, width), jnp.bfloat16),
            pltpu.SMEM(route.shape, jnp.int32),
            pltpu.SMEM(counts.shape, jnp.int32),
            pltpu.SemaphoreType.DMA((PIECES,)),
            pltpu.SemaphoreType.DMA((3,)),
        ],
        compiler_params=PARAMS,
        cost_estimate=SMALL,
    )(*in_hbm((route, counts, inputs, hidden)))


def own_kernel(experts, route, counts, inputs, hidden, columns, wide, *refs):
    out, ahead, rows, route_now, counts_now, column_sems, sems = refs
    chips, share, _ = out.shape
    model = columns.shape[1]
    copies = routed_copies(route, counts, route_now, counts_now, sems)
    copies.append(pltpu.make_async_copy(hidden.at[0], rows, sems.at[2]))
    column_copies = row_copies(inputs.at[0], ahead.at[:, :model], column_sems)
    for copy in copies + column_copies:
        copy.start()

    def step(k, carry):
        product = contracted(columns[:, owner_columns(k, False, share)], wide[...])
        out[k] = product.astype(out.dtype)
        return carry

    lax.fori_loop(0, chips, step, 0)
    for copy in copies:
        copy.wait()
    expand_hidden(route_now, counts_now, 0, rows, ahead.at[:, model:], route.shape[1], experts)
    for copy in column_copies:
        copy.wait()


def own_products(route, counts, inputs, hidden, columns, wide, share, chips, experts):
    rows, model = columns.shape
    return pl.pallas_call(
        functools.partial(own_kernel, experts),
        in_specs=[ANYWHERE] * 4 + [IN_VMEM] * 2,
        out_specs=[IN_VMEM] * 2,
        out_shape=[
            pltpu.VMEM((chips, share, wide.shape[1]), jnp.bfloat16),
            pltpu.VMEM((rows, model + wide.shape[1]), jnp.bfloat16),
        ],
        scratch_shapes=[
            pltpu.VMEM(hidden.shape[1:], jnp.bfloat16),
            pltpu.SMEM(route.shape, jnp.int32),
            pltpu.SMEM(counts.shape, jnp.int32),
            pltpu.SemaphoreType.DMA((PIECES,)),
            pltpu.SemaphoreType.DMA((3,)),
        ],
        compiler_params=PARAMS,
        cost_estimate=SMALL,
    )(*in_hbm((route, counts, inputs, hidden)), held(columns), held(wide))


def join_kernel(some, crossed, own, received, *refs):
    chips = own.shape[0]
    core = lax.axis_index("dp") % 2
    for piece, out in enumerate(refs[-chips:]):
        k = neighbour(piece, core, chips, crossed)
        total = own[k, some].astype(jnp.float32) + received[k].astype(jnp.float32)
        out[...] = total.astype(out.dtype)


def joined(own, received, some, passed, crossed):
    chips, rows, columns = received.shape
    outs = [pltpu.VMEM(x.shape, x.dtype) for x in passed]
    outs += [pltpu.VMEM((rows, columns), jnp.float32)]
    outs += [pltpu.VMEM((rows, columns), jnp.bfloat16)] * (chips - 1)
    return pl.pallas_call(
        functools.partial(join_kernel, some, crossed),
        in_specs=[IN_VMEM] * (2 + len(passed)),
        out_specs=[IN_VMEM] * len(outs),
        out_shape=outs,
        input_output_aliases={2 + i: i for i in range(len(passed))},
        compiler_params=PARAMS,
        cost_estimate=SMALL,
    )(*map(held, (own, received, *passed)))


def pair_kernel(count, messages, ahead, other, *refs):
    kept, *sent = refs[count:]
    share, columns = kept.shape
    model = ahead.shape[1] - columns
    chips = 1 + max(place for place, _ in messages)
    for k in range(chips):
        chip = neighbour(k, lax.axis_index("dp") % 2, chips, True)
        place = owner_columns(chip, False, share)
        total = contracted(ahead[:, place], ahead[:, model:])
        total = total + contracted(other[:, place], other[:, model:])
        if k == 0:
            kept[...] = total
        for (chip, some), out in zip(messages, sent):
            if chip == k:
                out[...] = total[some].astype(out.dtype)


def paired(ahead, other, after, share, columns, messages):
    outs = [pltpu.VMEM((share, columns), jnp.float32)]
    outs += [pltpu.VMEM((some.stop - some.start, columns), jnp.bfloat16) for _, some in messages]
    return pl.pallas_call(
        functools.partial(pair_kernel, len(after), messages),
        in_specs=[IN_VMEM] * 2 + [ANYWHERE] * len(after),
        out_specs=[IN_VMEM] * len(outs),
        out_shape=outs,
        compiler_params=PARAMS,
        cost_estimate=SMALL,
    )(held(ahead), held(other), *after)


def total_kernel(count, kept, *refs):
    total = kept[...]
    for part in refs[:count]:
        total = total + part[...].astype(jnp.float32)
    out = refs[-1]
    out[...] = total.astype(out.dtype)


def totalled(kept, received, after, dtype, cost=None):
    count = len(received)
    return pl.pallas_call(
        functools.partial(total_kernel, count),
        in_specs=[IN_VMEM] * (1 + count) + [ANYWHERE] * len(after),
        out_specs=IN_VMEM,
        out_shape=pltpu.VMEM(kept.shape, dtype),
        compiler_params=PARAMS,
        cost_estimate=cost or SMALL,
    )(held(kept), *map(held, received), *after)


def update_kernel(experts, cuts, messages, kept, *refs):
    count, parts = len(messages), len(cuts)
    received, partners = refs[:count], refs[count : count + parts]
    first, second, *outs = refs[count + parts : count + parts + 6]
    grad_out, first_out, second_out, step_out, sems = refs[count + parts + 6 :]
    share, columns = kept.shape
    lines = columns // LANES
    chunks = columns // experts // LANES
    steps = sorted({0, *(some.stop for some in cuts), *(some.stop for _, some in messages)})
    copies = []
    for i, (begin, end) in enumerate(zip(steps, steps[1:])):
        rows = end - begin

        def inside(spans):
            return [
                (ref, slice(begin - span.start, end - span.start))
                for ref, span in spans
                if span.start <= begin and end <= span.stop
            ]

        terms = inside(zip(received, (span for _, span in messages)))
        terms += inside(zip(partners, cuts))
        for line in range(lines):
            expert, chunk = line // chunks, line % chunks
            some = slice(line * LANES, (line + 1) * LANES)
            grad = kept[begin:end, some]
            for part, place in terms:
                grad = grad + part[place, some].astype(jnp.float32)
            place = begin * lines + chunk * experts + expert
            grad_out[pl.ds(place, rows, stride=lines), :] = grad
        some = slice(begin * lines, end * lines)
        grad = grad_out[some, :]
        new_first = beta_one * first[some, :] + (1.0 - beta_one) * grad
        new_second = beta_two * second[some, :] + (1.0 - beta_two) * grad * grad
        first_out[some, :] = new_first
        second_out[some, :] = new_second
        step_out[some, :] = (
            new_first / bias_first / (jnp.sqrt(new_second / bias_second) + adam_epsilon)
        )
        for j, (source, target) in enumerate(
            zip((grad_out, first_out, second_out, step_out), outs)
        ):
            copy = pltpu.make_async_copy(source.at[some], target.at[some], sems.at[i, j])
            copy.start()
            copies.append(copy)
    for copy in copies:
        copy.wait()


def in_lines(value):
    rows, experts, width = value.shape
    value = value.reshape(rows, experts, width // LANES, LANES)
    return value.transpose(0, 2, 1, 3).reshape(-1, LANES)


def from_lines(value, shape):
    rows, experts, width = shape
    value = value.reshape(rows, width // LANES, experts, LANES)
    return value.transpose(0, 2, 1, 3).reshape(shape)


def updated(kept, received, partners, first, second, cuts, messages):
    most = 1 + len(cuts) + len(messages)
    lines = pltpu.VMEM((first.size // LANES, LANES), jnp.float32)
    outs = pl.pallas_call(
        functools.partial(update_kernel, first.shape[1], cuts, messages),
        in_specs=[IN_VMEM] * (3 + len(received) + len(partners)),
        out_specs=[ANYWHERE] * 4,
        out_shape=[jax.ShapeDtypeStruct(lines.shape, jnp.float32)] * 4,
        scratch_shapes=[lines] * 4 + [pltpu.SemaphoreType.DMA((most, 4))],
        compiler_params=PARAMS,
        cost_estimate=SMALL,
    )(*map(held, (kept, *received, *partners, in_lines(first), in_lines(second))))
    return [from_lines(out, first.shape) for out in outs]


def fast_device(saved_inputs, hidden_grads, block_expert, live_counts, first_moment, second_moment):
    chips = lax.axis_size("dp") // 2
    share, experts, width = first_moment.shape[1:]
    given = (block_expert[0, 0], live_counts[0, 0], saved_inputs[0, 0], hidden_grads[0, 0])
    cuts = [slice(0, share // 2), slice(share // 2, share)]
    places = range(1, chips)
    messages = [(k, slice(0, share)) for k in places]

    def to_owners(pieces, name, crossed):
        sent = []
        for piece, k in zip(pieces, places):
            chip = functools.partial(neighbour, k, chips=chips, crossed=crossed)
            sent.append(exchanged(piece, "dp", lambda i: 2 * chip(i % 2), f"{name}_to_chip_{k}"))
        return sent

    with jax.named_scope("sibling_products"):
        *sibling, columns, wide = sibling_products(*given, chips, experts, cuts)
    others = [exchanged(part, "dp", lambda i: 1, f"sibling_{i}") for i, part in enumerate(sibling)]
    with jax.named_scope("own_products"):
        own, ahead = own_products(*given, columns, wide, share, chips, experts)
    parts = []
    for i, (other, some) in enumerate(zip(others, cuts)):
        with jax.named_scope(f"join_{i}"):
            if i == 0:
                ahead, kept, *sent = joined(own, other, some, [ahead], True)
            else:
                kept, *sent = joined(own, other, some, [], False)
        parts.append((kept, to_owners(sent, f"one_part_{i}", False if i else True)))
    other_ahead = exchanged(ahead, "dp", lambda i: 1, "operand_exchange")
    with jax.named_scope("pair"):
        kept_zero, *sent_zero = paired(
            ahead, other_ahead, [parts[0][1][1]], share, experts * width, messages
        )
    received_zero = to_owners(sent_zero, "zero", True)
    partners = []
    for i, (kept, received) in enumerate(parts):
        with jax.named_scope(f"total_{i}"):
            total = totalled(kept, received, [kept_zero], jnp.bfloat16, LARGE if i else SMALL)
        partners.append(mirrored(total, f"mirror_{i}"))
    with jax.named_scope("update"):
        outs = updated(
            kept_zero, received_zero, partners, first_moment[0], second_moment[0], cuts, messages
        )
    return tuple(out[None] for out in outs)


def route_select(block_expert, live_counts, block):
    experts = jnp.arange(live_counts.shape[-1], dtype=jnp.int32)
    onehot = (block_expert[..., :, None] == experts).astype(jnp.int32)
    earlier = jnp.cumsum(onehot, axis=-2) - onehot
    before = jnp.sum(earlier * onehot, axis=-1)
    limits = jnp.sum(live_counts[..., None, :] * onehot, axis=-1)
    positions = before[..., None] * block + jnp.arange(block, dtype=jnp.int32)
    return positions < limits[..., None], onehot


def plain_device(saved_inputs, hidden_grads, block_expert, live_counts, first_moment, second_moment):
    _, _, _, rows, model_width = saved_inputs.shape
    hidden = hidden_grads.shape[4]
    blocks = block_expert.shape[3]
    block = rows // blocks
    live_rows, onehot = route_select(block_expert[0, 0], live_counts[0, 0], block)
    masked = hidden_grads.reshape(2, blocks, block, hidden) * live_rows[..., None].astype(
        jnp.bfloat16
    )
    wide = masked[:, :, :, None, :] * onehot[:, :, None, :, None].astype(jnp.bfloat16)
    wide = wide.reshape(2, rows, -1)
    parts = jnp.einsum(
        "krd,krc->kdc", saved_inputs[0, 0], wide, preferred_element_type=jnp.float32
    )
    sent = lax.optimization_barrier(parts[1].astype(jnp.bfloat16)).astype(jnp.float32)
    summed = lax.psum_scatter(
        jnp.stack([parts[0], sent], axis=1), "dp", scatter_dimension=0, tiled=True
    )
    grad_total = (summed[:, 0] + mirrored(summed[:, 1])).reshape(first_moment.shape[1:])
    new_first = beta_one * first_moment[0] + (1.0 - beta_one) * grad_total
    new_second = beta_two * second_moment[0] + (1.0 - beta_two) * grad_total * grad_total
    step_direction = new_first / bias_first / (jnp.sqrt(new_second / bias_second) + adam_epsilon)
    return (grad_total[None], new_first[None], new_second[None], step_direction[None])


def solution(mesh):
    in_specs = (
        P("section", "dp", None, None, None),
        P("section", "dp", None, None, None),
        P("section", "dp", None, None),
        P("section", "dp", None, None),
        P("section", "dp", None, None),
        P("section", "dp", None, None),
    )
    out_specs = (P("section", "dp", None, None),) * 4

    def run(*arrays):
        ranks = mesh.shape["dp"]
        paired = ranks % 2 == 0 and ranks & (ranks - 1) == 0
        per_device = fast_device if paired and arrays[4].shape[1] // ranks % LANES == 0 else plain_device
        return jax.shard_map(
            per_device, mesh=mesh, in_specs=in_specs, out_specs=out_specs, check_vma=False
        )(*arrays)

    return run
```

```python
import functools

import jax
import jax.numpy as jnp
from jax import lax
from jax.experimental import pallas as pl
from jax.experimental.pallas import tpu as pltpu
from jax.sharding import PartitionSpec as P

beta_one = 0.9
beta_two = 0.95
adam_epsilon = 1e-08
bias_first = 1.0 - 0.9**50
bias_second = 1.0 - 0.95**50

LANES = 128


def neighbour(piece, core, chips, crossed):
    if crossed and piece in (1, 2) and chips > 2:
        return 1 + core if piece == 1 else 2 - core
    return piece


def exchanged(value, axis, mask_of, name):
    count = lax.axis_size(axis)
    with jax.named_scope(name):
        return lax.ppermute(value, axis, [(i, i ^ mask_of(i)) for i in range(count)])


def mirrored(value, name="mirror"):
    count = lax.axis_size("section")
    pairs = [(source, (source + count // 2) % count) for source in range(count)]
    with jax.named_scope(name):
        return lax.ppermute(value, "section", pairs)


def expand_hidden(route, counts, direction, hidden, wide, blocks, experts):
    rows, width = hidden.shape
    block = rows // blocks
    seen = [jnp.int32(0) for _ in range(experts)]
    place = lax.broadcasted_iota(jnp.int32, (block, width), 0)
    for b in range(blocks):
        expert = route[direction, b]
        values = hidden[b * block : (b + 1) * block, :].astype(jnp.float32)
        for e in range(experts):
            named = expert == e
            limit = jnp.where(named, counts[direction, e] - seen[e] * block, 0)
            kept = jnp.where(place < limit, values, 0.0)
            wide[b * block : (b + 1) * block, e * width : (e + 1) * width] = kept.astype(wide.dtype)
            seen[e] = seen[e] + named.astype(jnp.int32)


VMEM_BYTES = 16 << 20
ANYWHERE = pl.BlockSpec(memory_space=pl.ANY)
IN_VMEM = pl.BlockSpec(memory_space=pltpu.VMEM)
PARAMS = pltpu.CompilerParams(vmem_limit_bytes=VMEM_BYTES)
PIECES = 4
SMALL = pl.CostEstimate(flops=1, bytes_accessed=1, transcendentals=0)
LARGE = pl.CostEstimate(flops=1 << 33, bytes_accessed=1, transcendentals=0)


def in_hbm(values):
    return [pltpu.with_memory_space_constraint(x, pltpu.HBM) for x in values]


def held(value):
    return pltpu.with_memory_space_constraint(value, pltpu.VMEM)


def routed_copies(route, counts, route_now, counts_now, sems):
    return [
        pltpu.make_async_copy(route, route_now, sems.at[0]),
        pltpu.make_async_copy(counts, counts_now, sems.at[1]),
    ]


def row_copies(source, target, sems):
    pieces = sems.shape[0]
    rows = source.shape[0] // pieces
    some = [pl.ds(i * rows, rows) for i in range(pieces)]
    return [
        pltpu.make_async_copy(source.at[place], target.at[place], sems.at[i])
        for i, place in enumerate(some)
    ]


def contracted(columns, wide):
    return lax.dot_general(
        columns, wide, (((0,), (0,)), ((), ())), preferred_element_type=jnp.float32
    )


def owner_columns(chip, sibling, share):
    me = lax.axis_index("dp")
    core = 1 - me % 2 if sibling else me % 2
    begin = (lax.bitwise_xor(me // 2, chip) * 2 + core) * share
    return pl.ds(pl.multiple_of(begin, share), share)


def sibling_kernel(experts, cuts, route, counts, inputs, hidden, *refs):
    outs = refs[: len(cuts)]
    columns, wide, rows, route_now, counts_now, column_sems, sems = refs[len(cuts) :]
    copies = routed_copies(route, counts, route_now, counts_now, sems)
    copies.append(pltpu.make_async_copy(hidden.at[1], rows, sems.at[2]))
    column_copies = row_copies(inputs.at[1], columns, column_sems)
    for copy in copies + column_copies:
        copy.start()
    for copy in copies:
        copy.wait()
    expand_hidden(route_now, counts_now, 1, rows, wide, route.shape[1], experts)
    for copy in column_copies:
        copy.wait()
    chips, _, _ = outs[0].shape
    share = cuts[-1].stop
    for k in range(chips):
        product = contracted(columns[:, owner_columns(k, True, share)], wide[...])
        for out, some in zip(outs, cuts):
            out[k] = product[some].astype(out.dtype)


def sibling_products(route, counts, inputs, hidden, chips, experts, cuts):
    _, rows, model = inputs.shape
    width = hidden.shape[2]
    columns = experts * width
    outs = [pltpu.VMEM((chips, some.stop - some.start, columns), jnp.bfloat16) for some in cuts]
    outs += [pltpu.VMEM((rows, model), jnp.bfloat16), pltpu.VMEM((rows, columns), jnp.bfloat16)]
    return pl.pallas_call(
        functools.partial(sibling_kernel, experts, cuts),
        in_specs=[ANYWHERE] * 4,
        out_specs=[IN_VMEM] * len(outs),
        out_shape=outs,
        scratch_shapes=[
            pltpu.VMEM((rows, width), jnp.bfloat16),
            pltpu.SMEM(route.shape, jnp.int32),
            pltpu.SMEM(counts.shape, jnp.int32),
            pltpu.SemaphoreType.DMA((PIECES,)),
            pltpu.SemaphoreType.DMA((3,)),
        ],
        compiler_params=PARAMS,
        cost_estimate=SMALL,
    )(*in_hbm((route, counts, inputs, hidden)))


def own_kernel(experts, route, counts, inputs, hidden, columns, wide, *refs):
    out, ahead, rows, route_now, counts_now, column_sems, sems = refs
    chips, share, _ = out.shape
    model = columns.shape[1]
    copies = routed_copies(route, counts, route_now, counts_now, sems)
    copies.append(pltpu.make_async_copy(hidden.at[0], rows, sems.at[2]))
    column_copies = row_copies(inputs.at[0], ahead.at[:, :model], column_sems)
    for copy in copies + column_copies:
        copy.start()

    def step(k, carry):
        product = contracted(columns[:, owner_columns(k, False, share)], wide[...])
        out[k] = product.astype(out.dtype)
        return carry

    lax.fori_loop(0, chips, step, 0)
    for copy in copies:
        copy.wait()
    expand_hidden(route_now, counts_now, 0, rows, ahead.at[:, model:], route.shape[1], experts)
    for copy in column_copies:
        copy.wait()


def own_products(route, counts, inputs, hidden, columns, wide, share, chips, experts):
    rows, model = columns.shape
    return pl.pallas_call(
        functools.partial(own_kernel, experts),
        in_specs=[ANYWHERE] * 4 + [IN_VMEM] * 2,
        out_specs=[IN_VMEM] * 2,
        out_shape=[
            pltpu.VMEM((chips, share, wide.shape[1]), jnp.bfloat16),
            pltpu.VMEM((rows, model + wide.shape[1]), jnp.bfloat16),
        ],
        scratch_shapes=[
            pltpu.VMEM(hidden.shape[1:], jnp.bfloat16),
            pltpu.SMEM(route.shape, jnp.int32),
            pltpu.SMEM(counts.shape, jnp.int32),
            pltpu.SemaphoreType.DMA((PIECES,)),
            pltpu.SemaphoreType.DMA((3,)),
        ],
        compiler_params=PARAMS,
        cost_estimate=SMALL,
    )(*in_hbm((route, counts, inputs, hidden)), held(columns), held(wide))


def join_kernel(some, crossed, own, received, *refs):
    chips = own.shape[0]
    core = lax.axis_index("dp") % 2
    for piece, out in enumerate(refs[-chips:]):
        k = neighbour(piece, core, chips, crossed)
        total = own[k, some].astype(jnp.float32) + received[k].astype(jnp.float32)
        out[...] = total.astype(out.dtype)


def joined(own, received, some, passed, crossed):
    chips, rows, columns = received.shape
    outs = [pltpu.VMEM(x.shape, x.dtype) for x in passed]
    outs += [pltpu.VMEM((rows, columns), jnp.float32)]
    outs += [pltpu.VMEM((rows, columns), jnp.bfloat16)] * (chips - 1)
    return pl.pallas_call(
        functools.partial(join_kernel, some, crossed),
        in_specs=[IN_VMEM] * (2 + len(passed)),
        out_specs=[IN_VMEM] * len(outs),
        out_shape=outs,
        input_output_aliases={2 + i: i for i in range(len(passed))},
        compiler_params=PARAMS,
        cost_estimate=SMALL,
    )(*map(held, (own, received, *passed)))


def pair_kernel(count, messages, ahead, other, *refs):
    kept, *sent = refs[count:]
    share, columns = kept.shape
    model = ahead.shape[1] - columns
    chips = 1 + max(place for place, _ in messages)
    for k in range(chips):
        chip = neighbour(k, lax.axis_index("dp") % 2, chips, True)
        place = owner_columns(chip, False, share)
        total = contracted(ahead[:, place], ahead[:, model:])
        total = total + contracted(other[:, place], other[:, model:])
        if k == 0:
            kept[...] = total
        for (chip, some), out in zip(messages, sent):
            if chip == k:
                out[...] = total[some].astype(out.dtype)


def paired(ahead, other, after, share, columns, messages):
    outs = [pltpu.VMEM((share, columns), jnp.float32)]
    outs += [pltpu.VMEM((some.stop - some.start, columns), jnp.bfloat16) for _, some in messages]
    return pl.pallas_call(
        functools.partial(pair_kernel, len(after), messages),
        in_specs=[IN_VMEM] * 2 + [ANYWHERE] * len(after),
        out_specs=[IN_VMEM] * len(outs),
        out_shape=outs,
        compiler_params=PARAMS,
        cost_estimate=SMALL,
    )(held(ahead), held(other), *after)


def total_kernel(count, kept, *refs):
    total = kept[...]
    for part in refs[:count]:
        total = total + part[...].astype(jnp.float32)
    out = refs[-1]
    out[...] = total.astype(out.dtype)


def totalled(kept, received, after, dtype, cost=None):
    count = len(received)
    return pl.pallas_call(
        functools.partial(total_kernel, count),
        in_specs=[IN_VMEM] * (1 + count) + [ANYWHERE] * len(after),
        out_specs=IN_VMEM,
        out_shape=pltpu.VMEM(kept.shape, dtype),
        compiler_params=PARAMS,
        cost_estimate=cost or SMALL,
    )(held(kept), *map(held, received), *after)


def update_kernel(experts, cuts, messages, kept, *refs):
    count, parts = len(messages), len(cuts)
    received, partners = refs[:count], refs[count : count + parts]
    first, second, *outs = refs[count + parts : count + parts + 6]
    grad_out, first_out, second_out, step_out, sems = refs[count + parts + 6 :]
    share, columns = kept.shape
    lines = columns // LANES
    chunks = columns // experts // LANES
    steps = sorted({0, *(some.stop for some in cuts), *(some.stop for _, some in messages)})
    copies = []
    for i, (begin, end) in enumerate(zip(steps, steps[1:])):
        rows = end - begin

        def inside(spans):
            return [
                (ref, slice(begin - span.start, end - span.start))
                for ref, span in spans
                if span.start <= begin and end <= span.stop
            ]

        terms = inside(zip(received, (span for _, span in messages)))
        terms += inside(zip(partners, cuts))
        for line in range(lines):
            expert, chunk = line // chunks, line % chunks
            some = slice(line * LANES, (line + 1) * LANES)
            grad = kept[begin:end, some]
            for part, place in terms:
                grad = grad + part[place, some].astype(jnp.float32)
            place = begin * lines + chunk * experts + expert
            grad_out[pl.ds(place, rows, stride=lines), :] = grad
        some = slice(begin * lines, end * lines)
        grad = grad_out[some, :]
        new_first = beta_one * first[some, :] + (1.0 - beta_one) * grad
        new_second = beta_two * second[some, :] + (1.0 - beta_two) * grad * grad
        first_out[some, :] = new_first
        second_out[some, :] = new_second
        step_out[some, :] = (
            new_first / bias_first / (jnp.sqrt(new_second / bias_second) + adam_epsilon)
        )
        for j, (source, target) in enumerate(
            zip((grad_out, first_out, second_out, step_out), outs)
        ):
            copy = pltpu.make_async_copy(source.at[some], target.at[some], sems.at[i, j])
            copy.start()
            copies.append(copy)
    for copy in copies:
        copy.wait()


def in_lines(value):
    rows, experts, width = value.shape
    value = value.reshape(rows, experts, width // LANES, LANES)
    return value.transpose(0, 2, 1, 3).reshape(-1, LANES)


def from_lines(value, shape):
    rows, experts, width = shape
    value = value.reshape(rows, width // LANES, experts, LANES)
    return value.transpose(0, 2, 1, 3).reshape(shape)


def updated(kept, received, partners, first, second, cuts, messages):
    most = 1 + len(cuts) + len(messages)
    lines = pltpu.VMEM((first.size // LANES, LANES), jnp.float32)
    outs = pl.pallas_call(
        functools.partial(update_kernel, first.shape[1], cuts, messages),
        in_specs=[IN_VMEM] * (3 + len(received) + len(partners)),
        out_specs=[ANYWHERE] * 4,
        out_shape=[jax.ShapeDtypeStruct(lines.shape, jnp.float32)] * 4,
        scratch_shapes=[pltpu.VMEM((first.size // LANES + 8, LANES), jnp.float32)]
        + [lines] * 3
        + [pltpu.SemaphoreType.DMA((most, 4))],
        compiler_params=PARAMS,
        cost_estimate=SMALL,
    )(*map(held, (kept, *received, *partners, in_lines(first), in_lines(second))))
    return [from_lines(out, first.shape) for out in outs]


def fast_device(saved_inputs, hidden_grads, block_expert, live_counts, first_moment, second_moment):
    chips = lax.axis_size("dp") // 2
    share, experts, width = first_moment.shape[1:]
    given = (block_expert[0, 0], live_counts[0, 0], saved_inputs[0, 0], hidden_grads[0, 0])
    cuts = [slice(0, share // 2), slice(share // 2, share)]
    places = range(1, chips)
    messages = [(k, slice(0, share)) for k in places]

    def to_owners(pieces, name, crossed):
        sent = []
        for piece, k in zip(pieces, places):
            chip = functools.partial(neighbour, k, chips=chips, crossed=crossed)
            sent.append(exchanged(piece, "dp", lambda i: 2 * chip(i % 2), f"{name}_to_chip_{k}"))
        return sent

    with jax.named_scope("sibling_products"):
        *sibling, columns, wide = sibling_products(*given, chips, experts, cuts)
    others = [exchanged(part, "dp", lambda i: 1, f"sibling_{i}") for i, part in enumerate(sibling)]
    with jax.named_scope("own_products"):
        own, ahead = own_products(*given, columns, wide, share, chips, experts)
    parts = []
    for i, (other, some) in enumerate(zip(others, cuts)):
        with jax.named_scope(f"join_{i}"):
            if i == 0:
                ahead, kept, *sent = joined(own, other, some, [ahead], True)
            else:
                kept, *sent = joined(own, other, some, [], False)
        parts.append((kept, to_owners(sent, f"one_part_{i}", False if i else True)))
    other_ahead = exchanged(ahead, "dp", lambda i: 1, "operand_exchange")
    with jax.named_scope("pair"):
        kept_zero, *sent_zero = paired(
            ahead, other_ahead, [parts[0][1][1]], share, experts * width, messages
        )
    received_zero = to_owners(sent_zero, "zero", True)
    partners = []
    for i, (kept, received) in enumerate(parts):
        with jax.named_scope(f"total_{i}"):
            total = totalled(kept, received, [kept_zero], jnp.bfloat16, LARGE if i else SMALL)
        partners.append(mirrored(total, f"mirror_{i}"))
    with jax.named_scope("update"):
        outs = updated(
            kept_zero, received_zero, partners, first_moment[0], second_moment[0], cuts, messages
        )
    return tuple(out[None] for out in outs)


def route_select(block_expert, live_counts, block):
    experts = jnp.arange(live_counts.shape[-1], dtype=jnp.int32)
    onehot = (block_expert[..., :, None] == experts).astype(jnp.int32)
    earlier = jnp.cumsum(onehot, axis=-2) - onehot
    before = jnp.sum(earlier * onehot, axis=-1)
    limits = jnp.sum(live_counts[..., None, :] * onehot, axis=-1)
    positions = before[..., None] * block + jnp.arange(block, dtype=jnp.int32)
    return positions < limits[..., None], onehot


def plain_device(saved_inputs, hidden_grads, block_expert, live_counts, first_moment, second_moment):
    _, _, _, rows, model_width = saved_inputs.shape
    hidden = hidden_grads.shape[4]
    blocks = block_expert.shape[3]
    block = rows // blocks
    live_rows, onehot = route_select(block_expert[0, 0], live_counts[0, 0], block)
    masked = hidden_grads.reshape(2, blocks, block, hidden) * live_rows[..., None].astype(
        jnp.bfloat16
    )
    wide = masked[:, :, :, None, :] * onehot[:, :, None, :, None].astype(jnp.bfloat16)
    wide = wide.reshape(2, rows, -1)
    parts = jnp.einsum(
        "krd,krc->kdc", saved_inputs[0, 0], wide, preferred_element_type=jnp.float32
    )
    sent = lax.optimization_barrier(parts[1].astype(jnp.bfloat16)).astype(jnp.float32)
    summed = lax.psum_scatter(
        jnp.stack([parts[0], sent], axis=1), "dp", scatter_dimension=0, tiled=True
    )
    grad_total = (summed[:, 0] + mirrored(summed[:, 1])).reshape(first_moment.shape[1:])
    new_first = beta_one * first_moment[0] + (1.0 - beta_one) * grad_total
    new_second = beta_two * second_moment[0] + (1.0 - beta_two) * grad_total * grad_total
    step_direction = new_first / bias_first / (jnp.sqrt(new_second / bias_second) + adam_epsilon)
    return (grad_total[None], new_first[None], new_second[None], step_direction[None])


def solution(mesh):
    in_specs = (
        P("section", "dp", None, None, None),
        P("section", "dp", None, None, None),
        P("section", "dp", None, None),
        P("section", "dp", None, None),
        P("section", "dp", None, None),
        P("section", "dp", None, None),
    )
    out_specs = (P("section", "dp", None, None),) * 4

    def run(*arrays):
        ranks = mesh.shape["dp"]
        paired = ranks > 2 and ranks & (ranks - 1) == 0
        per_device = fast_device if paired and arrays[4].shape[1] // ranks % LANES == 0 else plain_device
        return jax.shard_map(
            per_device, mesh=mesh, in_specs=in_specs, out_specs=out_specs, check_vma=False
        )(*arrays)

    return run
```

```python
import functools

import jax
import jax.numpy as jnp
from jax import lax
from jax.experimental import pallas as pl
from jax.experimental.pallas import tpu as pltpu
from jax.sharding import PartitionSpec as P

beta_one = 0.9
beta_two = 0.95
adam_epsilon = 1e-08
bias_first = 1.0 - 0.9**50
bias_second = 1.0 - 0.95**50

LANES = 128


def neighbour(piece, core, chips, crossed):
    if crossed and piece in (1, 2) and chips > 2:
        return 1 + core if piece == 1 else 2 - core
    return piece


def exchanged(value, axis, mask_of, name):
    count = lax.axis_size(axis)
    with jax.named_scope(name):
        return lax.ppermute(value, axis, [(i, i ^ mask_of(i)) for i in range(count)])


def mirrored(value, name="mirror"):
    count = lax.axis_size("section")
    pairs = [(source, (source + count // 2) % count) for source in range(count)]
    with jax.named_scope(name):
        return lax.ppermute(value, "section", pairs)


def expand_hidden(route, counts, direction, hidden, wide, blocks, experts):
    rows, width = hidden.shape
    block = rows // blocks
    seen = [jnp.int32(0) for _ in range(experts)]
    place = lax.broadcasted_iota(jnp.int32, (block, width), 0)
    for b in range(blocks):
        expert = route[direction, b]
        values = hidden[b * block : (b + 1) * block, :].astype(jnp.float32)
        for e in range(experts):
            named = expert == e
            limit = jnp.where(named, counts[direction, e] - seen[e] * block, 0)
            kept = jnp.where(place < limit, values, 0.0)
            wide[b * block : (b + 1) * block, e * width : (e + 1) * width] = kept.astype(wide.dtype)
            seen[e] = seen[e] + named.astype(jnp.int32)


VMEM_BYTES = 16 << 20
ANYWHERE = pl.BlockSpec(memory_space=pl.ANY)
IN_VMEM = pl.BlockSpec(memory_space=pltpu.VMEM)
PARAMS = pltpu.CompilerParams(vmem_limit_bytes=VMEM_BYTES)
PIECES = 4
STEPS = 4
SMALL = pl.CostEstimate(flops=1, bytes_accessed=1, transcendentals=0)
LARGE = pl.CostEstimate(flops=1 << 33, bytes_accessed=1, transcendentals=0)


def in_hbm(values):
    return [pltpu.with_memory_space_constraint(x, pltpu.HBM) for x in values]


def held(value):
    return pltpu.with_memory_space_constraint(value, pltpu.VMEM)


def routed_copies(route, counts, route_now, counts_now, sems):
    return [
        pltpu.make_async_copy(route, route_now, sems.at[0]),
        pltpu.make_async_copy(counts, counts_now, sems.at[1]),
    ]


def row_copies(source, target, sems):
    pieces = sems.shape[0]
    rows = source.shape[0] // pieces
    some = [pl.ds(i * rows, rows) for i in range(pieces)]
    return [
        pltpu.make_async_copy(source.at[place], target.at[place], sems.at[i])
        for i, place in enumerate(some)
    ]


def contracted(columns, wide):
    return lax.dot_general(
        columns, wide, (((0,), (0,)), ((), ())), preferred_element_type=jnp.float32
    )


def owner_columns(chip, sibling, share):
    me = lax.axis_index("dp")
    core = 1 - me % 2 if sibling else me % 2
    begin = (lax.bitwise_xor(me // 2, chip) * 2 + core) * share
    return pl.ds(pl.multiple_of(begin, share), share)


def sibling_kernel(experts, cuts, route, counts, inputs, hidden, *refs):
    outs = refs[: len(cuts)]
    columns, wide, rows, route_now, counts_now, column_sems, sems = refs[len(cuts) :]
    copies = routed_copies(route, counts, route_now, counts_now, sems)
    copies.append(pltpu.make_async_copy(hidden.at[1], rows, sems.at[2]))
    chips, _, _ = outs[0].shape
    share = cuts[-1].stop
    column_copies = []
    for sibling in (True, False):
        for k in range(chips):
            place = owner_columns(k, sibling, share)
            sem = column_sems.at[k + (0 if sibling else chips)]
            copy = pltpu.make_async_copy(inputs.at[1, :, place], columns.at[:, place], sem)
            column_copies.append(copy)
    for copy in copies[2:] + column_copies[:chips] + copies[:2] + column_copies[chips:]:
        copy.start()
    for copy in copies:
        copy.wait()
    expand_hidden(route_now, counts_now, 1, rows, wide, route.shape[1], experts)
    for copy in column_copies[:chips]:
        copy.wait()
    for k in range(chips):
        product = contracted(columns[:, owner_columns(k, True, share)], wide[...])
        for out, some in zip(outs, cuts):
            out[k] = product[some].astype(out.dtype)
    for copy in column_copies[chips:]:
        copy.wait()


def sibling_products(route, counts, inputs, hidden, chips, experts, cuts):
    _, rows, model = inputs.shape
    width = hidden.shape[2]
    columns = experts * width
    outs = [pltpu.VMEM((chips, some.stop - some.start, columns), jnp.bfloat16) for some in cuts]
    outs += [pltpu.VMEM((rows, model), jnp.bfloat16), pltpu.VMEM((rows, columns), jnp.bfloat16)]
    return pl.pallas_call(
        functools.partial(sibling_kernel, experts, cuts),
        in_specs=[ANYWHERE] * 4,
        out_specs=[IN_VMEM] * len(outs),
        out_shape=outs,
        scratch_shapes=[
            pltpu.VMEM((rows, width), jnp.bfloat16),
            pltpu.SMEM(route.shape, jnp.int32),
            pltpu.SMEM(counts.shape, jnp.int32),
            pltpu.SemaphoreType.DMA((2 * chips,)),
            pltpu.SemaphoreType.DMA((3,)),
        ],
        compiler_params=PARAMS,
        cost_estimate=SMALL,
    )(*in_hbm((route, counts, inputs, hidden)))


def own_kernel(experts, route, counts, inputs, hidden, columns, wide, *refs):
    out, ahead, rows, route_now, counts_now, column_sems, sems = refs
    chips, share, _ = out.shape
    model = columns.shape[1]
    copies = routed_copies(route, counts, route_now, counts_now, sems)
    copies.append(pltpu.make_async_copy(hidden.at[0], rows, sems.at[2]))
    column_copies = row_copies(inputs.at[0], ahead.at[:, :model], column_sems)
    for copy in copies + column_copies:
        copy.start()

    def step(k, carry):
        product = contracted(columns[:, owner_columns(k, False, share)], wide[...])
        out[k] = product.astype(out.dtype)
        return carry

    lax.fori_loop(0, chips, step, 0)
    for copy in copies:
        copy.wait()
    expand_hidden(route_now, counts_now, 0, rows, ahead.at[:, model:], route.shape[1], experts)
    for copy in column_copies:
        copy.wait()


def own_products(route, counts, inputs, hidden, columns, wide, share, chips, experts):
    rows, model = columns.shape
    return pl.pallas_call(
        functools.partial(own_kernel, experts),
        in_specs=[ANYWHERE] * 4 + [IN_VMEM] * 2,
        out_specs=[IN_VMEM] * 2,
        out_shape=[
            pltpu.VMEM((chips, share, wide.shape[1]), jnp.bfloat16),
            pltpu.VMEM((rows, model + wide.shape[1]), jnp.bfloat16),
        ],
        scratch_shapes=[
            pltpu.VMEM(hidden.shape[1:], jnp.bfloat16),
            pltpu.SMEM(route.shape, jnp.int32),
            pltpu.SMEM(counts.shape, jnp.int32),
            pltpu.SemaphoreType.DMA((PIECES,)),
            pltpu.SemaphoreType.DMA((3,)),
        ],
        compiler_params=PARAMS,
        cost_estimate=SMALL,
    )(*in_hbm((route, counts, inputs, hidden)), held(columns), held(wide))


def join_kernel(some, crossed, own, received, *refs):
    chips = own.shape[0]
    core = lax.axis_index("dp") % 2
    for piece, out in enumerate(refs[-chips:]):
        k = neighbour(piece, core, chips, crossed)
        total = own[k, some].astype(jnp.float32) + received[k].astype(jnp.float32)
        out[...] = total.astype(out.dtype)


def joined(own, received, some, passed, crossed):
    chips, rows, columns = received.shape
    outs = [pltpu.VMEM(x.shape, x.dtype) for x in passed]
    outs += [pltpu.VMEM((rows, columns), jnp.float32)]
    outs += [pltpu.VMEM((rows, columns), jnp.bfloat16)] * (chips - 1)
    return pl.pallas_call(
        functools.partial(join_kernel, some, crossed),
        in_specs=[IN_VMEM] * (2 + len(passed)),
        out_specs=[IN_VMEM] * len(outs),
        out_shape=outs,
        input_output_aliases={2 + i: i for i in range(len(passed))},
        compiler_params=PARAMS,
        cost_estimate=SMALL,
    )(*map(held, (own, received, *passed)))


def pair_kernel(count, messages, ahead, other, *refs):
    kept, *sent = refs[count:]
    share, columns = kept.shape
    model = ahead.shape[1] - columns
    chips = 1 + max(place for place, _ in messages)
    for k in range(chips):
        chip = neighbour(k, lax.axis_index("dp") % 2, chips, True)
        place = owner_columns(chip, False, share)
        total = contracted(ahead[:, place], ahead[:, model:])
        total = total + contracted(other[:, place], other[:, model:])
        if k == 0:
            kept[...] = total
        for (chip, some), out in zip(messages, sent):
            if chip == k:
                out[...] = total[some].astype(out.dtype)


def paired(ahead, other, after, share, columns, messages):
    outs = [pltpu.VMEM((share, columns), jnp.float32)]
    outs += [pltpu.VMEM((some.stop - some.start, columns), jnp.bfloat16) for _, some in messages]
    return pl.pallas_call(
        functools.partial(pair_kernel, len(after), messages),
        in_specs=[IN_VMEM] * 2 + [ANYWHERE] * len(after),
        out_specs=[IN_VMEM] * len(outs),
        out_shape=outs,
        compiler_params=PARAMS,
        cost_estimate=SMALL,
    )(held(ahead), held(other), *after)


def total_kernel(count, kept, *refs):
    total = kept[...]
    for part in refs[:count]:
        total = total + part[...].astype(jnp.float32)
    out = refs[-1]
    out[...] = total.astype(out.dtype)


def totalled(kept, received, after, dtype, cost=None):
    count = len(received)
    return pl.pallas_call(
        functools.partial(total_kernel, count),
        in_specs=[IN_VMEM] * (1 + count) + [ANYWHERE] * len(after),
        out_specs=IN_VMEM,
        out_shape=pltpu.VMEM(kept.shape, dtype),
        compiler_params=PARAMS,
        cost_estimate=cost or SMALL,
    )(held(kept), *map(held, received), *after)


def update_kernel(experts, cuts, messages, kept, *refs):
    count, parts = len(messages), len(cuts)
    received, partners = refs[:count], refs[count : count + parts]
    first, second, *outs = refs[count + parts : count + parts + 6]
    grad_out, first_out, second_out, step_out, sems = refs[count + parts + 6 :]
    share, columns = kept.shape
    lines = columns // LANES
    chunks = columns // experts // LANES
    steps = range(0, share + 1, share // STEPS)
    copies = []
    for i, (begin, end) in enumerate(zip(steps, steps[1:])):
        rows = end - begin

        def inside(spans):
            return [
                (ref, slice(begin - span.start, end - span.start))
                for ref, span in spans
                if span.start <= begin and end <= span.stop
            ]

        terms = inside(zip(received, (span for _, span in messages)))
        terms += inside(zip(partners, cuts))
        for line in range(lines):
            expert, chunk = line // chunks, line % chunks
            some = slice(line * LANES, (line + 1) * LANES)
            grad = kept[begin:end, some]
            for part, place in terms:
                grad = grad + part[place, some].astype(jnp.float32)
            place = begin * lines + chunk * experts + expert
            grad_out[pl.ds(place, rows, stride=lines), :] = grad
        some = slice(begin * lines, end * lines)
        grad = grad_out[some, :]
        new_first = beta_one * first[some, :] + (1.0 - beta_one) * grad
        new_second = beta_two * second[some, :] + (1.0 - beta_two) * grad * grad
        first_out[some, :] = new_first
        second_out[some, :] = new_second
        step_out[some, :] = (
            new_first / bias_first / (jnp.sqrt(new_second / bias_second) + adam_epsilon)
        )
        for j, (source, target) in enumerate(
            zip((grad_out, first_out, second_out, step_out), outs)
        ):
            copy = pltpu.make_async_copy(source.at[some], target.at[some], sems.at[i, j])
            copy.start()
            copies.append(copy)
    for copy in copies:
        copy.wait()


def in_lines(value):
    rows, experts, width = value.shape
    value = value.reshape(rows, experts, width // LANES, LANES)
    return value.transpose(0, 2, 1, 3).reshape(-1, LANES)


def from_lines(value, shape):
    rows, experts, width = shape
    value = value.reshape(rows, width // LANES, experts, LANES)
    return value.transpose(0, 2, 1, 3).reshape(shape)


def updated(kept, received, partners, first, second, cuts, messages):
    lines = pltpu.VMEM((first.size // LANES, LANES), jnp.float32)
    outs = pl.pallas_call(
        functools.partial(update_kernel, first.shape[1], cuts, messages),
        in_specs=[IN_VMEM] * (3 + len(received) + len(partners)),
        out_specs=[ANYWHERE] * 4,
        out_shape=[jax.ShapeDtypeStruct(lines.shape, jnp.float32)] * 4,
        scratch_shapes=[pltpu.VMEM((first.size // LANES + 8, LANES), jnp.float32)]
        + [lines] * 3
        + [pltpu.SemaphoreType.DMA((STEPS, 4))],
        compiler_params=PARAMS,
        cost_estimate=SMALL,
    )(*map(held, (kept, *received, *partners, in_lines(first), in_lines(second))))
    return [from_lines(out, first.shape) for out in outs]


def fast_device(saved_inputs, hidden_grads, block_expert, live_counts, first_moment, second_moment):
    chips = lax.axis_size("dp") // 2
    share, experts, width = first_moment.shape[1:]
    given = (block_expert[0, 0], live_counts[0, 0], saved_inputs[0, 0], hidden_grads[0, 0])
    cuts = [slice(0, share // 2), slice(share // 2, share)]
    places = range(1, chips)
    messages = [(k, slice(0, share)) for k in places]

    def to_owners(pieces, name, crossed):
        sent = []
        for piece, k in zip(pieces, places):
            chip = functools.partial(neighbour, k, chips=chips, crossed=crossed)
            sent.append(exchanged(piece, "dp", lambda i: 2 * chip(i % 2), f"{name}_to_chip_{k}"))
        return sent

    with jax.named_scope("sibling_products"):
        *sibling, columns, wide = sibling_products(*given, chips, experts, cuts)
    others = [exchanged(part, "dp", lambda i: 1, f"sibling_{i}") for i, part in enumerate(sibling)]
    with jax.named_scope("own_products"):
        own, ahead = own_products(*given, columns, wide, share, chips, experts)
    parts = []
    for i, (other, some) in enumerate(zip(others, cuts)):
        with jax.named_scope(f"join_{i}"):
            if i == 0:
                ahead, kept, *sent = joined(own, other, some, [ahead], True)
            else:
                kept, *sent = joined(own, other, some, [], False)
        parts.append((kept, to_owners(sent, f"one_part_{i}", False if i else True)))
    other_ahead = exchanged(ahead, "dp", lambda i: 1, "operand_exchange")
    with jax.named_scope("pair"):
        kept_zero, *sent_zero = paired(
            ahead, other_ahead, [parts[0][1][1]], share, experts * width, messages
        )
    received_zero = to_owners(sent_zero, "zero", True)
    partners = []
    for i, (kept, received) in enumerate(parts):
        with jax.named_scope(f"total_{i}"):
            total = totalled(kept, received, [kept_zero], jnp.bfloat16, LARGE if i else SMALL)
        partners.append(mirrored(total, f"mirror_{i}"))
    with jax.named_scope("update"):
        outs = updated(
            kept_zero, received_zero, partners, first_moment[0], second_moment[0], cuts, messages
        )
    return tuple(out[None] for out in outs)


def route_select(block_expert, live_counts, block):
    experts = jnp.arange(live_counts.shape[-1], dtype=jnp.int32)
    onehot = (block_expert[..., :, None] == experts).astype(jnp.int32)
    earlier = jnp.cumsum(onehot, axis=-2) - onehot
    before = jnp.sum(earlier * onehot, axis=-1)
    limits = jnp.sum(live_counts[..., None, :] * onehot, axis=-1)
    positions = before[..., None] * block + jnp.arange(block, dtype=jnp.int32)
    return positions < limits[..., None], onehot


def plain_device(saved_inputs, hidden_grads, block_expert, live_counts, first_moment, second_moment):
    _, _, _, rows, model_width = saved_inputs.shape
    hidden = hidden_grads.shape[4]
    blocks = block_expert.shape[3]
    block = rows // blocks
    live_rows, onehot = route_select(block_expert[0, 0], live_counts[0, 0], block)
    masked = hidden_grads.reshape(2, blocks, block, hidden) * live_rows[..., None].astype(
        jnp.bfloat16
    )
    wide = masked[:, :, :, None, :] * onehot[:, :, None, :, None].astype(jnp.bfloat16)
    wide = wide.reshape(2, rows, -1)
    parts = jnp.einsum(
        "krd,krc->kdc", saved_inputs[0, 0], wide, preferred_element_type=jnp.float32
    )
    sent = lax.optimization_barrier(parts[1].astype(jnp.bfloat16)).astype(jnp.float32)
    summed = lax.psum_scatter(
        jnp.stack([parts[0], sent], axis=1), "dp", scatter_dimension=0, tiled=True
    )
    grad_total = (summed[:, 0] + mirrored(summed[:, 1])).reshape(first_moment.shape[1:])
    new_first = beta_one * first_moment[0] + (1.0 - beta_one) * grad_total
    new_second = beta_two * second_moment[0] + (1.0 - beta_two) * grad_total * grad_total
    step_direction = new_first / bias_first / (jnp.sqrt(new_second / bias_second) + adam_epsilon)
    return (grad_total[None], new_first[None], new_second[None], step_direction[None])


def solution(mesh):
    in_specs = (
        P("section", "dp", None, None, None),
        P("section", "dp", None, None, None),
        P("section", "dp", None, None),
        P("section", "dp", None, None),
        P("section", "dp", None, None),
        P("section", "dp", None, None),
    )
    out_specs = (P("section", "dp", None, None),) * 4

    def run(*arrays):
        ranks = mesh.shape["dp"]
        paired = ranks > 2 and ranks & (ranks - 1) == 0
        per_device = fast_device if paired and arrays[4].shape[1] // ranks % LANES == 0 else plain_device
        return jax.shard_map(
            per_device, mesh=mesh, in_specs=in_specs, out_specs=out_specs, check_vma=False
        )(*arrays)

    return run
```

```python
import functools

import jax
import jax.numpy as jnp
from jax import lax
from jax.experimental import pallas as pl
from jax.experimental.pallas import tpu as pltpu
from jax.sharding import PartitionSpec as P

beta_one = 0.9
beta_two = 0.95
adam_epsilon = 1e-08
bias_first = 1.0 - 0.9**50
bias_second = 1.0 - 0.95**50

LANES = 128


def neighbour(piece, core, chips, crossed):
    if crossed and piece in (1, 2) and chips > 2:
        return 1 + core if piece == 1 else 2 - core
    return piece


def exchanged(value, axis, mask_of, name):
    count = lax.axis_size(axis)
    with jax.named_scope(name):
        return lax.ppermute(value, axis, [(i, i ^ mask_of(i)) for i in range(count)])


def mirrored(value, name="mirror"):
    count = lax.axis_size("section")
    pairs = [(source, (source + count // 2) % count) for source in range(count)]
    with jax.named_scope(name):
        return lax.ppermute(value, "section", pairs)


def expand_hidden(route, counts, direction, hidden, wide, blocks, experts):
    rows, width = hidden.shape
    block = rows // blocks
    seen = [jnp.int32(0) for _ in range(experts)]
    place = lax.broadcasted_iota(jnp.int32, (block, width), 0)
    for b in range(blocks):
        expert = route[direction, b]
        values = hidden[b * block : (b + 1) * block, :].astype(jnp.float32)
        for e in range(experts):
            named = expert == e
            limit = jnp.where(named, counts[direction, e] - seen[e] * block, 0)
            kept = jnp.where(place < limit, values, 0.0)
            wide[b * block : (b + 1) * block, e * width : (e + 1) * width] = kept.astype(wide.dtype)
            seen[e] = seen[e] + named.astype(jnp.int32)


VMEM_BYTES = 16 << 20
ANYWHERE = pl.BlockSpec(memory_space=pl.ANY)
IN_VMEM = pl.BlockSpec(memory_space=pltpu.VMEM)
PARAMS = pltpu.CompilerParams(vmem_limit_bytes=VMEM_BYTES)
PIECES = 4
STEPS = 4
SMALL = pl.CostEstimate(flops=1, bytes_accessed=1, transcendentals=0)
LARGE = pl.CostEstimate(flops=1 << 33, bytes_accessed=1, transcendentals=0)


def in_hbm(values):
    return [pltpu.with_memory_space_constraint(x, pltpu.HBM) for x in values]


def held(value):
    return pltpu.with_memory_space_constraint(value, pltpu.VMEM)


def routed_copies(route, counts, route_now, counts_now, sems):
    return [
        pltpu.make_async_copy(route, route_now, sems.at[0]),
        pltpu.make_async_copy(counts, counts_now, sems.at[1]),
    ]


def row_copies(source, target, sems):
    pieces = sems.shape[0]
    rows = source.shape[0] // pieces
    some = [pl.ds(i * rows, rows) for i in range(pieces)]
    return [
        pltpu.make_async_copy(source.at[place], target.at[place], sems.at[i])
        for i, place in enumerate(some)
    ]


def contracted(columns, wide):
    return lax.dot_general(
        columns, wide, (((0,), (0,)), ((), ())), preferred_element_type=jnp.float32
    )


def owner_columns(chip, sibling, share, some=None):
    me = lax.axis_index("dp")
    core = 1 - me % 2 if sibling else me % 2
    begin = (lax.bitwise_xor(me // 2, chip) * 2 + core) * share
    some = some or slice(0, share)
    width = some.stop - some.start
    return pl.ds(pl.multiple_of(begin + some.start, width), width)


def sibling_kernel(experts, share, route, counts, inputs, hidden, *refs):
    out, columns, wide, rows, route_now, counts_now, column_sems, sems = refs
    copies = routed_copies(route, counts, route_now, counts_now, sems)
    copies.append(pltpu.make_async_copy(hidden.at[1], rows, sems.at[2]))
    chips, part, _ = out.shape
    column_copies = []
    for sibling in (True, False):
        for k in range(chips):
            place = owner_columns(k, sibling, share)
            sem = column_sems.at[k + (0 if sibling else chips)]
            copy = pltpu.make_async_copy(inputs.at[1, :, place], columns.at[:, place], sem)
            column_copies.append(copy)
    for copy in copies[2:] + column_copies[:chips] + copies[:2] + column_copies[chips:]:
        copy.start()
    for copy in copies:
        copy.wait()
    expand_hidden(route_now, counts_now, 1, rows, wide, route.shape[1], experts)
    for copy in column_copies[:chips]:
        copy.wait()
    for k in range(chips):
        place = owner_columns(k, True, share, slice(0, part))
        out[k] = contracted(columns[:, place], wide[...]).astype(out.dtype)
    for copy in column_copies[chips:]:
        copy.wait()


def sibling_products(route, counts, inputs, hidden, chips, experts, cuts):
    _, rows, model = inputs.shape
    width = hidden.shape[2]
    columns = experts * width
    outs = [pltpu.VMEM((chips, cuts[0].stop, columns), jnp.bfloat16)]
    outs += [pltpu.VMEM((rows, model), jnp.bfloat16), pltpu.VMEM((rows, columns), jnp.bfloat16)]
    return pl.pallas_call(
        functools.partial(sibling_kernel, experts, cuts[-1].stop),
        in_specs=[ANYWHERE] * 4,
        out_specs=[IN_VMEM] * len(outs),
        out_shape=outs,
        scratch_shapes=[
            pltpu.VMEM((rows, width), jnp.bfloat16),
            pltpu.SMEM(route.shape, jnp.int32),
            pltpu.SMEM(counts.shape, jnp.int32),
            pltpu.SemaphoreType.DMA((2 * chips,)),
            pltpu.SemaphoreType.DMA((3,)),
        ],
        compiler_params=PARAMS,
        cost_estimate=SMALL,
    )(*in_hbm((route, counts, inputs, hidden)))


def own_kernel(experts, route, counts, inputs, hidden, columns, wide, *refs):
    out, later, ahead, rows, route_now, counts_now, column_sems, sems = refs
    chips, share, _ = out.shape
    part = later.shape[1]
    model = columns.shape[1]
    copies = routed_copies(route, counts, route_now, counts_now, sems)
    copies.append(pltpu.make_async_copy(hidden.at[0], rows, sems.at[2]))
    column_copies = row_copies(inputs.at[0], ahead.at[:, :model], column_sems)
    for copy in copies + column_copies:
        copy.start()

    def step(k, carry):
        product = contracted(columns[:, owner_columns(k, False, share)], wide[...])
        out[k] = product.astype(out.dtype)
        place = owner_columns(k, True, share, slice(share - part, share))
        later[k] = contracted(columns[:, place], wide[...]).astype(later.dtype)
        return carry

    lax.fori_loop(0, chips, step, 0)
    for copy in copies:
        copy.wait()
    expand_hidden(route_now, counts_now, 0, rows, ahead.at[:, model:], route.shape[1], experts)
    for copy in column_copies:
        copy.wait()


def own_products(route, counts, inputs, hidden, columns, wide, share, chips, experts, cuts):
    rows, model = columns.shape
    return pl.pallas_call(
        functools.partial(own_kernel, experts),
        in_specs=[ANYWHERE] * 4 + [IN_VMEM] * 2,
        out_specs=[IN_VMEM] * 3,
        out_shape=[
            pltpu.VMEM((chips, share, wide.shape[1]), jnp.bfloat16),
            pltpu.VMEM((chips, share - cuts[0].stop, wide.shape[1]), jnp.bfloat16),
            pltpu.VMEM((rows, model + wide.shape[1]), jnp.bfloat16),
        ],
        scratch_shapes=[
            pltpu.VMEM(hidden.shape[1:], jnp.bfloat16),
            pltpu.SMEM(route.shape, jnp.int32),
            pltpu.SMEM(counts.shape, jnp.int32),
            pltpu.SemaphoreType.DMA((PIECES,)),
            pltpu.SemaphoreType.DMA((3,)),
        ],
        compiler_params=PARAMS,
        cost_estimate=SMALL,
    )(*in_hbm((route, counts, inputs, hidden)), held(columns), held(wide))


def join_kernel(some, crossed, own, received, *refs):
    chips = own.shape[0]
    core = lax.axis_index("dp") % 2
    for piece, out in enumerate(refs[-chips:]):
        k = neighbour(piece, core, chips, crossed)
        total = own[k, some].astype(jnp.float32) + received[k].astype(jnp.float32)
        out[...] = total.astype(out.dtype)


def joined(own, received, some, passed, crossed):
    chips, rows, columns = received.shape
    outs = [pltpu.VMEM(x.shape, x.dtype) for x in passed]
    outs += [pltpu.VMEM((rows, columns), jnp.float32)]
    outs += [pltpu.VMEM((rows, columns), jnp.bfloat16)] * (chips - 1)
    return pl.pallas_call(
        functools.partial(join_kernel, some, crossed),
        in_specs=[IN_VMEM] * (2 + len(passed)),
        out_specs=[IN_VMEM] * len(outs),
        out_shape=outs,
        input_output_aliases={2 + i: i for i in range(len(passed))},
        compiler_params=PARAMS,
        cost_estimate=SMALL,
    )(*map(held, (own, received, *passed)))


def pair_kernel(count, messages, ahead, other, *refs):
    kept, *sent = refs[count:]
    share, columns = kept.shape
    model = ahead.shape[1] - columns
    chips = 1 + max(place for place, _ in messages)
    for k in range(chips):
        chip = neighbour(k, lax.axis_index("dp") % 2, chips, True)
        place = owner_columns(chip, False, share)
        total = contracted(ahead[:, place], ahead[:, model:])
        total = total + contracted(other[:, place], other[:, model:])
        if k == 0:
            kept[...] = total
        for (chip, some), out in zip(messages, sent):
            if chip == k:
                out[...] = total[some].astype(out.dtype)


def paired(ahead, other, after, share, columns, messages):
    outs = [pltpu.VMEM((share, columns), jnp.float32)]
    outs += [pltpu.VMEM((some.stop - some.start, columns), jnp.bfloat16) for _, some in messages]
    return pl.pallas_call(
        functools.partial(pair_kernel, len(after), messages),
        in_specs=[IN_VMEM] * 2 + [ANYWHERE] * len(after),
        out_specs=[IN_VMEM] * len(outs),
        out_shape=outs,
        compiler_params=PARAMS,
        cost_estimate=SMALL,
    )(held(ahead), held(other), *after)


def total_kernel(count, kept, *refs):
    total = kept[...]
    for part in refs[:count]:
        total = total + part[...].astype(jnp.float32)
    out = refs[-1]
    out[...] = total.astype(out.dtype)


def totalled(kept, received, after, dtype, cost=None):
    count = len(received)
    return pl.pallas_call(
        functools.partial(total_kernel, count),
        in_specs=[IN_VMEM] * (1 + count) + [ANYWHERE] * len(after),
        out_specs=IN_VMEM,
        out_shape=pltpu.VMEM(kept.shape, dtype),
        compiler_params=PARAMS,
        cost_estimate=cost or SMALL,
    )(held(kept), *map(held, received), *after)


def update_kernel(experts, cuts, messages, kept, *refs):
    count, parts = len(messages), len(cuts)
    received, partners = refs[:count], refs[count : count + parts]
    first, second, *outs = refs[count + parts : count + parts + 6]
    grad_out, first_out, second_out, step_out, sems = refs[count + parts + 6 :]
    share, columns = kept.shape
    lines = columns // LANES
    chunks = columns // experts // LANES
    steps = range(0, share + 1, share // STEPS)
    copies = []
    for i, (begin, end) in enumerate(zip(steps, steps[1:])):
        rows = end - begin

        def inside(spans):
            return [
                (ref, slice(begin - span.start, end - span.start))
                for ref, span in spans
                if span.start <= begin and end <= span.stop
            ]

        terms = inside(zip(received, (span for _, span in messages)))
        terms += inside(zip(partners, cuts))
        for line in range(lines):
            expert, chunk = line // chunks, line % chunks
            some = slice(line * LANES, (line + 1) * LANES)
            grad = kept[begin:end, some]
            for part, place in terms:
                grad = grad + part[place, some].astype(jnp.float32)
            place = begin * lines + chunk * experts + expert
            grad_out[pl.ds(place, rows, stride=lines), :] = grad
        some = slice(begin * lines, end * lines)
        grad = grad_out[some, :]
        new_first = beta_one * first[some, :] + (1.0 - beta_one) * grad
        new_second = beta_two * second[some, :] + (1.0 - beta_two) * grad * grad
        first_out[some, :] = new_first
        second_out[some, :] = new_second
        step_out[some, :] = (
            new_first / bias_first / (jnp.sqrt(new_second / bias_second) + adam_epsilon)
        )
        for j, (source, target) in enumerate(
            zip((grad_out, first_out, second_out, step_out), outs)
        ):
            copy = pltpu.make_async_copy(source.at[some], target.at[some], sems.at[i, j])
            copy.start()
            copies.append(copy)
    for copy in copies:
        copy.wait()


def in_lines(value):
    rows, experts, width = value.shape
    value = value.reshape(rows, experts, width // LANES, LANES)
    return value.transpose(0, 2, 1, 3).reshape(-1, LANES)


def from_lines(value, shape):
    rows, experts, width = shape
    value = value.reshape(rows, width // LANES, experts, LANES)
    return value.transpose(0, 2, 1, 3).reshape(shape)


def updated(kept, received, partners, first, second, cuts, messages):
    lines = pltpu.VMEM((first.size // LANES, LANES), jnp.float32)
    outs = pl.pallas_call(
        functools.partial(update_kernel, first.shape[1], cuts, messages),
        in_specs=[IN_VMEM] * (3 + len(received) + len(partners)),
        out_specs=[ANYWHERE] * 4,
        out_shape=[jax.ShapeDtypeStruct(lines.shape, jnp.float32)] * 4,
        scratch_shapes=[pltpu.VMEM((first.size // LANES + 8, LANES), jnp.float32)]
        + [lines] * 3
        + [pltpu.SemaphoreType.DMA((STEPS, 4))],
        compiler_params=PARAMS,
        cost_estimate=SMALL,
    )(*map(held, (kept, *received, *partners, in_lines(first), in_lines(second))))
    return [from_lines(out, first.shape) for out in outs]


def fast_device(saved_inputs, hidden_grads, block_expert, live_counts, first_moment, second_moment):
    chips = lax.axis_size("dp") // 2
    share, experts, width = first_moment.shape[1:]
    given = (block_expert[0, 0], live_counts[0, 0], saved_inputs[0, 0], hidden_grads[0, 0])
    cuts = [slice(0, share // 2), slice(share // 2, share)]
    places = range(1, chips)
    messages = [(k, slice(0, share)) for k in places]

    def to_owners(pieces, name, crossed):
        sent = []
        for piece, k in zip(pieces, places):
            chip = functools.partial(neighbour, k, chips=chips, crossed=crossed)
            sent.append(exchanged(piece, "dp", lambda i: 2 * chip(i % 2), f"{name}_to_chip_{k}"))
        return sent

    with jax.named_scope("sibling_products"):
        sibling, columns, wide = sibling_products(*given, chips, experts, cuts)
    others = [exchanged(sibling, "dp", lambda i: 1, "sibling_0")]
    with jax.named_scope("own_products"):
        own, later, ahead = own_products(*given, columns, wide, share, chips, experts, cuts)
    others.append(exchanged(later, "dp", lambda i: 1, "sibling_1"))
    parts = []
    for i, (other, some) in enumerate(zip(others, cuts)):
        with jax.named_scope(f"join_{i}"):
            if i == 0:
                ahead, kept, *sent = joined(own, other, some, [ahead], True)
            else:
                kept, *sent = joined(own, other, some, [], False)
        parts.append((kept, to_owners(sent, f"one_part_{i}", False if i else True)))
    other_ahead = exchanged(ahead, "dp", lambda i: 1, "operand_exchange")
    with jax.named_scope("pair"):
        kept_zero, *sent_zero = paired(
            ahead, other_ahead, [parts[0][1][1]], share, experts * width, messages
        )
    received_zero = to_owners(sent_zero, "zero", True)
    partners = []
    for i, (kept, received) in enumerate(parts):
        with jax.named_scope(f"total_{i}"):
            total = totalled(kept, received, [kept_zero], jnp.bfloat16, LARGE if i else SMALL)
        partners.append(mirrored(total, f"mirror_{i}"))
    with jax.named_scope("update"):
        outs = updated(
            kept_zero, received_zero, partners, first_moment[0], second_moment[0], cuts, messages
        )
    return tuple(out[None] for out in outs)


def route_select(block_expert, live_counts, block):
    experts = jnp.arange(live_counts.shape[-1], dtype=jnp.int32)
    onehot = (block_expert[..., :, None] == experts).astype(jnp.int32)
    earlier = jnp.cumsum(onehot, axis=-2) - onehot
    before = jnp.sum(earlier * onehot, axis=-1)
    limits = jnp.sum(live_counts[..., None, :] * onehot, axis=-1)
    positions = before[..., None] * block + jnp.arange(block, dtype=jnp.int32)
    return positions < limits[..., None], onehot


def plain_device(saved_inputs, hidden_grads, block_expert, live_counts, first_moment, second_moment):
    _, _, _, rows, model_width = saved_inputs.shape
    hidden = hidden_grads.shape[4]
    blocks = block_expert.shape[3]
    block = rows // blocks
    live_rows, onehot = route_select(block_expert[0, 0], live_counts[0, 0], block)
    masked = hidden_grads.reshape(2, blocks, block, hidden) * live_rows[..., None].astype(
        jnp.bfloat16
    )
    wide = masked[:, :, :, None, :] * onehot[:, :, None, :, None].astype(jnp.bfloat16)
    wide = wide.reshape(2, rows, -1)
    parts = jnp.einsum(
        "krd,krc->kdc", saved_inputs[0, 0], wide, preferred_element_type=jnp.float32
    )
    sent = lax.optimization_barrier(parts[1].astype(jnp.bfloat16)).astype(jnp.float32)
    summed = lax.psum_scatter(
        jnp.stack([parts[0], sent], axis=1), "dp", scatter_dimension=0, tiled=True
    )
    grad_total = (summed[:, 0] + mirrored(summed[:, 1])).reshape(first_moment.shape[1:])
    new_first = beta_one * first_moment[0] + (1.0 - beta_one) * grad_total
    new_second = beta_two * second_moment[0] + (1.0 - beta_two) * grad_total * grad_total
    step_direction = new_first / bias_first / (jnp.sqrt(new_second / bias_second) + adam_epsilon)
    return (grad_total[None], new_first[None], new_second[None], step_direction[None])


def solution(mesh):
    in_specs = (
        P("section", "dp", None, None, None),
        P("section", "dp", None, None, None),
        P("section", "dp", None, None),
        P("section", "dp", None, None),
        P("section", "dp", None, None),
        P("section", "dp", None, None),
    )
    out_specs = (P("section", "dp", None, None),) * 4

    def run(*arrays):
        ranks = mesh.shape["dp"]
        paired = ranks > 2 and ranks & (ranks - 1) == 0
        per_device = fast_device if paired and arrays[4].shape[1] // ranks % LANES == 0 else plain_device
        return jax.shard_map(
            per_device, mesh=mesh, in_specs=in_specs, out_specs=out_specs, check_vma=False
        )(*arrays)

    return run
```

```python
import functools

import jax
import jax.numpy as jnp
from jax import lax
from jax.experimental import pallas as pl
from jax.experimental.pallas import tpu as pltpu
from jax.sharding import PartitionSpec as P

beta_one = 0.9
beta_two = 0.95
adam_epsilon = 1e-08
bias_first = 1.0 - 0.9**50
bias_second = 1.0 - 0.95**50

LANES = 128


def neighbour(piece, core, chips, crossed):
    if crossed and piece in (1, 2) and chips > 2:
        return 1 + core if piece == 1 else 2 - core
    return piece


def exchanged(value, axis, mask_of, name):
    count = lax.axis_size(axis)
    with jax.named_scope(name):
        return lax.ppermute(value, axis, [(i, i ^ mask_of(i)) for i in range(count)])


def mirrored(value, name="mirror"):
    count = lax.axis_size("section")
    pairs = [(source, (source + count // 2) % count) for source in range(count)]
    with jax.named_scope(name):
        return lax.ppermute(value, "section", pairs)


def expand_hidden(route, counts, direction, hidden, wide, blocks, experts):
    rows, width = hidden.shape
    block = rows // blocks
    seen = [jnp.int32(0) for _ in range(experts)]
    place = lax.broadcasted_iota(jnp.int32, (block, width), 0)
    for b in range(blocks):
        expert = route[direction, b]
        values = hidden[b * block : (b + 1) * block, :].astype(jnp.float32)
        for e in range(experts):
            named = expert == e
            limit = jnp.where(named, counts[direction, e] - seen[e] * block, 0)
            kept = jnp.where(place < limit, values, 0.0)
            wide[b * block : (b + 1) * block, e * width : (e + 1) * width] = kept.astype(wide.dtype)
            seen[e] = seen[e] + named.astype(jnp.int32)


VMEM_BYTES = 16 << 20
ANYWHERE = pl.BlockSpec(memory_space=pl.ANY)
IN_VMEM = pl.BlockSpec(memory_space=pltpu.VMEM)
PARAMS = pltpu.CompilerParams(vmem_limit_bytes=VMEM_BYTES)
PIECES = 4
STEPS = 4
SMALL = pl.CostEstimate(flops=1, bytes_accessed=1, transcendentals=0)
LARGE = pl.CostEstimate(flops=1 << 33, bytes_accessed=1, transcendentals=0)


def in_hbm(values):
    return [pltpu.with_memory_space_constraint(x, pltpu.HBM) for x in values]


def held(value):
    return pltpu.with_memory_space_constraint(value, pltpu.VMEM)


def routed_copies(route, counts, route_now, counts_now, sems):
    return [
        pltpu.make_async_copy(route, route_now, sems.at[0]),
        pltpu.make_async_copy(counts, counts_now, sems.at[1]),
    ]


def row_copies(source, target, sems):
    pieces = sems.shape[0]
    rows = source.shape[0] // pieces
    some = [pl.ds(i * rows, rows) for i in range(pieces)]
    return [
        pltpu.make_async_copy(source.at[place], target.at[place], sems.at[i])
        for i, place in enumerate(some)
    ]


def contracted(columns, wide):
    return lax.dot_general(
        columns, wide, (((0,), (0,)), ((), ())), preferred_element_type=jnp.float32
    )


def owner_columns(chip, sibling, share, some=None):
    me = lax.axis_index("dp")
    core = 1 - me % 2 if sibling else me % 2
    begin = (lax.bitwise_xor(me // 2, chip) * 2 + core) * share
    some = some or slice(0, share)
    width = some.stop - some.start
    return pl.ds(pl.multiple_of(begin + some.start, width), width)


def sibling_kernel(experts, share, route, counts, inputs, hidden, *refs):
    out, columns, wide, rows, route_now, counts_now, column_sems, sems = refs
    copies = routed_copies(route, counts, route_now, counts_now, sems)
    copies.append(pltpu.make_async_copy(hidden.at[1], rows, sems.at[2]))
    chips, part, _ = out.shape
    column_copies = []
    for sibling in (True, False):
        for k in range(chips):
            place = owner_columns(k, sibling, share)
            sem = column_sems.at[k + (0 if sibling else chips)]
            copy = pltpu.make_async_copy(inputs.at[1, :, place], columns.at[:, place], sem)
            column_copies.append(copy)
    for copy in copies[2:] + column_copies[:chips] + copies[:2] + column_copies[chips:]:
        copy.start()
    for copy in copies:
        copy.wait()
    expand_hidden(route_now, counts_now, 1, rows, wide, route.shape[1], experts)
    for copy in column_copies[:chips]:
        copy.wait()
    for k in range(chips):
        place = owner_columns(k, True, share, slice(0, part))
        out[k] = contracted(columns[:, place], wide[...]).astype(out.dtype)
    for copy in column_copies[chips:]:
        copy.wait()


def sibling_products(route, counts, inputs, hidden, chips, experts, cuts):
    _, rows, model = inputs.shape
    width = hidden.shape[2]
    columns = experts * width
    outs = [pltpu.VMEM((chips, cuts[0].stop, columns), jnp.bfloat16)]
    outs += [pltpu.VMEM((rows, model), jnp.bfloat16), pltpu.VMEM((rows, columns), jnp.bfloat16)]
    return pl.pallas_call(
        functools.partial(sibling_kernel, experts, cuts[-1].stop),
        in_specs=[ANYWHERE] * 4,
        out_specs=[IN_VMEM] * len(outs),
        out_shape=outs,
        scratch_shapes=[
            pltpu.VMEM((rows, width), jnp.bfloat16),
            pltpu.SMEM(route.shape, jnp.int32),
            pltpu.SMEM(counts.shape, jnp.int32),
            pltpu.SemaphoreType.DMA((2 * chips,)),
            pltpu.SemaphoreType.DMA((3,)),
        ],
        compiler_params=PARAMS,
        cost_estimate=SMALL,
    )(*in_hbm((route, counts, inputs, hidden)))


def own_kernel(experts, route, counts, inputs, hidden, columns, wide, *refs):
    out, later, ahead, rows, route_now, counts_now, column_sems, sems = refs
    chips, share, _ = out.shape
    part = later.shape[1]
    model = columns.shape[1]
    copies = routed_copies(route, counts, route_now, counts_now, sems)
    copies.append(pltpu.make_async_copy(hidden.at[0], rows, sems.at[2]))
    column_copies = row_copies(inputs.at[0], ahead.at[:, :model], column_sems)
    for copy in copies + column_copies:
        copy.start()

    def step(i, carry):
        for k in (2 * i, 2 * i + 1):
            product = contracted(columns[:, owner_columns(k, False, share)], wide[...])
            out[k] = product.astype(out.dtype)
            place = owner_columns(k, True, share, slice(share - part, share))
            later[k] = contracted(columns[:, place], wide[...]).astype(later.dtype)
        return carry

    lax.fori_loop(0, chips // 2, step, 0)
    for copy in copies:
        copy.wait()
    expand_hidden(route_now, counts_now, 0, rows, ahead.at[:, model:], route.shape[1], experts)
    for copy in column_copies:
        copy.wait()


def own_products(route, counts, inputs, hidden, columns, wide, share, chips, experts, cuts):
    rows, model = columns.shape
    return pl.pallas_call(
        functools.partial(own_kernel, experts),
        in_specs=[ANYWHERE] * 4 + [IN_VMEM] * 2,
        out_specs=[IN_VMEM] * 3,
        out_shape=[
            pltpu.VMEM((chips, share, wide.shape[1]), jnp.bfloat16),
            pltpu.VMEM((chips, share - cuts[0].stop, wide.shape[1]), jnp.bfloat16),
            pltpu.VMEM((rows, model + wide.shape[1]), jnp.bfloat16),
        ],
        scratch_shapes=[
            pltpu.VMEM(hidden.shape[1:], jnp.bfloat16),
            pltpu.SMEM(route.shape, jnp.int32),
            pltpu.SMEM(counts.shape, jnp.int32),
            pltpu.SemaphoreType.DMA((PIECES,)),
            pltpu.SemaphoreType.DMA((3,)),
        ],
        compiler_params=PARAMS,
        cost_estimate=SMALL,
    )(*in_hbm((route, counts, inputs, hidden)), held(columns), held(wide))


def join_kernel(some, crossed, own, received, *refs):
    chips = own.shape[0]
    core = lax.axis_index("dp") % 2
    for piece, out in enumerate(refs[-chips:]):
        k = neighbour(piece, core, chips, crossed)
        total = own[k, some].astype(jnp.float32) + received[k].astype(jnp.float32)
        out[...] = total.astype(out.dtype)


def joined(own, received, some, passed, crossed):
    chips, rows, columns = received.shape
    outs = [pltpu.VMEM(x.shape, x.dtype) for x in passed]
    outs += [pltpu.VMEM((rows, columns), jnp.float32)]
    outs += [pltpu.VMEM((rows, columns), jnp.bfloat16)] * (chips - 1)
    return pl.pallas_call(
        functools.partial(join_kernel, some, crossed),
        in_specs=[IN_VMEM] * (2 + len(passed)),
        out_specs=[IN_VMEM] * len(outs),
        out_shape=outs,
        input_output_aliases={2 + i: i for i in range(len(passed))},
        compiler_params=PARAMS,
        cost_estimate=SMALL,
    )(*map(held, (own, received, *passed)))


def pair_kernel(count, messages, ahead, other, *refs):
    kept, *sent = refs[count:]
    share, columns = kept.shape
    model = ahead.shape[1] - columns
    chips = 1 + max(place for place, _ in messages)
    for k in range(chips):
        chip = neighbour(k, lax.axis_index("dp") % 2, chips, True)
        place = owner_columns(chip, False, share)
        total = contracted(ahead[:, place], ahead[:, model:])
        total = total + contracted(other[:, place], other[:, model:])
        if k == 0:
            kept[...] = total
        for (chip, some), out in zip(messages, sent):
            if chip == k:
                out[...] = total[some].astype(out.dtype)


def paired(ahead, other, after, share, columns, messages):
    outs = [pltpu.VMEM((share, columns), jnp.float32)]
    outs += [pltpu.VMEM((some.stop - some.start, columns), jnp.bfloat16) for _, some in messages]
    return pl.pallas_call(
        functools.partial(pair_kernel, len(after), messages),
        in_specs=[IN_VMEM] * 2 + [ANYWHERE] * len(after),
        out_specs=[IN_VMEM] * len(outs),
        out_shape=outs,
        compiler_params=PARAMS,
        cost_estimate=SMALL,
    )(held(ahead), held(other), *after)


def total_kernel(count, kept, *refs):
    total = kept[...]
    for part in refs[:count]:
        total = total + part[...].astype(jnp.float32)
    out = refs[-1]
    out[...] = total.astype(out.dtype)


def totalled(kept, received, after, dtype, cost=None):
    count = len(received)
    return pl.pallas_call(
        functools.partial(total_kernel, count),
        in_specs=[IN_VMEM] * (1 + count) + [ANYWHERE] * len(after),
        out_specs=IN_VMEM,
        out_shape=pltpu.VMEM(kept.shape, dtype),
        compiler_params=PARAMS,
        cost_estimate=cost or SMALL,
    )(held(kept), *map(held, received), *after)


def update_kernel(experts, cuts, messages, kept, *refs):
    count, parts = len(messages), len(cuts)
    received, partners = refs[:count], refs[count : count + parts]
    first, second, *outs = refs[count + parts : count + parts + 6]
    grad_out, first_out, second_out, step_out, sems = refs[count + parts + 6 :]
    share, columns = kept.shape
    lines = columns // LANES
    chunks = columns // experts // LANES
    steps = range(0, share + 1, share // STEPS)
    copies = []
    for i, (begin, end) in enumerate(zip(steps, steps[1:])):
        rows = end - begin

        def inside(spans):
            return [
                (ref, slice(begin - span.start, end - span.start))
                for ref, span in spans
                if span.start <= begin and end <= span.stop
            ]

        terms = inside(zip(received, (span for _, span in messages)))
        terms += inside(zip(partners, cuts))
        for line in range(lines):
            expert, chunk = line // chunks, line % chunks
            some = slice(line * LANES, (line + 1) * LANES)
            grad = kept[begin:end, some]
            for part, place in terms:
                grad = grad + part[place, some].astype(jnp.float32)
            place = begin * lines + chunk * experts + expert
            grad_out[pl.ds(place, rows, stride=lines), :] = grad
        some = slice(begin * lines, end * lines)
        grad = grad_out[some, :]
        new_first = beta_one * first[some, :] + (1.0 - beta_one) * grad
        new_second = beta_two * second[some, :] + (1.0 - beta_two) * grad * grad
        first_out[some, :] = new_first
        second_out[some, :] = new_second
        step_out[some, :] = (
            new_first / bias_first / (jnp.sqrt(new_second / bias_second) + adam_epsilon)
        )
        for j, (source, target) in enumerate(
            zip((grad_out, first_out, second_out, step_out), outs)
        ):
            copy = pltpu.make_async_copy(source.at[some], target.at[some], sems.at[i, j])
            copy.start()
            copies.append(copy)
    for copy in copies:
        copy.wait()


def in_lines(value):
    rows, experts, width = value.shape
    value = value.reshape(rows, experts, width // LANES, LANES)
    return value.transpose(0, 2, 1, 3).reshape(-1, LANES)


def from_lines(value, shape):
    rows, experts, width = shape
    value = value.reshape(rows, width // LANES, experts, LANES)
    return value.transpose(0, 2, 1, 3).reshape(shape)


def updated(kept, received, partners, first, second, cuts, messages):
    lines = pltpu.VMEM((first.size // LANES, LANES), jnp.float32)
    outs = pl.pallas_call(
        functools.partial(update_kernel, first.shape[1], cuts, messages),
        in_specs=[IN_VMEM] * (3 + len(received) + len(partners)),
        out_specs=[ANYWHERE] * 4,
        out_shape=[jax.ShapeDtypeStruct(lines.shape, jnp.float32)] * 4,
        scratch_shapes=[pltpu.VMEM((first.size // LANES + 8, LANES), jnp.float32)]
        + [lines] * 3
        + [pltpu.SemaphoreType.DMA((STEPS, 4))],
        compiler_params=PARAMS,
        cost_estimate=SMALL,
    )(*map(held, (kept, *received, *partners, in_lines(first), in_lines(second))))
    return [from_lines(out, first.shape) for out in outs]


def fast_device(saved_inputs, hidden_grads, block_expert, live_counts, first_moment, second_moment):
    chips = lax.axis_size("dp") // 2
    share, experts, width = first_moment.shape[1:]
    given = (block_expert[0, 0], live_counts[0, 0], saved_inputs[0, 0], hidden_grads[0, 0])
    cuts = [slice(0, share // 2), slice(share // 2, share)]
    places = range(1, chips)
    messages = [(k, slice(0, share)) for k in places]

    def to_owners(pieces, name, crossed):
        sent = []
        for piece, k in zip(pieces, places):
            chip = functools.partial(neighbour, k, chips=chips, crossed=crossed)
            sent.append(exchanged(piece, "dp", lambda i: 2 * chip(i % 2), f"{name}_to_chip_{k}"))
        return sent

    with jax.named_scope("sibling_products"):
        sibling, columns, wide = sibling_products(*given, chips, experts, cuts)
    others = [exchanged(sibling, "dp", lambda i: 1, "sibling_0")]
    with jax.named_scope("own_products"):
        own, later, ahead = own_products(*given, columns, wide, share, chips, experts, cuts)
    others.append(exchanged(later, "dp", lambda i: 1, "sibling_1"))
    parts = []
    for i, (other, some) in enumerate(zip(others, cuts)):
        with jax.named_scope(f"join_{i}"):
            if i == 0:
                ahead, kept, *sent = joined(own, other, some, [ahead], True)
            else:
                kept, *sent = joined(own, other, some, [], False)
        parts.append((kept, to_owners(sent, f"one_part_{i}", False if i else True)))
    other_ahead = exchanged(ahead, "dp", lambda i: 1, "operand_exchange")
    with jax.named_scope("pair"):
        kept_zero, *sent_zero = paired(
            ahead, other_ahead, [parts[0][1][1]], share, experts * width, messages
        )
    received_zero = to_owners(sent_zero, "zero", True)
    partners = []
    for i, (kept, received) in enumerate(parts):
        with jax.named_scope(f"total_{i}"):
            total = totalled(kept, received, [kept_zero], jnp.bfloat16, LARGE if i else SMALL)
        partners.append(mirrored(total, f"mirror_{i}"))
    with jax.named_scope("update"):
        outs = updated(
            kept_zero, received_zero, partners, first_moment[0], second_moment[0], cuts, messages
        )
    return tuple(out[None] for out in outs)


def route_select(block_expert, live_counts, block):
    experts = jnp.arange(live_counts.shape[-1], dtype=jnp.int32)
    onehot = (block_expert[..., :, None] == experts).astype(jnp.int32)
    earlier = jnp.cumsum(onehot, axis=-2) - onehot
    before = jnp.sum(earlier * onehot, axis=-1)
    limits = jnp.sum(live_counts[..., None, :] * onehot, axis=-1)
    positions = before[..., None] * block + jnp.arange(block, dtype=jnp.int32)
    return positions < limits[..., None], onehot


def plain_device(saved_inputs, hidden_grads, block_expert, live_counts, first_moment, second_moment):
    _, _, _, rows, model_width = saved_inputs.shape
    hidden = hidden_grads.shape[4]
    blocks = block_expert.shape[3]
    block = rows // blocks
    live_rows, onehot = route_select(block_expert[0, 0], live_counts[0, 0], block)
    masked = hidden_grads.reshape(2, blocks, block, hidden) * live_rows[..., None].astype(
        jnp.bfloat16
    )
    wide = masked[:, :, :, None, :] * onehot[:, :, None, :, None].astype(jnp.bfloat16)
    wide = wide.reshape(2, rows, -1)
    parts = jnp.einsum(
        "krd,krc->kdc", saved_inputs[0, 0], wide, preferred_element_type=jnp.float32
    )
    sent = lax.optimization_barrier(parts[1].astype(jnp.bfloat16)).astype(jnp.float32)
    summed = lax.psum_scatter(
        jnp.stack([parts[0], sent], axis=1), "dp", scatter_dimension=0, tiled=True
    )
    grad_total = (summed[:, 0] + mirrored(summed[:, 1])).reshape(first_moment.shape[1:])
    new_first = beta_one * first_moment[0] + (1.0 - beta_one) * grad_total
    new_second = beta_two * second_moment[0] + (1.0 - beta_two) * grad_total * grad_total
    step_direction = new_first / bias_first / (jnp.sqrt(new_second / bias_second) + adam_epsilon)
    return (grad_total[None], new_first[None], new_second[None], step_direction[None])


def solution(mesh):
    in_specs = (
        P("section", "dp", None, None, None),
        P("section", "dp", None, None, None),
        P("section", "dp", None, None),
        P("section", "dp", None, None),
        P("section", "dp", None, None),
        P("section", "dp", None, None),
    )
    out_specs = (P("section", "dp", None, None),) * 4

    def run(*arrays):
        ranks = mesh.shape["dp"]
        paired = ranks > 2 and ranks & (ranks - 1) == 0
        per_device = fast_device if paired and arrays[4].shape[1] // ranks % LANES == 0 else plain_device
        return jax.shard_map(
            per_device, mesh=mesh, in_specs=in_specs, out_specs=out_specs, check_vma=False
        )(*arrays)

    return run
```

```python
import functools

import jax
import jax.numpy as jnp
from jax import lax
from jax.experimental import pallas as pl
from jax.experimental.pallas import tpu as pltpu
from jax.sharding import PartitionSpec as P

beta_one = 0.9
beta_two = 0.95
adam_epsilon = 1e-08
bias_first = 1.0 - 0.9**50
bias_second = 1.0 - 0.95**50

LANES = 128


def neighbour(piece, core, chips, crossed):
    if crossed and piece in (1, 2) and chips > 2:
        return 1 + core if piece == 1 else 2 - core
    return piece


def exchanged(value, axis, mask_of, name):
    count = lax.axis_size(axis)
    with jax.named_scope(name):
        return lax.ppermute(value, axis, [(i, i ^ mask_of(i)) for i in range(count)])


def mirrored(value, name="mirror"):
    count = lax.axis_size("section")
    pairs = [(source, (source + count // 2) % count) for source in range(count)]
    with jax.named_scope(name):
        return lax.ppermute(value, "section", pairs)


def expand_hidden(route, counts, direction, hidden, wide, blocks, experts):
    rows, width = hidden.shape
    block = rows // blocks
    seen = [jnp.int32(0) for _ in range(experts)]
    place = lax.broadcasted_iota(jnp.int32, (block, width), 0)
    for b in range(blocks):
        expert = route[direction, b]
        values = hidden[b * block : (b + 1) * block, :].astype(jnp.float32)
        for e in range(experts):
            named = expert == e
            limit = jnp.where(named, counts[direction, e] - seen[e] * block, 0)
            kept = jnp.where(place < limit, values, 0.0)
            wide[b * block : (b + 1) * block, e * width : (e + 1) * width] = kept.astype(wide.dtype)
            seen[e] = seen[e] + named.astype(jnp.int32)


VMEM_BYTES = 16 << 20
ANYWHERE = pl.BlockSpec(memory_space=pl.ANY)
IN_VMEM = pl.BlockSpec(memory_space=pltpu.VMEM)
PARAMS = pltpu.CompilerParams(vmem_limit_bytes=VMEM_BYTES)
PIECES = 2
STEPS = 4
SMALL = pl.CostEstimate(flops=1, bytes_accessed=1, transcendentals=0)
LARGE = pl.CostEstimate(flops=1 << 33, bytes_accessed=1, transcendentals=0)


def in_hbm(values):
    return [pltpu.with_memory_space_constraint(x, pltpu.HBM) for x in values]


def held(value):
    return pltpu.with_memory_space_constraint(value, pltpu.VMEM)


def routed_copies(route, counts, route_now, counts_now, sems):
    return [
        pltpu.make_async_copy(route, route_now, sems.at[0]),
        pltpu.make_async_copy(counts, counts_now, sems.at[1]),
    ]


def row_copies(source, target, sems):
    pieces = sems.shape[0]
    rows = source.shape[0] // pieces
    some = [pl.ds(i * rows, rows) for i in range(pieces)]
    return [
        pltpu.make_async_copy(source.at[place], target.at[place], sems.at[i])
        for i, place in enumerate(some)
    ]


def contracted(columns, wide):
    return lax.dot_general(
        columns, wide, (((0,), (0,)), ((), ())), preferred_element_type=jnp.float32
    )


def owner_columns(chip, sibling, share, some=None):
    me = lax.axis_index("dp")
    core = 1 - me % 2 if sibling else me % 2
    begin = (lax.bitwise_xor(me // 2, chip) * 2 + core) * share
    some = some or slice(0, share)
    width = some.stop - some.start
    return pl.ds(pl.multiple_of(begin + some.start, width), width)


def sibling_kernel(experts, share, route, counts, inputs, hidden, *refs):
    out, columns, wide, rows, route_now, counts_now, column_sems, sems = refs
    copies = routed_copies(route, counts, route_now, counts_now, sems)
    copies.append(pltpu.make_async_copy(hidden.at[1], rows, sems.at[2]))
    chips, part, _ = out.shape
    column_copies = []
    for sibling in (True, False):
        for k in range(chips):
            place = owner_columns(k, sibling, share)
            sem = column_sems.at[k + (0 if sibling else chips)]
            copy = pltpu.make_async_copy(inputs.at[1, :, place], columns.at[:, place], sem)
            column_copies.append(copy)
    for copy in copies[2:] + column_copies[:chips] + copies[:2] + column_copies[chips:]:
        copy.start()
    for copy in copies:
        copy.wait()
    expand_hidden(route_now, counts_now, 1, rows, wide, route.shape[1], experts)
    for copy in column_copies[:chips]:
        copy.wait()
    for k in range(chips):
        place = owner_columns(k, True, share, slice(0, part))
        out[k] = contracted(columns[:, place], wide[...]).astype(out.dtype)
    for copy in column_copies[chips:]:
        copy.wait()


def sibling_products(route, counts, inputs, hidden, chips, experts, cuts):
    _, rows, model = inputs.shape
    width = hidden.shape[2]
    columns = experts * width
    outs = [pltpu.VMEM((chips, cuts[0].stop, columns), jnp.bfloat16)]
    outs += [pltpu.VMEM((rows, model), jnp.bfloat16), pltpu.VMEM((rows, columns), jnp.bfloat16)]
    return pl.pallas_call(
        functools.partial(sibling_kernel, experts, cuts[-1].stop),
        in_specs=[ANYWHERE] * 4,
        out_specs=[IN_VMEM] * len(outs),
        out_shape=outs,
        scratch_shapes=[
            pltpu.VMEM((rows, width), jnp.bfloat16),
            pltpu.SMEM(route.shape, jnp.int32),
            pltpu.SMEM(counts.shape, jnp.int32),
            pltpu.SemaphoreType.DMA((2 * chips,)),
            pltpu.SemaphoreType.DMA((3,)),
        ],
        compiler_params=PARAMS,
        cost_estimate=SMALL,
    )(*in_hbm((route, counts, inputs, hidden)))


def own_kernel(experts, route, counts, inputs, hidden, columns, wide, *refs):
    out, later, ahead, rows, route_now, counts_now, column_sems, sems = refs
    chips, share, _ = out.shape
    part = later.shape[1]
    model = columns.shape[1]
    copies = routed_copies(route, counts, route_now, counts_now, sems)
    copies.append(pltpu.make_async_copy(hidden.at[0], rows, sems.at[2]))
    column_copies = row_copies(inputs.at[0], ahead.at[:, :model], column_sems)
    for copy in copies + column_copies:
        copy.start()

    def step(i, carry):
        for k in (2 * i, 2 * i + 1):
            product = contracted(columns[:, owner_columns(k, False, share)], wide[...])
            out[k] = product.astype(out.dtype)
            place = owner_columns(k, True, share, slice(share - part, share))
            later[k] = contracted(columns[:, place], wide[...]).astype(later.dtype)
        return carry

    lax.fori_loop(0, chips // 2, step, 0)
    for copy in copies:
        copy.wait()
    expand_hidden(route_now, counts_now, 0, rows, ahead.at[:, model:], route.shape[1], experts)
    for copy in column_copies:
        copy.wait()


def own_products(route, counts, inputs, hidden, columns, wide, share, chips, experts, cuts):
    rows, model = columns.shape
    return pl.pallas_call(
        functools.partial(own_kernel, experts),
        in_specs=[ANYWHERE] * 4 + [IN_VMEM] * 2,
        out_specs=[IN_VMEM] * 3,
        out_shape=[
            pltpu.VMEM((chips, share, wide.shape[1]), jnp.bfloat16),
            pltpu.VMEM((chips, share - cuts[0].stop, wide.shape[1]), jnp.bfloat16),
            pltpu.VMEM((rows, model + wide.shape[1]), jnp.bfloat16),
        ],
        scratch_shapes=[
            pltpu.VMEM(hidden.shape[1:], jnp.bfloat16),
            pltpu.SMEM(route.shape, jnp.int32),
            pltpu.SMEM(counts.shape, jnp.int32),
            pltpu.SemaphoreType.DMA((PIECES,)),
            pltpu.SemaphoreType.DMA((3,)),
        ],
        compiler_params=PARAMS,
        cost_estimate=SMALL,
    )(*in_hbm((route, counts, inputs, hidden)), held(columns), held(wide))


def join_kernel(some, crossed, own, received, *refs):
    chips = own.shape[0]
    core = lax.axis_index("dp") % 2
    for piece, out in enumerate(refs[-chips:]):
        k = neighbour(piece, core, chips, crossed)
        total = own[k, some].astype(jnp.float32) + received[k].astype(jnp.float32)
        out[...] = total.astype(out.dtype)


def joined(own, received, some, passed, crossed):
    chips, rows, columns = received.shape
    outs = [pltpu.VMEM(x.shape, x.dtype) for x in passed]
    outs += [pltpu.VMEM((rows, columns), jnp.float32)]
    outs += [pltpu.VMEM((rows, columns), jnp.bfloat16)] * (chips - 1)
    return pl.pallas_call(
        functools.partial(join_kernel, some, crossed),
        in_specs=[IN_VMEM] * (2 + len(passed)),
        out_specs=[IN_VMEM] * len(outs),
        out_shape=outs,
        input_output_aliases={2 + i: i for i in range(len(passed))},
        compiler_params=PARAMS,
        cost_estimate=SMALL,
    )(*map(held, (own, received, *passed)))


def pair_kernel(count, messages, ahead, other, *refs):
    kept, *sent = refs[count:]
    share, columns = kept.shape
    model = ahead.shape[1] - columns
    chips = 1 + max(place for place, _ in messages)
    for k in range(chips):
        chip = neighbour(k, lax.axis_index("dp") % 2, chips, True)
        place = owner_columns(chip, False, share)
        total = contracted(ahead[:, place], ahead[:, model:])
        total = total + contracted(other[:, place], other[:, model:])
        if k == 0:
            kept[...] = total
        for (chip, some), out in zip(messages, sent):
            if chip == k:
                out[...] = total[some].astype(out.dtype)


def paired(ahead, other, after, share, columns, messages):
    outs = [pltpu.VMEM((share, columns), jnp.float32)]
    outs += [pltpu.VMEM((some.stop - some.start, columns), jnp.bfloat16) for _, some in messages]
    return pl.pallas_call(
        functools.partial(pair_kernel, len(after), messages),
        in_specs=[IN_VMEM] * 2 + [ANYWHERE] * len(after),
        out_specs=[IN_VMEM] * len(outs),
        out_shape=outs,
        compiler_params=PARAMS,
        cost_estimate=SMALL,
    )(held(ahead), held(other), *after)


def total_kernel(count, kept, *refs):
    total = kept[...]
    for part in refs[:count]:
        total = total + part[...].astype(jnp.float32)
    out = refs[-1]
    out[...] = total.astype(out.dtype)


def totalled(kept, received, after, dtype, cost=None):
    count = len(received)
    return pl.pallas_call(
        functools.partial(total_kernel, count),
        in_specs=[IN_VMEM] * (1 + count) + [ANYWHERE] * len(after),
        out_specs=IN_VMEM,
        out_shape=pltpu.VMEM(kept.shape, dtype),
        compiler_params=PARAMS,
        cost_estimate=cost or SMALL,
    )(held(kept), *map(held, received), *after)


def update_kernel(experts, cuts, messages, kept, *refs):
    count, parts = len(messages), len(cuts)
    received, partners = refs[:count], refs[count : count + parts]
    first, second, *outs = refs[count + parts : count + parts + 6]
    grad_out, first_out, second_out, step_out, sems = refs[count + parts + 6 :]
    share, columns = kept.shape
    lines = columns // LANES
    chunks = columns // experts // LANES
    steps = range(0, share + 1, share // STEPS)
    copies = []
    for i, (begin, end) in enumerate(zip(steps, steps[1:])):
        rows = end - begin

        def inside(spans):
            return [
                (ref, slice(begin - span.start, end - span.start))
                for ref, span in spans
                if span.start <= begin and end <= span.stop
            ]

        terms = inside(zip(received, (span for _, span in messages)))
        terms += inside(zip(partners, cuts))
        for line in range(lines):
            expert, chunk = line // chunks, line % chunks
            some = slice(line * LANES, (line + 1) * LANES)
            grad = kept[begin:end, some]
            for part, place in terms:
                grad = grad + part[place, some].astype(jnp.float32)
            place = begin * lines + chunk * experts + expert
            grad_out[pl.ds(place, rows, stride=lines), :] = grad
        some = slice(begin * lines, end * lines)
        grad = grad_out[some, :]
        new_first = beta_one * first[some, :] + (1.0 - beta_one) * grad
        new_second = beta_two * second[some, :] + (1.0 - beta_two) * grad * grad
        first_out[some, :] = new_first
        second_out[some, :] = new_second
        step_out[some, :] = (
            new_first / bias_first / (jnp.sqrt(new_second / bias_second) + adam_epsilon)
        )
        for j, (source, target) in enumerate(
            zip((grad_out, first_out, second_out, step_out), outs)
        ):
            copy = pltpu.make_async_copy(source.at[some], target.at[some], sems.at[i, j])
            copy.start()
            copies.append(copy)
    for copy in copies:
        copy.wait()


def in_lines(value):
    rows, experts, width = value.shape
    value = value.reshape(rows, experts, width // LANES, LANES)
    return value.transpose(0, 2, 1, 3).reshape(-1, LANES)


def from_lines(value, shape):
    rows, experts, width = shape
    value = value.reshape(rows, width // LANES, experts, LANES)
    return value.transpose(0, 2, 1, 3).reshape(shape)


def updated(kept, received, partners, first, second, cuts, messages):
    lines = pltpu.VMEM((first.size // LANES, LANES), jnp.float32)
    outs = pl.pallas_call(
        functools.partial(update_kernel, first.shape[1], cuts, messages),
        in_specs=[IN_VMEM] * (3 + len(received) + len(partners)),
        out_specs=[ANYWHERE] * 4,
        out_shape=[jax.ShapeDtypeStruct(lines.shape, jnp.float32)] * 4,
        scratch_shapes=[pltpu.VMEM((first.size // LANES + 8, LANES), jnp.float32)]
        + [lines] * 3
        + [pltpu.SemaphoreType.DMA((STEPS, 4))],
        compiler_params=PARAMS,
        cost_estimate=SMALL,
    )(*map(held, (kept, *received, *partners, in_lines(first), in_lines(second))))
    return [from_lines(out, first.shape) for out in outs]


def fast_device(saved_inputs, hidden_grads, block_expert, live_counts, first_moment, second_moment):
    chips = lax.axis_size("dp") // 2
    share, experts, width = first_moment.shape[1:]
    given = (block_expert[0, 0], live_counts[0, 0], saved_inputs[0, 0], hidden_grads[0, 0])
    cuts = [slice(0, share // 2), slice(share // 2, share)]
    places = range(1, chips)
    messages = [(k, slice(0, share)) for k in places]

    def to_owners(pieces, name, crossed):
        sent = []
        for piece, k in zip(pieces, places):
            chip = functools.partial(neighbour, k, chips=chips, crossed=crossed)
            sent.append(exchanged(piece, "dp", lambda i: 2 * chip(i % 2), f"{name}_to_chip_{k}"))
        return sent

    with jax.named_scope("sibling_products"):
        sibling, columns, wide = sibling_products(*given, chips, experts, cuts)
    others = [exchanged(sibling, "dp", lambda i: 1, "sibling_0")]
    with jax.named_scope("own_products"):
        own, later, ahead = own_products(*given, columns, wide, share, chips, experts, cuts)
    others.append(exchanged(later, "dp", lambda i: 1, "sibling_1"))
    parts = []
    for i, (other, some) in enumerate(zip(others, cuts)):
        with jax.named_scope(f"join_{i}"):
            if i == 0:
                ahead, kept, *sent = joined(own, other, some, [ahead], True)
            else:
                kept, *sent = joined(own, other, some, [], False)
        parts.append((kept, to_owners(sent, f"one_part_{i}", False if i else True)))
    other_ahead = exchanged(ahead, "dp", lambda i: 1, "operand_exchange")
    with jax.named_scope("pair"):
        kept_zero, *sent_zero = paired(
            ahead, other_ahead, [parts[0][1][1]], share, experts * width, messages
        )
    received_zero = to_owners(sent_zero, "zero", True)
    partners = []
    for i, (kept, received) in enumerate(parts):
        with jax.named_scope(f"total_{i}"):
            total = totalled(kept, received, [kept_zero], jnp.bfloat16, LARGE if i else SMALL)
        partners.append(mirrored(total, f"mirror_{i}"))
    with jax.named_scope("update"):
        outs = updated(
            kept_zero, received_zero, partners, first_moment[0], second_moment[0], cuts, messages
        )
    return tuple(out[None] for out in outs)


def route_select(block_expert, live_counts, block):
    experts = jnp.arange(live_counts.shape[-1], dtype=jnp.int32)
    onehot = (block_expert[..., :, None] == experts).astype(jnp.int32)
    earlier = jnp.cumsum(onehot, axis=-2) - onehot
    before = jnp.sum(earlier * onehot, axis=-1)
    limits = jnp.sum(live_counts[..., None, :] * onehot, axis=-1)
    positions = before[..., None] * block + jnp.arange(block, dtype=jnp.int32)
    return positions < limits[..., None], onehot


def plain_device(saved_inputs, hidden_grads, block_expert, live_counts, first_moment, second_moment):
    _, _, _, rows, model_width = saved_inputs.shape
    hidden = hidden_grads.shape[4]
    blocks = block_expert.shape[3]
    block = rows // blocks
    live_rows, onehot = route_select(block_expert[0, 0], live_counts[0, 0], block)
    masked = hidden_grads.reshape(2, blocks, block, hidden) * live_rows[..., None].astype(
        jnp.bfloat16
    )
    wide = masked[:, :, :, None, :] * onehot[:, :, None, :, None].astype(jnp.bfloat16)
    wide = wide.reshape(2, rows, -1)
    parts = jnp.einsum(
        "krd,krc->kdc", saved_inputs[0, 0], wide, preferred_element_type=jnp.float32
    )
    sent = lax.optimization_barrier(parts[1].astype(jnp.bfloat16)).astype(jnp.float32)
    summed = lax.psum_scatter(
        jnp.stack([parts[0], sent], axis=1), "dp", scatter_dimension=0, tiled=True
    )
    grad_total = (summed[:, 0] + mirrored(summed[:, 1])).reshape(first_moment.shape[1:])
    new_first = beta_one * first_moment[0] + (1.0 - beta_one) * grad_total
    new_second = beta_two * second_moment[0] + (1.0 - beta_two) * grad_total * grad_total
    step_direction = new_first / bias_first / (jnp.sqrt(new_second / bias_second) + adam_epsilon)
    return (grad_total[None], new_first[None], new_second[None], step_direction[None])


def solution(mesh):
    in_specs = (
        P("section", "dp", None, None, None),
        P("section", "dp", None, None, None),
        P("section", "dp", None, None),
        P("section", "dp", None, None),
        P("section", "dp", None, None),
        P("section", "dp", None, None),
    )
    out_specs = (P("section", "dp", None, None),) * 4

    def run(*arrays):
        ranks = mesh.shape["dp"]
        paired = ranks > 2 and ranks & (ranks - 1) == 0
        per_device = fast_device if paired and arrays[4].shape[1] // ranks % LANES == 0 else plain_device
        return jax.shard_map(
            per_device, mesh=mesh, in_specs=in_specs, out_specs=out_specs, check_vma=False
        )(*arrays)

    return run
```

```python
import functools

import jax
import jax.numpy as jnp
from jax import lax
from jax.experimental import pallas as pl
from jax.experimental.pallas import tpu as pltpu
from jax.sharding import PartitionSpec as P

beta_one = 0.9
beta_two = 0.95
adam_epsilon = 1e-08
bias_first = 1.0 - 0.9**50
bias_second = 1.0 - 0.95**50

LANES = 128


def neighbour(piece, core, chips, crossed):
    if crossed and piece in (1, 2) and chips > 2:
        return 1 + core if piece == 1 else 2 - core
    return piece


def exchanged(value, axis, mask_of, name):
    count = lax.axis_size(axis)
    with jax.named_scope(name):
        return lax.ppermute(value, axis, [(i, i ^ mask_of(i)) for i in range(count)])


def mirrored(value, name="mirror"):
    count = lax.axis_size("section")
    pairs = [(source, (source + count // 2) % count) for source in range(count)]
    with jax.named_scope(name):
        return lax.ppermute(value, "section", pairs)


def expand_hidden(route, counts, direction, hidden, wide, blocks, experts):
    rows, width = hidden.shape
    block = rows // blocks
    seen = [jnp.int32(0) for _ in range(experts)]
    place = lax.broadcasted_iota(jnp.int32, (block, width), 0)
    for b in range(blocks):
        expert = route[direction, b]
        values = hidden[b * block : (b + 1) * block, :].astype(jnp.float32)
        for e in range(experts):
            named = expert == e
            limit = jnp.where(named, counts[direction, e] - seen[e] * block, 0)
            kept = jnp.where(place < limit, values, 0.0)
            wide[b * block : (b + 1) * block, e * width : (e + 1) * width] = kept.astype(wide.dtype)
            seen[e] = seen[e] + named.astype(jnp.int32)


VMEM_BYTES = 16 << 20
ANYWHERE = pl.BlockSpec(memory_space=pl.ANY)
IN_VMEM = pl.BlockSpec(memory_space=pltpu.VMEM)
PARAMS = pltpu.CompilerParams(vmem_limit_bytes=VMEM_BYTES)
PIECES = 4
STEPS = 4
SMALL = pl.CostEstimate(flops=1, bytes_accessed=1, transcendentals=0)
LARGE = pl.CostEstimate(flops=1 << 33, bytes_accessed=1, transcendentals=0)


def in_hbm(values):
    return [pltpu.with_memory_space_constraint(x, pltpu.HBM) for x in values]


def held(value):
    return pltpu.with_memory_space_constraint(value, pltpu.VMEM)


def routed_copies(route, counts, route_now, counts_now, sems):
    return [
        pltpu.make_async_copy(route, route_now, sems.at[0]),
        pltpu.make_async_copy(counts, counts_now, sems.at[1]),
    ]


def row_copies(source, target, sems):
    pieces = sems.shape[0]
    rows = source.shape[0] // pieces
    some = [pl.ds(i * rows, rows) for i in range(pieces)]
    return [
        pltpu.make_async_copy(source.at[place], target.at[place], sems.at[i])
        for i, place in enumerate(some)
    ]


def contracted(columns, wide):
    return lax.dot_general(
        columns, wide, (((0,), (0,)), ((), ())), preferred_element_type=jnp.float32
    )


def owner_columns(chip, sibling, share, some=None):
    me = lax.axis_index("dp")
    core = 1 - me % 2 if sibling else me % 2
    begin = (lax.bitwise_xor(me // 2, chip) * 2 + core) * share
    some = some or slice(0, share)
    width = some.stop - some.start
    return pl.ds(pl.multiple_of(begin + some.start, width), width)


def sibling_kernel(experts, share, route, counts, inputs, hidden, *refs):
    out, columns, wide, rows, route_now, counts_now, column_sems, sems = refs
    copies = routed_copies(route, counts, route_now, counts_now, sems)
    copies.append(pltpu.make_async_copy(hidden.at[1], rows, sems.at[2]))
    chips, part, _ = out.shape
    column_copies = []
    for sibling in (True, False):
        for k in range(chips):
            place = owner_columns(k, sibling, share)
            sem = column_sems.at[k + (0 if sibling else chips)]
            copy = pltpu.make_async_copy(inputs.at[1, :, place], columns.at[:, place], sem)
            column_copies.append(copy)
    for copy in copies[2:] + column_copies[:chips] + copies[:2] + column_copies[chips:]:
        copy.start()
    for copy in copies:
        copy.wait()
    expand_hidden(route_now, counts_now, 1, rows, wide, route.shape[1], experts)
    for copy in column_copies[:chips]:
        copy.wait()
    for k in range(chips):
        place = owner_columns(k, True, share, slice(0, part))
        out[k] = contracted(columns[:, place], wide[...]).astype(out.dtype)
    for copy in column_copies[chips:]:
        copy.wait()


def sibling_products(route, counts, inputs, hidden, chips, experts, cuts):
    _, rows, model = inputs.shape
    width = hidden.shape[2]
    columns = experts * width
    outs = [pltpu.VMEM((chips, cuts[0].stop, columns), jnp.bfloat16)]
    outs += [pltpu.VMEM((rows, model), jnp.bfloat16), pltpu.VMEM((rows, columns), jnp.bfloat16)]
    return pl.pallas_call(
        functools.partial(sibling_kernel, experts, cuts[-1].stop),
        in_specs=[ANYWHERE] * 4,
        out_specs=[IN_VMEM] * len(outs),
        out_shape=outs,
        scratch_shapes=[
            pltpu.VMEM((rows, width), jnp.bfloat16),
            pltpu.SMEM(route.shape, jnp.int32),
            pltpu.SMEM(counts.shape, jnp.int32),
            pltpu.SemaphoreType.DMA((2 * chips,)),
            pltpu.SemaphoreType.DMA((3,)),
        ],
        compiler_params=PARAMS,
        cost_estimate=SMALL,
    )(*in_hbm((route, counts, inputs, hidden)))


def own_kernel(experts, route, counts, inputs, hidden, columns, wide, *refs):
    out, later, ahead, rows, route_now, counts_now, column_sems, sems = refs
    chips, share, _ = out.shape
    part = later.shape[1]
    model = columns.shape[1]
    copies = routed_copies(route, counts, route_now, counts_now, sems)
    copies.append(pltpu.make_async_copy(hidden.at[0], rows, sems.at[2]))
    column_copies = row_copies(inputs.at[0], ahead.at[:, :model], column_sems)
    for copy in copies + column_copies:
        copy.start()

    def step(i, carry):
        for k in (2 * i, 2 * i + 1):
            product = contracted(columns[:, owner_columns(k, False, share)], wide[...])
            out[k] = product.astype(out.dtype)
            place = owner_columns(k, True, share, slice(share - part, share))
            later[k] = contracted(columns[:, place], wide[...]).astype(later.dtype)
        return carry

    lax.fori_loop(0, chips // 2, step, 0)
    for copy in copies:
        copy.wait()
    expand_hidden(route_now, counts_now, 0, rows, ahead.at[:, model:], route.shape[1], experts)
    for copy in column_copies:
        copy.wait()


def own_products(route, counts, inputs, hidden, columns, wide, share, chips, experts, cuts):
    rows, model = columns.shape
    return pl.pallas_call(
        functools.partial(own_kernel, experts),
        in_specs=[ANYWHERE] * 4 + [IN_VMEM] * 2,
        out_specs=[IN_VMEM] * 3,
        out_shape=[
            pltpu.VMEM((chips, share, wide.shape[1]), jnp.bfloat16),
            pltpu.VMEM((chips, share - cuts[0].stop, wide.shape[1]), jnp.bfloat16),
            pltpu.VMEM((rows, model + wide.shape[1]), jnp.bfloat16),
        ],
        scratch_shapes=[
            pltpu.VMEM(hidden.shape[1:], jnp.bfloat16),
            pltpu.SMEM(route.shape, jnp.int32),
            pltpu.SMEM(counts.shape, jnp.int32),
            pltpu.SemaphoreType.DMA((PIECES,)),
            pltpu.SemaphoreType.DMA((3,)),
        ],
        compiler_params=PARAMS,
        cost_estimate=SMALL,
    )(*in_hbm((route, counts, inputs, hidden)), held(columns), held(wide))


def join_kernel(some, crossed, own, received, *refs):
    chips = own.shape[0]
    core = lax.axis_index("dp") % 2
    for piece, out in enumerate(refs[-chips:]):
        k = neighbour(piece, core, chips, crossed)
        total = own[k, some].astype(jnp.float32) + received[k].astype(jnp.float32)
        out[...] = total.astype(out.dtype)


def joined(own, received, some, passed, crossed):
    chips, rows, columns = received.shape
    outs = [pltpu.VMEM(x.shape, x.dtype) for x in passed]
    outs += [pltpu.VMEM((rows, columns), jnp.float32)]
    outs += [pltpu.VMEM((rows, columns), jnp.bfloat16)] * (chips - 1)
    return pl.pallas_call(
        functools.partial(join_kernel, some, crossed),
        in_specs=[IN_VMEM] * (2 + len(passed)),
        out_specs=[IN_VMEM] * len(outs),
        out_shape=outs,
        input_output_aliases={2 + i: i for i in range(len(passed))},
        compiler_params=PARAMS,
        cost_estimate=SMALL,
    )(*map(held, (own, received, *passed)))


def pair_kernel(count, messages, ahead, other, *refs):
    kept, *sent = refs[count:]
    share, columns = kept.shape
    model = ahead.shape[1] - columns
    chips = 1 + max(place for place, _ in messages)
    wide_both = jnp.concatenate([ahead[:, model:], other[:, model:]], axis=0)
    for k in range(chips):
        chip = neighbour(k, lax.axis_index("dp") % 2, chips, True)
        place = owner_columns(chip, False, share)
        columns_both = jnp.concatenate([ahead[:, place], other[:, place]], axis=0)
        total = contracted(columns_both, wide_both)
        if k == 0:
            kept[...] = total
        for (chip, some), out in zip(messages, sent):
            if chip == k:
                out[...] = total[some].astype(out.dtype)


def paired(ahead, other, after, share, columns, messages):
    outs = [pltpu.VMEM((share, columns), jnp.float32)]
    outs += [pltpu.VMEM((some.stop - some.start, columns), jnp.bfloat16) for _, some in messages]
    return pl.pallas_call(
        functools.partial(pair_kernel, len(after), messages),
        in_specs=[IN_VMEM] * 2 + [ANYWHERE] * len(after),
        out_specs=[IN_VMEM] * len(outs),
        out_shape=outs,
        compiler_params=PARAMS,
        cost_estimate=SMALL,
    )(held(ahead), held(other), *after)


def total_kernel(count, kept, *refs):
    total = kept[...]
    for part in refs[:count]:
        total = total + part[...].astype(jnp.float32)
    out = refs[-1]
    out[...] = total.astype(out.dtype)


def totalled(kept, received, after, dtype, cost=None):
    count = len(received)
    return pl.pallas_call(
        functools.partial(total_kernel, count),
        in_specs=[IN_VMEM] * (1 + count) + [ANYWHERE] * len(after),
        out_specs=IN_VMEM,
        out_shape=pltpu.VMEM(kept.shape, dtype),
        compiler_params=PARAMS,
        cost_estimate=cost or SMALL,
    )(held(kept), *map(held, received), *after)


def update_kernel(experts, cuts, messages, kept, *refs):
    count, parts = len(messages), len(cuts)
    received, partners = refs[:count], refs[count : count + parts]
    first, second, *outs = refs[count + parts : count + parts + 6]
    grad_out, first_out, second_out, step_out, sems = refs[count + parts + 6 :]
    share, columns = kept.shape
    lines = columns // LANES
    chunks = columns // experts // LANES
    steps = range(0, share + 1, share // STEPS)
    copies = []
    for i, (begin, end) in enumerate(zip(steps, steps[1:])):
        rows = end - begin

        def inside(spans):
            return [
                (ref, slice(begin - span.start, end - span.start))
                for ref, span in spans
                if span.start <= begin and end <= span.stop
            ]

        terms = inside(zip(received, (span for _, span in messages)))
        terms += inside(zip(partners, cuts))
        for line in range(lines):
            expert, chunk = line // chunks, line % chunks
            some = slice(line * LANES, (line + 1) * LANES)
            grad = kept[begin:end, some]
            for part, place in terms:
                grad = grad + part[place, some].astype(jnp.float32)
            place = begin * lines + chunk * experts + expert
            grad_out[pl.ds(place, rows, stride=lines), :] = grad
        some = slice(begin * lines, end * lines)
        grad = grad_out[some, :]
        new_first = beta_one * first[some, :] + (1.0 - beta_one) * grad
        new_second = beta_two * second[some, :] + (1.0 - beta_two) * grad * grad
        first_out[some, :] = new_first
        second_out[some, :] = new_second
        step_out[some, :] = (
            new_first / bias_first / (jnp.sqrt(new_second / bias_second) + adam_epsilon)
        )
        for j, (source, target) in enumerate(
            zip((grad_out, first_out, second_out, step_out), outs)
        ):
            copy = pltpu.make_async_copy(source.at[some], target.at[some], sems.at[i, j])
            copy.start()
            copies.append(copy)
    for copy in copies:
        copy.wait()


def in_lines(value):
    rows, experts, width = value.shape
    value = value.reshape(rows, experts, width // LANES, LANES)
    return value.transpose(0, 2, 1, 3).reshape(-1, LANES)


def from_lines(value, shape):
    rows, experts, width = shape
    value = value.reshape(rows, width // LANES, experts, LANES)
    return value.transpose(0, 2, 1, 3).reshape(shape)


def updated(kept, received, partners, first, second, cuts, messages):
    lines = pltpu.VMEM((first.size // LANES, LANES), jnp.float32)
    outs = pl.pallas_call(
        functools.partial(update_kernel, first.shape[1], cuts, messages),
        in_specs=[IN_VMEM] * (3 + len(received) + len(partners)),
        out_specs=[ANYWHERE] * 4,
        out_shape=[jax.ShapeDtypeStruct(lines.shape, jnp.float32)] * 4,
        scratch_shapes=[pltpu.VMEM((first.size // LANES + 8, LANES), jnp.float32)]
        + [lines] * 3
        + [pltpu.SemaphoreType.DMA((STEPS, 4))],
        compiler_params=PARAMS,
        cost_estimate=SMALL,
    )(*map(held, (kept, *received, *partners, in_lines(first), in_lines(second))))
    return [from_lines(out, first.shape) for out in outs]


def fast_device(saved_inputs, hidden_grads, block_expert, live_counts, first_moment, second_moment):
    chips = lax.axis_size("dp") // 2
    share, experts, width = first_moment.shape[1:]
    given = (block_expert[0, 0], live_counts[0, 0], saved_inputs[0, 0], hidden_grads[0, 0])
    cuts = [slice(0, share // 2), slice(share // 2, share)]
    places = range(1, chips)
    messages = [(k, slice(0, share)) for k in places]

    def to_owners(pieces, name, crossed):
        sent = []
        for piece, k in zip(pieces, places):
            chip = functools.partial(neighbour, k, chips=chips, crossed=crossed)
            sent.append(exchanged(piece, "dp", lambda i: 2 * chip(i % 2), f"{name}_to_chip_{k}"))
        return sent

    with jax.named_scope("sibling_products"):
        sibling, columns, wide = sibling_products(*given, chips, experts, cuts)
    others = [exchanged(sibling, "dp", lambda i: 1, "sibling_0")]
    with jax.named_scope("own_products"):
        own, later, ahead = own_products(*given, columns, wide, share, chips, experts, cuts)
    others.append(exchanged(later, "dp", lambda i: 1, "sibling_1"))
    parts = []
    for i, (other, some) in enumerate(zip(others, cuts)):
        with jax.named_scope(f"join_{i}"):
            if i == 0:
                ahead, kept, *sent = joined(own, other, some, [ahead], True)
            else:
                kept, *sent = joined(own, other, some, [], False)
        parts.append((kept, to_owners(sent, f"one_part_{i}", False if i else True)))
    other_ahead = exchanged(ahead, "dp", lambda i: 1, "operand_exchange")
    with jax.named_scope("pair"):
        kept_zero, *sent_zero = paired(
            ahead, other_ahead, [parts[0][1][1]], share, experts * width, messages
        )
    received_zero = to_owners(sent_zero, "zero", True)
    partners = []
    for i, (kept, received) in enumerate(parts):
        with jax.named_scope(f"total_{i}"):
            total = totalled(kept, received, [kept_zero], jnp.bfloat16, LARGE if i else SMALL)
        partners.append(mirrored(total, f"mirror_{i}"))
    with jax.named_scope("update"):
        outs = updated(
            kept_zero, received_zero, partners, first_moment[0], second_moment[0], cuts, messages
        )
    return tuple(out[None] for out in outs)


def route_select(block_expert, live_counts, block):
    experts = jnp.arange(live_counts.shape[-1], dtype=jnp.int32)
    onehot = (block_expert[..., :, None] == experts).astype(jnp.int32)
    earlier = jnp.cumsum(onehot, axis=-2) - onehot
    before = jnp.sum(earlier * onehot, axis=-1)
    limits = jnp.sum(live_counts[..., None, :] * onehot, axis=-1)
    positions = before[..., None] * block + jnp.arange(block, dtype=jnp.int32)
    return positions < limits[..., None], onehot


def plain_device(saved_inputs, hidden_grads, block_expert, live_counts, first_moment, second_moment):
    _, _, _, rows, model_width = saved_inputs.shape
    hidden = hidden_grads.shape[4]
    blocks = block_expert.shape[3]
    block = rows // blocks
    live_rows, onehot = route_select(block_expert[0, 0], live_counts[0, 0], block)
    masked = hidden_grads.reshape(2, blocks, block, hidden) * live_rows[..., None].astype(
        jnp.bfloat16
    )
    wide = masked[:, :, :, None, :] * onehot[:, :, None, :, None].astype(jnp.bfloat16)
    wide = wide.reshape(2, rows, -1)
    parts = jnp.einsum(
        "krd,krc->kdc", saved_inputs[0, 0], wide, preferred_element_type=jnp.float32
    )
    sent = lax.optimization_barrier(parts[1].astype(jnp.bfloat16)).astype(jnp.float32)
    summed = lax.psum_scatter(
        jnp.stack([parts[0], sent], axis=1), "dp", scatter_dimension=0, tiled=True
    )
    grad_total = (summed[:, 0] + mirrored(summed[:, 1])).reshape(first_moment.shape[1:])
    new_first = beta_one * first_moment[0] + (1.0 - beta_one) * grad_total
    new_second = beta_two * second_moment[0] + (1.0 - beta_two) * grad_total * grad_total
    step_direction = new_first / bias_first / (jnp.sqrt(new_second / bias_second) + adam_epsilon)
    return (grad_total[None], new_first[None], new_second[None], step_direction[None])


def solution(mesh):
    in_specs = (
        P("section", "dp", None, None, None),
        P("section", "dp", None, None, None),
        P("section", "dp", None, None),
        P("section", "dp", None, None),
        P("section", "dp", None, None),
        P("section", "dp", None, None),
    )
    out_specs = (P("section", "dp", None, None),) * 4

    def run(*arrays):
        ranks = mesh.shape["dp"]
        paired = ranks > 2 and ranks & (ranks - 1) == 0
        per_device = fast_device if paired and arrays[4].shape[1] // ranks % LANES == 0 else plain_device
        return jax.shard_map(
            per_device, mesh=mesh, in_specs=in_specs, out_specs=out_specs, check_vma=False
        )(*arrays)

    return run
```
